512 devices in a mesh: rng: 32 (over z, x), az: 16 (over y, core).
Axes of the slice: x: 4, y: 8, z: 8, core: 2. Of those that a mesh axis runs over, the one named last changes fastest.
Arguments:
- sar_image: float32 [2, 2048, 16384], P(None, 'rng', 'az'), may hold values from -6 to 6
- strong_index: int32 [1024], P('rng'), may hold values from 0 to 2047, as said below
- shifts: int32 [1024], P('rng'), may hold values from 0 to 16383
- widths: int32 [1024], P('rng'), may hold values from 256 to 2048
Outputs:
- focused_image: float32 [2, 2048, 16384], P(None, 'rng', 'az')
- phase_error: float32 [16384], P('az')
The draws below stay inside these ranges and needn't reach their ends.
Inputs may be any that keep to these rules, and one draw needn't show every extreme that they name: `strong_index`: entries r * 32 to (r + 1) * 32 - 1 are distinct range bins of the block r * 64 to (r + 1) * 64 - 1.
All inputs are finite; a program needn't handle non-finite values.
Results may differ from the reference program's by a relative error of at most 0.0003.
Values sent between devices are 32-bit elements; how exact they have to be, the bound alone decides.
No kernel may reach another device: no remote copies, remote signals or barrier semaphores. Data moves between devices by JAX's collectives and lax.ppermute only.
A program may use at most 64 MiB of HBM per device.

```python
import jax
import jax.numpy as jnp

PULSES = 16384
RNG_DEV = 64
STRONG_DEV = 32
ITERS = 2
RANGE = 2048
STRONG_TOTAL = 1024


def draw_strong_index(key, part):
    key = jax.random.fold_in(key, 5)
    blocks = RANGE // RNG_DEV
    keys = jax.random.split(key, blocks)
    picks = jax.vmap(lambda single: jax.random.permutation(single, RNG_DEV)[:STRONG_DEV])(keys)
    offsets = jnp.arange(blocks, dtype=jnp.int32) * RNG_DEV
    return (picks.astype(jnp.int32) + offsets[:, None]).reshape(-1).astype(jnp.int32)


def with_ends(array, key, least, top_value):
    longest = array.shape.index(max(array.shape))
    spots = []
    for shift in (0, 1):
        where = [jax.random.randint(jax.random.fold_in(key, axis), (), 0, length) for axis, length in enumerate(array.shape)]
        where[longest] = (where[longest] + shift) % array.shape[longest]
        spots.append(tuple(where))
    return array.at[spots[0]].set(least).at[spots[1]].set(top_value)


def block_levels(rng, extent, cuts, low, top_value):
    def one(axis_at, parts):
        draws = jax.random.uniform(jax.random.fold_in(jax.random.fold_in(rng, 6), axis_at), (parts,), jnp.float32, low / len(cuts), top_value / len(cuts))
        return jnp.repeat(jnp.exp(draws), extent[axis_at] // parts).reshape((-1,) + (1,) * (len(extent) - axis_at - 1))

    loudness = one(*cuts[0])
    for cut in cuts[1:]:
        loudness = loudness * one(*cut)
    return loudness


def gaussian(own_key, dims, spread, limit, shards=(), held_as=jnp.bfloat16):
    level = block_levels(own_key, dims, shards, -0.22, 0.18) if shards else 1.0
    result = jax.random.normal(own_key, dims, jnp.float32) * spread * level
    return jnp.minimum(jnp.maximum(result, -limit), limit).astype(held_as)


def setup_inputs(seed: int = 0) -> dict:
    key_of = jax.random.split(jax.random.key(seed), 5)
    sar_image = gaussian(key_of[0], (2, RANGE, PULSES), 1.0, 6.0, ((1, 32), (2, 16)), jnp.float32)
    strong_index = draw_strong_index(jax.random.fold_in(key_of[4], 71), 0)
    shifts = with_ends(jax.random.randint(key_of[2], (STRONG_TOTAL,), 0, PULSES), jax.random.fold_in(key_of[2], 1), 0, PULSES - 1).astype(jnp.int32)
    widths = with_ends(jax.random.randint(key_of[3], (STRONG_TOTAL,), PULSES // 64, PULSES // 8 + 1), jax.random.fold_in(key_of[3], 1), PULSES // 64, (PULSES // 8 + 1) - 1).astype(jnp.int32)
    return dict(sar_image=sar_image, strong_index=strong_index, shifts=shifts, widths=widths)


epsilon = 1e-6


def reference(sar_image, strong_index, shifts, widths):
    pulses = sar_image.shape[2]
    field = sar_image[0] + 1j * sar_image[1]
    history = jnp.fft.fft(field, axis=1, norm="ortho")
    cells = jnp.arange(pulses, dtype=jnp.int32)
    source = (cells[None, :] + shifts[:, None] - pulses // 2) % pulses
    lower = pulses // 2 - widths // 2
    window = (cells[None, :] >= lower[:, None]) & (cells[None, :] < (lower + widths)[:, None])
    total = jnp.zeros((pulses,), jnp.float32)
    for step in range(ITERS):
        if step == 0:
            current = field[strong_index]
        else:
            current = jnp.fft.ifft(history[strong_index] * jnp.exp(-1j * total)[None, :], axis=1, norm="ortho")
        centered = jnp.take_along_axis(current, source, axis=1) * window
        spectra = jnp.fft.fft(centered, axis=1, norm="ortho")
        cross = jnp.sum(jnp.imag(jnp.conj(spectra[:, :-1]) * spectra[:, 1:]), axis=0)
        numerator = jnp.concatenate([jnp.zeros((1,), cross.dtype), cross])
        denominator = jnp.sum(jnp.real(spectra) ** 2 + jnp.imag(spectra) ** 2, axis=0)
        total = total + jnp.cumsum(numerator / (denominator + epsilon))
    final = jnp.fft.ifft(history * jnp.exp(-1j * total)[None, :], axis=1, norm="ortho")
    focused_image = jnp.stack([jnp.real(final), jnp.imag(final)]).astype(jnp.float32)
    return focused_image, total.astype(jnp.float32)
```

```python
import math

import jax
import jax.numpy as jnp
import numpy as np
from jax import lax
from jax.experimental import pallas as pl
from jax.experimental.pallas import tpu as pltpu
from jax.sharding import PartitionSpec as P

EPSILON = 1e-06
SIDE = 128
SUB = 8
HIGHEST = lax.Precision.HIGHEST


def tables():
    grid = np.arange(SIDE)
    product = grid[:, None] * grid[None, :]
    angle = 2.0 * np.pi * (product % SIDE) / SIDE
    cosine, sine = np.cos(angle), np.sin(angle)
    right = np.block([[cosine, -sine], [sine, cosine]])
    twist = 2.0 * np.pi * product / (SIDE * SIDE)
    twist = np.stack([np.cos(twist), np.sin(twist)]) / SIDE
    return right.astype(np.float32), np.ascontiguousarray(right.T).astype(np.float32), twist.astype(np.float32)


def multiply(left, right):
    return jnp.dot(left, right, precision=HIGHEST, preferred_element_type=jnp.float32)


def forward(lines, right, right_t, twist):
    cosine, sine = twist
    stacked = jnp.concatenate([jnp.concatenate(line, axis=0) for line in lines], axis=1)
    first = multiply(right_t, stacked)
    turned = []
    for at in range(len(lines)):
        real = first[:SIDE, at * SIDE : (at + 1) * SIDE]
        imag = first[SIDE:, at * SIDE : (at + 1) * SIDE]
        turned.append(jnp.concatenate([real * cosine + imag * sine, imag * cosine - real * sine], axis=1))
    second = multiply(jnp.concatenate(turned, axis=0), right)
    return [
        (second[at * SIDE : (at + 1) * SIDE, :SIDE], second[at * SIDE : (at + 1) * SIDE, SIDE:])
        for at in range(len(lines))
    ]


def inverse(lines, right, right_t, twist):
    cosine, sine = twist
    stacked = jnp.concatenate([jnp.concatenate(line, axis=1) for line in lines], axis=0)
    first = multiply(stacked, right_t)
    turned = []
    for at in range(len(lines)):
        real = first[at * SIDE : (at + 1) * SIDE, :SIDE]
        imag = first[at * SIDE : (at + 1) * SIDE, SIDE:]
        turned.append(jnp.concatenate([real * cosine - imag * sine, imag * cosine + real * sine], axis=0))
    second = multiply(right, jnp.concatenate(turned, axis=1))
    return [
        (second[:SIDE, at * SIDE : (at + 1) * SIDE], second[SIDE:, at * SIDE : (at + 1) * SIDE])
        for at in range(len(lines))
    ]


def running_sum(gradient):
    rows = lax.broadcasted_iota(jnp.int32, (SIDE, SIDE), 0)
    cols = lax.broadcasted_iota(jnp.int32, (SIDE, SIDE), 1)
    within = multiply((cols <= rows).astype(jnp.float32), gradient)
    sums = jnp.broadcast_to(within[SIDE - 1 :, :], (SUB, SIDE))
    before = multiply(sums, (rows < cols).astype(jnp.float32))
    return within + before[:1, :]


def window_lines(lines, a_index, shifts_ref, widths_ref):
    rows = lax.broadcasted_iota(jnp.int32, (SIDE, SIDE), 0)
    cols = lax.broadcasted_iota(jnp.int32, (SIDE, SIDE), 1)
    cells = rows * SIDE + cols
    pulses = SIDE * SIDE
    out = []
    for at, (real, imag) in enumerate(lines):
        line = a_index * len(lines) + at
        width = widths_ref[line]
        start = shifts_ref[line] - width // 2
        inside = ((cells - start) & (pulses - 1)) < width
        out.append((jnp.where(inside, real, 0.0), jnp.where(inside, imag, 0.0)))
    return out


def gradient_sums(lines, a_index, shifts_ref):
    rows = lax.broadcasted_iota(jnp.int32, (SIDE, SIDE), 0)
    cols = lax.broadcasted_iota(jnp.int32, (SIDE, SIDE), 1)
    pulses = SIDE * SIDE
    numerator = jnp.zeros((SIDE, SIDE), jnp.float32)
    denominator = jnp.zeros((SIDE, SIDE), jnp.float32)

    def before(part):
        down = pltpu.roll(part, 1, 0)
        return jnp.where(rows == 0, pltpu.roll(down, 1, 1), down)

    for at, (real, imag) in enumerate(lines):
        shift = shifts_ref[a_index * len(lines) + at] - pulses // 2
        angle = jnp.full((SUB, SIDE), shift, jnp.int32).astype(jnp.float32) * (2.0 * math.pi / pulses)
        turn_r, turn_i = jnp.cos(angle)[:1, :], jnp.sin(angle)[:1, :]
        real_b, imag_b = before(real), before(imag)
        cross_r = real_b * real + imag_b * imag
        cross_i = real_b * imag - imag_b * real
        numerator = numerator + (cross_i * turn_r + cross_r * turn_i)
        denominator = denominator + (real * real + imag * imag)
    first = jnp.logical_and(rows == 0, cols == 0)
    return jnp.where(first, 0.0, numerator), denominator


def turn_back(lines, total):
    cosine, sine = jnp.cos(total), jnp.sin(total)
    return [(real * cosine + imag * sine, imag * cosine - real * sine) for real, imag in lines]


def square(ref, *at):
    return ref[(slice(None),) + at].reshape(SIDE, SIDE)


def store_sums(out_ref, numerator, denominator):
    out_ref[:, 0] = numerator.reshape(SIDE // SUB, SUB, SIDE)
    out_ref[:, 1] = denominator.reshape(SIDE // SUB, SUB, SIDE)


def pack_kernel(strong_ref, image_ref, out_ref, place_ref, tiles_ref):
    bins = image_ref.shape[1]
    strong = strong_ref.shape[0]

    def clear(at, carry):
        place_ref[at] = -1
        return carry

    def mark(at, carry):
        place_ref[strong_ref[at] % bins] = at
        return carry

    def count(at, others):
        held = place_ref[at]
        other = held < 0
        here = jnp.where(other, others, held)
        slot = here % 2 + jnp.where(other, 2, 0)
        place_ref[at] = (here // 2) * 4 + slot
        return others + jnp.where(other, 1, 0)

    lax.fori_loop(0, bins, clear, 0)
    lax.fori_loop(0, strong, mark, 0)
    lax.fori_loop(0, bins, count, 0)
    for part in range(2):
        for group in range(bins // SUB):
            for block in range(SUB):
                at = ((part * (bins // SUB) + group) * SUB + block) * SUB
                tiles_ref[pl.ds(at, SUB), :] = image_ref[
                    part, group * SUB : (group + 1) * SUB, block * SIDE : (block + 1) * SIDE
                ]
    for row in range(bins):
        place = place_ref[row]
        device, slot = place // 4, place % 4
        for part in range(2):
            at = (part * (bins // SUB) + row // SUB) * SUB * SUB + row % SUB
            out_ref[device, part * 4 + slot] = tiles_ref[pl.ds(at, SUB, stride=SUB), :]


def unpack_kernel(place_ref, rows_ref, image_ref, tiles_ref):
    bins = image_ref.shape[1]
    for row in range(bins):
        place = place_ref[row]
        device, slot = place // 4, place % 4
        for part in range(2):
            at = (part * (bins // SUB) + row // SUB) * SUB * SUB + row % SUB
            tiles_ref[pl.ds(at, SUB, stride=SUB), :] = rows_ref[device, part * 4 + slot]
    for part in range(2):
        for group in range(bins // SUB):
            for block in range(SUB):
                at = ((part * (bins // SUB) + group) * SUB + block) * SUB
                image_ref[part, group * SUB : (group + 1) * SUB, block * SIDE : (block + 1) * SIDE] = tiles_ref[
                    pl.ds(at, SUB), :
                ]


def first_kernel(a_ref, shifts_ref, widths_ref, rows_ref, right_ref, right_t_ref, twist_ref, out_ref):
    a_index = a_ref[0]
    consts = (right_ref[...], right_t_ref[...], (twist_ref[0], twist_ref[1]))
    lines = [(square(rows_ref, at), square(rows_ref, 4 + at)) for at in range(2)]
    spectra = forward(window_lines(lines, a_index, shifts_ref, widths_ref), *consts)
    store_sums(out_ref, *gradient_sums(spectra, a_index, shifts_ref))


def history_kernel(rows_ref, right_ref, right_t_ref, twist_ref, out_ref):
    consts = (right_ref[...], right_t_ref[...], (twist_ref[0], twist_ref[1]))
    lines = [(square(rows_ref, at), square(rows_ref, 4 + at)) for at in range(4)]
    for at, (real, imag) in enumerate(forward(lines, *consts)):
        out_ref[at, 0] = real
        out_ref[at, 1] = imag


def gather_sums_kernel(in_ref, out_ref):
    out_ref[...] = jnp.broadcast_to(jnp.sum(in_ref[...], axis=0)[None], out_ref.shape)


def gradient_kernel(in_ref, out_ref):
    sums = jnp.sum(in_ref[...], axis=0)
    gradient = sums[0] / (sums[1] + EPSILON)
    out_ref[...] = jnp.broadcast_to(gradient[None], out_ref.shape)


def second_kernel(
    a_ref, shifts_ref, widths_ref, gradient_ref, history_ref, right_ref, right_t_ref, twist_ref, out_ref, total_ref
):
    a_index = a_ref[0]
    consts = (right_ref[...], right_t_ref[...], (twist_ref[0], twist_ref[1]))
    total = running_sum(gradient_ref[...].reshape(SIDE, SIDE))
    total_ref[...] = total
    lines = [(history_ref[at, 0], history_ref[at, 1]) for at in range(2)]
    lines = inverse(turn_back(lines, total), *consts)
    spectra = forward(window_lines(lines, a_index, shifts_ref, widths_ref), *consts)
    store_sums(out_ref, *gradient_sums(spectra, a_index, shifts_ref))


def final_kernel(
    a_ref, gradient_ref, total_ref, history_ref, right_ref, right_t_ref, twist_ref, out_ref, phase_ref, turned_ref
):
    a_index = a_ref[0]
    consts = (right_ref[...], right_t_ref[...], (twist_ref[0], twist_ref[1]))
    total = total_ref[...] + running_sum(gradient_ref[...].reshape(SIDE, SIDE))
    turned_ref[...] = total.T
    phase_ref[...] = turned_ref[pl.ds(pl.multiple_of(a_index * SUB, SUB), SUB), :]
    lines = [(history_ref[at, 0], history_ref[at, 1]) for at in range(4)]
    for at, (real, imag) in enumerate(inverse(turn_back(lines, total), *consts)):
        out_ref[:, at] = real.reshape(SIDE // SUB, SUB, SIDE)
        out_ref[:, 4 + at] = imag.reshape(SIDE // SUB, SUB, SIDE)


SMEM = pl.BlockSpec(memory_space=pltpu.SMEM)
VMEM = pl.BlockSpec(memory_space=pltpu.VMEM)


def call(kernel, shapes, specs, *operands, scratch=(), out_specs=None):
    out_shape = [jax.ShapeDtypeStruct(*shape) for shape in shapes]
    out = pl.pallas_call(
        kernel,
        out_shape=out_shape,
        in_specs=list(specs),
        out_specs=out_specs or [VMEM] * len(out_shape),
        scratch_shapes=list(scratch),
        compiler_params=pltpu.CompilerParams(vmem_limit_bytes=32 * 1024 * 1024),
    )(*operands)
    return out if len(out) > 1 else out[0]


def exchange(array, axis):
    return lax.all_to_all(array, axis, split_axis=0, concat_axis=0, tiled=True)


def local(sar_image, strong_index, shifts, widths):
    f32 = jnp.float32
    az, rng = lax.axis_size("az"), lax.axis_size("rng")
    bins, pulses_local = sar_image.shape[1:]
    consts = tuple(jnp.asarray(table) for table in tables())
    a_index = lax.axis_index("az").astype(jnp.int32).reshape(1)
    tile = (SUB, SIDE)

    packed, place = call(
        pack_kernel,
        [((az, 8) + tile, f32), ((bins,), jnp.int32)],
        [SMEM, VMEM],
        strong_index,
        sar_image,
        scratch=[pltpu.VMEM((2 * bins * SUB, SIDE), f32)],
        out_specs=[VMEM, SMEM],
    )
    rows = exchange(packed, "az")
    sums = call(
        first_kernel,
        [((az, 2) + tile, f32)],
        [SMEM, SMEM, SMEM, VMEM, VMEM, VMEM, VMEM],
        a_index,
        shifts,
        widths,
        rows,
        *consts,
    )
    history = call(history_kernel, [((4, 2, SIDE, SIDE), f32)], [VMEM] * 4, rows, *consts)

    def all_gradient(sums):
        scattered = exchange(sums, "az")
        partial = call(gather_sums_kernel, [((rng, 2) + tile, f32)], [VMEM], scattered)
        everyone = exchange(partial, "rng")
        gradient = call(gradient_kernel, [((az,) + tile, f32)], [VMEM], everyone)
        return exchange(gradient, "az")

    gradient = all_gradient(sums)
    sums, total = call(
        second_kernel,
        [((az, 2) + tile, f32), ((SIDE, SIDE), f32)],
        [SMEM, SMEM, SMEM, VMEM, VMEM, VMEM, VMEM, VMEM],
        a_index,
        shifts,
        widths,
        gradient,
        history,
        *consts,
    )
    gradient = all_gradient(sums)
    corrected, phase = call(
        final_kernel,
        [((az, 8) + tile, f32), (tile, f32)],
        [SMEM] + [VMEM] * 6,
        a_index,
        gradient,
        total,
        history,
        *consts,
        scratch=[pltpu.VMEM((SIDE, SIDE), f32)],
    )
    returned = exchange(corrected, "az")
    focused = call(
        unpack_kernel,
        [(sar_image.shape, f32)],
        [SMEM, VMEM],
        place,
        returned,
        scratch=[pltpu.VMEM((2 * bins * SUB, SIDE), f32)],
    )
    return focused, phase.reshape(pulses_local)


def solution(mesh):
    placed = (P(None, "rng", "az"), P("rng"), P("rng"), P("rng"))
    return jax.shard_map(
        local,
        mesh=mesh,
        in_specs=placed,
        out_specs=(P(None, "rng", "az"), P("az")),
        check_vma=False,
    )
```

```python
import jax
import jax.numpy as jnp
import numpy as np
from jax import lax
from jax.experimental import pallas as pl
from jax.experimental.pallas import tpu as pltpu
from jax.sharding import Mesh, PartitionSpec as P

EPSILON = 1e-06
SIDE = 128
SUB = 8
TILES = SIDE // SUB
WINDOW = 16
FIRST = SIDE // 2 - WINDOW // 2
LOAD = 24
HIGHEST = lax.Precision.HIGHEST


def tables():
    grid = np.arange(SIDE)
    product = grid[:, None] * grid[None, :]
    angle = 2.0 * np.pi * (product % SIDE) / SIDE
    cosine, sine = np.cos(angle), np.sin(angle)
    right = np.block([[cosine, -sine], [sine, cosine]])
    rows = slice(FIRST, FIRST + WINDOW)
    window = np.block([[cosine[:, rows], sine[:, rows]], [-sine[:, rows], cosine[:, rows]]])
    around = np.arange(SIDE + LOAD) % SIDE
    ring = np.stack([cosine[around], sine[around]])
    twist = 2.0 * np.pi * product / (SIDE * SIDE)
    twist = np.stack([np.cos(twist), np.sin(twist)]) / SIDE
    made = dict(right=right, right_t=right.T, window=window, ring=ring, twist=twist)
    return {name: jnp.asarray(np.ascontiguousarray(table).astype(np.float32)) for name, table in made.items()}


def multiply(left, right):
    return jnp.dot(left, right, precision=HIGHEST, preferred_element_type=jnp.float32)


def forward(lines, left, right, twist_ref):
    cosine, sine = twist_ref[0], twist_ref[1]
    stacked = jnp.concatenate([jnp.concatenate(line, axis=0) for line in lines], axis=1)
    first = multiply(left, stacked)
    turned = []
    for at in range(len(lines)):
        real = first[:SIDE, at * SIDE : (at + 1) * SIDE]
        imag = first[SIDE:, at * SIDE : (at + 1) * SIDE]
        turned.append(jnp.concatenate([real * cosine + imag * sine, imag * cosine - real * sine], axis=1))
    second = multiply(jnp.concatenate(turned, axis=0), right)
    return [
        (second[at * SIDE : (at + 1) * SIDE, :SIDE], second[at * SIDE : (at + 1) * SIDE, SIDE:])
        for at in range(len(lines))
    ]


def inverse_start(lines, right_t, twist_ref):
    cosine, sine = twist_ref[0], twist_ref[1]
    stacked = jnp.concatenate([jnp.concatenate(line, axis=1) for line in lines], axis=0)
    first = multiply(stacked, right_t)
    turned = []
    for at in range(len(lines)):
        real = first[at * SIDE : (at + 1) * SIDE, :SIDE]
        imag = first[at * SIDE : (at + 1) * SIDE, SIDE:]
        turned.append(jnp.concatenate([real * cosine - imag * sine, imag * cosine + real * sine], axis=0))
    return turned


def grid_of(rows):
    return (
        lax.broadcasted_iota(jnp.int32, (rows, SIDE), 0),
        lax.broadcasted_iota(jnp.int32, (rows, SIDE), 1),
    )


def running_sum(gradient):
    rows, cols = grid_of(SIDE)
    within = multiply((cols <= rows).astype(jnp.float32), gradient)
    sums = jnp.broadcast_to(jnp.sum(gradient, axis=0, keepdims=True), (SUB, SIDE))
    before = multiply(sums, (rows < cols).astype(jnp.float32))
    return within + before[:1, :]


def phase_of(sums_ref):
    gradient = sums_ref[:TILES] / (sums_ref[TILES:] + EPSILON)
    return running_sum(gradient.reshape(SIDE, SIDE))


def cosine_sine(angle):
    quarters = jnp.floor(angle * (2.0 / np.pi) + 0.5)
    rest = angle - quarters * 1.5703125
    rest = rest - quarters * 4.837512969970703125e-4
    rest = rest - quarters * 7.54978995489188216e-8
    square = rest * rest
    sine = ((-1.9515295891e-4 * square + 8.3321608736e-3) * square - 1.6666654611e-1) * square * rest + rest
    cosine = (2.443315711809948e-5 * square - 1.388731625493765e-3) * square + 4.166664568298827e-2
    cosine = cosine * square * square - 0.5 * square + 1.0
    turn = quarters.astype(jnp.int32)
    odd = (turn & 1) == 1
    sine, cosine = jnp.where(odd, cosine, sine), jnp.where(odd, sine, cosine)
    return jnp.where(((turn + 1) & 2) == 2, -cosine, cosine), jnp.where((turn & 2) == 2, -sine, sine)


def turn_back(lines, total):
    cosine, sine = cosine_sine(total)
    return [(real * cosine + imag * sine, imag * cosine - real * sine) for real, imag in lines]


def row_offset(shift):
    begin = (shift + SIDE * SIDE // 2) & (SIDE * SIDE - 1)
    return ((begin >> 7) + FIRST) & (SIDE - 1), begin & (SIDE - 1)


def center(upper, lower, lane, width):
    rows, cols = grid_of(WINDOW)
    turn = (SIDE - lane) & (SIDE - 1)
    moved = jnp.where(cols >= SIDE - lane, pltpu.roll(lower, turn, 1), pltpu.roll(upper, turn, 1))
    cells = (rows + FIRST) * SIDE + cols
    least = SIDE * SIDE // 2 - width // 2
    return jnp.where((cells >= least) & (cells < least + width), moved, 0.0)


def gradient_sums(lines, out_ref):
    rows, cols = grid_of(SIDE)
    numerator = jnp.zeros((SIDE, SIDE), jnp.float32)
    denominator = jnp.zeros((SIDE, SIDE), jnp.float32)

    def before(part):
        down = pltpu.roll(part, 1, 0)
        return jnp.where(rows == 0, pltpu.roll(down, 1, 1), down)

    for real, imag in lines:
        numerator = numerator + (before(real) * imag - before(imag) * real)
        denominator = denominator + (real * real + imag * imag)
    numerator = jnp.where((rows == 0) & (cols == 0), 0.0, numerator)
    out_ref[:TILES] = numerator.reshape(TILES, SUB, SIDE)
    out_ref[TILES:] = denominator.reshape(TILES, SUB, SIDE)


def tile_at(bins, part, row):
    return (part * (bins // SUB) + row // SUB) * SUB * SUB + row % SUB


def pack_kernel(strong_hbm, image_hbm, out_ref, place_ref, strong_ref, image_ref, tiles_ref, small_sem, sems):
    bins = image_ref.shape[1]
    strong = strong_ref.shape[0]
    indices = pltpu.make_async_copy(strong_hbm, strong_ref, small_sem)
    indices.start()
    parts = [pltpu.make_async_copy(image_hbm.at[part], image_ref.at[part], sems.at[part]) for part in range(2)]
    for part in parts:
        part.start()
    for row in range(bins):
        place_ref[row] = -1
    indices.wait()
    for at in range(strong):
        place_ref[strong_ref[at] % bins] = at // 2 * 8 + at % 2
    others = jnp.int32(0)
    for row in range(bins):
        held = place_ref[row]
        place_ref[row] = jnp.where(held < 0, others // 2 * 8 + others % 2 + 2, held)
        others = others + jnp.where(held < 0, 1, 0)
    for part in range(2):
        parts[part].wait()
        for group in range(bins // SUB):
            for block in range(SUB):
                at = ((part * (bins // SUB) + group) * SUB + block) * SUB
                tiles_ref[at : at + SUB, :] = image_ref[
                    part, group * SUB : (group + 1) * SUB, block * SIDE : (block + 1) * SIDE
                ]
        for row in range(bins):
            out_ref[place_ref[row] + part * 4] = tiles_ref[pl.ds(tile_at(bins, part, row), SUB, stride=SUB), :]


def unpack_kernel(place_ref, rows_ref, image_hbm, image_ref, tiles_ref, sems):
    bins = image_ref.shape[1]
    copies = []
    for part in range(2):
        for row in range(bins):
            tiles_ref[pl.ds(tile_at(bins, part, row), SUB, stride=SUB), :] = rows_ref[place_ref[row] + part * 4]
        for half in range(2):
            span = slice(half * bins // 2, (half + 1) * bins // 2)
            for group in range(half * bins // 2 // SUB, (half + 1) * bins // 2 // SUB):
                for block in range(SUB):
                    at = ((part * (bins // SUB) + group) * SUB + block) * SUB
                    image_ref[part, group * SUB : (group + 1) * SUB, block * SIDE : (block + 1) * SIDE] = tiles_ref[
                        at : at + SUB, :
                    ]
            copies.append(
                pltpu.make_async_copy(
                    image_ref.at[part, span], image_hbm.at[part, span], sems.at[part * 2 + half]
                )
            )
            copies[-1].start()
    for copy in copies:
        copy.wait()


def first_kernel(a_ref, shifts_ref, widths_ref, rows_ref, window_ref, right_ref, twist_ref, out_ref, ring_ref):
    lines = []
    for at in range(2):
        line = a_ref[0] * 2 + at
        row, lane = row_offset(shifts_ref[line])
        parts = []
        for part in range(2):
            ring = ring_ref.at[at * 2 + part]
            ring[:SIDE, :] = rows_ref[:, part * 4 + at].reshape(SIDE, SIDE)
            ring[SIDE:, :] = rows_ref[: LOAD // SUB, part * 4 + at].reshape(LOAD, SIDE)
            parts.append(center(ring[pl.ds(row, WINDOW), :], ring[pl.ds(row + 1, WINDOW), :], lane, widths_ref[line]))
        lines.append(parts)
    gradient_sums(forward(lines, window_ref[...], right_ref[...], twist_ref), out_ref)


def history_kernel(rows_ref, right_ref, right_t_ref, twist_ref, out_ref):
    lines = [[rows_ref[:, part * 4 + at].reshape(SIDE, SIDE) for part in range(2)] for at in range(4)]
    for at, (real, imag) in enumerate(forward(lines, right_t_ref[...], right_ref[...], twist_ref)):
        out_ref[at, 0] = real
        out_ref[at, 1] = imag


def share_kernel(in_ref, out_ref):
    out_ref[...] = jnp.broadcast_to(jnp.sum(in_ref[...], axis=0)[None], out_ref.shape)


def second_kernel(
    a_ref, shifts_ref, widths_ref, sums_ref, history_ref, window_ref, ring_ref, right_ref, right_t_ref, twist_ref,
    out_ref, total_ref,
):
    total = phase_of(sums_ref)
    total_ref[...] = total
    lines = turn_back([(history_ref[at, 0], history_ref[at, 1]) for at in range(2)], total)
    centered = []
    for at, started in enumerate(inverse_start(lines, right_t_ref[...], twist_ref)):
        line = a_ref[0] * 2 + at
        row, lane = row_offset(shifts_ref[line])
        cosine, sine = ring_ref[0, pl.ds(row, LOAD), :], ring_ref[1, pl.ds(row, LOAD), :]
        left = [jnp.concatenate([cosine, -sine], axis=1), jnp.concatenate([sine, cosine], axis=1)]
        found = multiply(jnp.concatenate(left, axis=0), started)
        centered.append(
            [
                center(found[from_row : from_row + WINDOW], found[from_row + 1 : from_row + 1 + WINDOW], lane, widths_ref[line])
                for from_row in (0, LOAD)
            ]
        )
    gradient_sums(forward(centered, window_ref[...], right_ref[...], twist_ref), out_ref)


def final_kernel(
    a_ref, sums_ref, total_ref, history_ref, right_ref, right_t_ref, twist_ref, out_ref, phase_ref, turned_ref
):
    total = total_ref[...] + phase_of(sums_ref)
    lines = turn_back([(history_ref[at, 0], history_ref[at, 1]) for at in range(4)], total)
    found = multiply(right_ref[...], jnp.concatenate(inverse_start(lines, right_t_ref[...], twist_ref), axis=1))
    for at in range(4):
        for part in range(2):
            line = found[part * SIDE : (part + 1) * SIDE, at * SIDE : (at + 1) * SIDE]
            out_ref[:, part * 4 + at] = line.reshape(TILES, SUB, SIDE)
    turned_ref[...] = total.T
    phase_ref[...] = turned_ref[pl.ds(pl.multiple_of(a_ref[0] * SUB, SUB), SUB), :]


SMEM = pl.BlockSpec(memory_space=pltpu.SMEM)
VMEM = pl.BlockSpec(memory_space=pltpu.VMEM)
HBM = pl.BlockSpec(memory_space=pltpu.HBM)


def call(kernel, shapes, specs, *operands, scratch=(), out_specs=None):
    out = pl.pallas_call(
        kernel,
        out_shape=[jax.ShapeDtypeStruct(*shape) for shape in shapes],
        in_specs=list(specs),
        out_specs=out_specs or [VMEM] * len(shapes),
        scratch_shapes=list(scratch),
        compiler_params=pltpu.CompilerParams(vmem_limit_bytes=32 * 1024 * 1024),
    )(*operands)
    return out if len(out) > 1 else out[0]


def exchange(array, axes):
    return lax.all_to_all(array, axes, split_axis=0, concat_axis=0, tiled=True)


RNG = ("zh", "zl", "x")
AZ = ("yh", "yl", "core")
NEAR = ("zl", "x", "yl", "core")
FAR = ("zh", "yh")


def local(sar_image, strong_index, shifts, widths):
    f32, i32 = jnp.float32, jnp.int32
    az, near, far = lax.axis_size(AZ), lax.axis_size(NEAR), lax.axis_size(FAR)
    bins, pulses_local = sar_image.shape[1:]
    table = tables()
    a_index = lax.axis_index(AZ).astype(i32).reshape(1)
    tile = (SUB, SIDE)
    moved_tiles = pltpu.VMEM((2 * bins * SUB, SIDE), f32)

    packed, place = call(
        pack_kernel,
        [((az * 8,) + tile, f32), ((bins,), i32)],
        [HBM, HBM],
        strong_index,
        sar_image,
        scratch=[
            pltpu.SMEM(strong_index.shape, i32),
            pltpu.VMEM(sar_image.shape, f32),
            moved_tiles,
            pltpu.SemaphoreType.DMA,
            pltpu.SemaphoreType.DMA((2,)),
        ],
        out_specs=[VMEM, SMEM],
    )
    rows = exchange(packed.reshape((az, 8) + tile), AZ)
    sums = call(
        first_kernel,
        [((2 * TILES,) + tile, f32)],
        [SMEM] * 3 + [VMEM] * 4,
        a_index,
        shifts,
        widths,
        rows,
        table["window"],
        table["right"],
        table["twist"],
        scratch=[pltpu.VMEM((4, SIDE + LOAD, SIDE), f32)],
    )
    history = call(
        history_kernel,
        [((4, 2, SIDE, SIDE), f32)],
        [VMEM] * 4,
        rows,
        table["right"],
        table["right_t"],
        table["twist"],
    )

    def all_sums(sums):
        each = 2 * TILES // near
        scattered = exchange(sums.reshape((near, each) + tile), NEAR)
        partial = call(share_kernel, [((far, each) + tile, f32)], [VMEM], scattered)
        everyone = exchange(partial, FAR)
        whole = call(share_kernel, [((near, each) + tile, f32)], [VMEM], everyone)
        return exchange(whole, NEAR).reshape((2 * TILES,) + tile)

    summed = all_sums(sums)
    sums, total = call(
        second_kernel,
        [((2 * TILES,) + tile, f32), ((SIDE, SIDE), f32)],
        [SMEM] * 3 + [VMEM] * 7,
        a_index,
        shifts,
        widths,
        summed,
        history,
        table["window"],
        table["ring"],
        table["right"],
        table["right_t"],
        table["twist"],
    )
    summed = all_sums(sums)
    corrected, phase = call(
        final_kernel,
        [((az, 8) + tile, f32), (tile, f32)],
        [SMEM] + [VMEM] * 6,
        a_index,
        summed,
        total,
        history,
        table["right"],
        table["right_t"],
        table["twist"],
        scratch=[pltpu.VMEM((SIDE, SIDE), f32)],
    )
    returned = exchange(corrected, AZ)
    focused = call(
        unpack_kernel,
        [(sar_image.shape, f32)],
        [SMEM, VMEM],
        place,
        returned.reshape((az * 8,) + tile),
        scratch=[pltpu.VMEM(sar_image.shape, f32), moved_tiles, pltpu.SemaphoreType.DMA((4,))],
        out_specs=[HBM],
    )
    return focused, phase.reshape(pulses_local)


def solution(mesh):
    rng, az = mesh.devices.shape
    along_x = max(1, min(4, rng // 2))
    split = Mesh(
        mesh.devices.reshape(rng // (2 * along_x), 2, along_x, az // 4, 2, 2), RNG + AZ
    )
    placed = (P(None, RNG, AZ), P(RNG), P(RNG), P(RNG))
    return jax.shard_map(
        local,
        mesh=split,
        in_specs=placed,
        out_specs=(P(None, RNG, AZ), P(AZ)),
        check_vma=False,
    )
```

```python
import jax
import jax.numpy as jnp
import numpy as np
from jax import lax
from jax.experimental import pallas as pl
from jax.experimental.pallas import tpu as pltpu
from jax.sharding import Mesh, PartitionSpec as P

EPSILON = 1e-06
SIDE = 128
SUB = 8
TILES = SIDE // SUB
WINDOW = 16
FIRST = SIDE // 2 - WINDOW // 2
LOAD = 24
HIGHEST = lax.Precision.HIGHEST


def tables():
    grid = np.arange(SIDE)
    product = grid[:, None] * grid[None, :]
    angle = 2.0 * np.pi * (product % SIDE) / SIDE
    cosine, sine = np.cos(angle), np.sin(angle)
    right = np.block([[cosine, -sine], [sine, cosine]])
    rows = slice(FIRST, FIRST + WINDOW)
    window = np.block([[cosine[:, rows], sine[:, rows]], [-sine[:, rows], cosine[:, rows]]])
    around = np.arange(SIDE + LOAD) % SIDE
    ring = np.stack([cosine[around], sine[around]])
    twist = 2.0 * np.pi * product / (SIDE * SIDE)
    twist = np.stack([np.cos(twist), np.sin(twist)]) / SIDE
    made = dict(right=right, right_t=right.T, window=window, ring=ring, twist=twist)
    return {name: jnp.asarray(np.ascontiguousarray(table).astype(np.float32)) for name, table in made.items()}


def multiply(left, right):
    return jnp.dot(left, right, precision=HIGHEST, preferred_element_type=jnp.float32)


def forward(lines, left, right, twist_ref):
    cosine, sine = twist_ref[0], twist_ref[1]
    stacked = jnp.concatenate([jnp.concatenate(line, axis=0) for line in lines], axis=1)
    first = multiply(left, stacked)
    turned = []
    for at in range(len(lines)):
        real = first[:SIDE, at * SIDE : (at + 1) * SIDE]
        imag = first[SIDE:, at * SIDE : (at + 1) * SIDE]
        turned.append(jnp.concatenate([real * cosine + imag * sine, imag * cosine - real * sine], axis=1))
    second = multiply(jnp.concatenate(turned, axis=0), right)
    return [
        (second[at * SIDE : (at + 1) * SIDE, :SIDE], second[at * SIDE : (at + 1) * SIDE, SIDE:])
        for at in range(len(lines))
    ]


def inverse_start(lines, right_t, twist_ref):
    cosine, sine = twist_ref[0], twist_ref[1]
    stacked = jnp.concatenate([jnp.concatenate(line, axis=1) for line in lines], axis=0)
    first = multiply(stacked, right_t)
    turned = []
    for at in range(len(lines)):
        real = first[at * SIDE : (at + 1) * SIDE, :SIDE]
        imag = first[at * SIDE : (at + 1) * SIDE, SIDE:]
        turned.append(jnp.concatenate([real * cosine - imag * sine, imag * cosine + real * sine], axis=0))
    return turned


def grid_of(rows):
    return (
        lax.broadcasted_iota(jnp.int32, (rows, SIDE), 0),
        lax.broadcasted_iota(jnp.int32, (rows, SIDE), 1),
    )


def running_sum(gradient):
    rows, cols = grid_of(SIDE)
    within = multiply((cols <= rows).astype(jnp.float32), gradient)
    sums = jnp.broadcast_to(jnp.sum(gradient, axis=0, keepdims=True), (SUB, SIDE))
    before = multiply(sums, (rows < cols).astype(jnp.float32))
    return within + before[:1, :]


def phase_of(sums_ref):
    gradient = sums_ref[:TILES] / (sums_ref[TILES:] + EPSILON)
    return running_sum(gradient.reshape(SIDE, SIDE))


def cosine_sine(angle):
    quarters = jnp.floor(angle * (2.0 / np.pi) + 0.5)
    rest = angle - quarters * 1.5703125
    rest = rest - quarters * 4.837512969970703125e-4
    rest = rest - quarters * 7.54978995489188216e-8
    square = rest * rest
    sine = ((-1.9515295891e-4 * square + 8.3321608736e-3) * square - 1.6666654611e-1) * square * rest + rest
    cosine = (2.443315711809948e-5 * square - 1.388731625493765e-3) * square + 4.166664568298827e-2
    cosine = cosine * square * square - 0.5 * square + 1.0
    turn = quarters.astype(jnp.int32)
    odd = (turn & 1) == 1
    sine, cosine = jnp.where(odd, cosine, sine), jnp.where(odd, sine, cosine)
    return jnp.where(((turn + 1) & 2) == 2, -cosine, cosine), jnp.where((turn & 2) == 2, -sine, sine)


def turn_back(lines, total):
    cosine, sine = cosine_sine(total)
    return [(real * cosine + imag * sine, imag * cosine - real * sine) for real, imag in lines]


def row_offset(shift):
    begin = (shift + SIDE * SIDE // 2) & (SIDE * SIDE - 1)
    return ((begin >> 7) + FIRST) & (SIDE - 1), begin & (SIDE - 1)


def center(upper, lower, lane, width):
    rows, cols = grid_of(WINDOW)
    turn = (SIDE - lane) & (SIDE - 1)
    moved = jnp.where(cols >= SIDE - lane, pltpu.roll(lower, turn, 1), pltpu.roll(upper, turn, 1))
    cells = (rows + FIRST) * SIDE + cols
    least = SIDE * SIDE // 2 - width // 2
    return jnp.where((cells >= least) & (cells < least + width), moved, 0.0)


def gradient_sums(lines, out_ref):
    rows, cols = grid_of(SIDE)
    numerator = jnp.zeros((SIDE, SIDE), jnp.float32)
    denominator = jnp.zeros((SIDE, SIDE), jnp.float32)

    def before(part):
        down = pltpu.roll(part, 1, 0)
        return jnp.where(rows == 0, pltpu.roll(down, 1, 1), down)

    for real, imag in lines:
        numerator = numerator + (before(real) * imag - before(imag) * real)
        denominator = denominator + (real * real + imag * imag)
    numerator = jnp.where((rows == 0) & (cols == 0), 0.0, numerator)
    out_ref[:TILES] = numerator.reshape(TILES, SUB, SIDE)
    out_ref[TILES:] = denominator.reshape(TILES, SUB, SIDE)


def tile_at(bins, part, row):
    return (part * (bins // SUB) + row // SUB) * SUB * SUB + row % SUB


def pack_kernel(
    strong_hbm, shifts_hbm, widths_hbm, image_hbm, out_hbm, at_ref,
    place_ref, strong_ref, shifts_ref, widths_ref, image_ref, tiles_ref, out_ref, small_sems, sems, out_sems,
):
    bins = image_ref.shape[1]
    strong = strong_ref.shape[0]
    indices = pltpu.make_async_copy(strong_hbm, strong_ref, small_sems.at[0])
    indices.start()
    parts = [pltpu.make_async_copy(image_hbm.at[part], image_ref.at[part], sems.at[part]) for part in range(2)]
    for part in parts:
        part.start()
    others_in = [
        pltpu.make_async_copy(shifts_hbm, shifts_ref, small_sems.at[1]),
        pltpu.make_async_copy(widths_hbm, widths_ref, small_sems.at[2]),
    ]
    for copy in others_in:
        copy.start()
    for row in range(bins):
        place_ref[row] = -1
    indices.wait()
    for at in range(strong):
        place_ref[strong_ref[at] % bins] = at // 2 * 8 + at % 2
    others = jnp.int32(0)
    for row in range(bins):
        held = place_ref[row]
        place = jnp.where(held < 0, others // 2 * 8 + others % 2 + 2, held)
        place_ref[row] = place
        at_ref[SUB + row : SUB + row + 1, :] = jnp.full((1, SIDE), place, jnp.int32)
        others = others + jnp.where(held < 0, 1, 0)
    for copy in others_in:
        copy.wait()
    for at in range(2):
        line = lax.axis_index(AZ) * 2 + at
        for where, value in enumerate(row_offset(shifts_ref[line]) + (widths_ref[line],)):
            at_ref[4 * at + where : 4 * at + where + 1, :] = jnp.full((1, SIDE), value, jnp.int32)
    copies = []
    for part in range(2):
        parts[part].wait()
        for group in range(bins // SUB):
            for block in range(SUB):
                at = ((part * (bins // SUB) + group) * SUB + block) * SUB
                tiles_ref[at : at + SUB, :] = image_ref[
                    part, group * SUB : (group + 1) * SUB, block * SIDE : (block + 1) * SIDE
                ]
        for row in range(bins):
            out_ref[part, place_ref[row] // 8, place_ref[row] % 8] = tiles_ref[
                pl.ds(tile_at(bins, part, row), SUB, stride=SUB), :
            ]
        copies.append(
            pltpu.make_async_copy(out_ref.at[part], out_hbm.at[:, pl.ds(part * 4, 4)], out_sems.at[part])
        )
        copies[-1].start()
    for copy in copies:
        copy.wait()


def unpack_kernel(at_ref, rows_ref, phase_ref, image_hbm, phase_hbm, image_ref, tiles_ref, sems):
    bins = image_ref.shape[1]
    copies = [pltpu.make_async_copy(phase_ref, phase_hbm, sems.at[4])]
    copies[0].start()
    places = [at_ref[SUB + row, 0] for row in range(bins)]
    for part in range(2):
        for row in range(bins):
            tiles_ref[pl.ds(tile_at(bins, part, row), SUB, stride=SUB), :] = rows_ref[places[row] + part * 4]
        for half in range(2):
            span = slice(half * bins // 2, (half + 1) * bins // 2)
            for group in range(half * bins // 2 // SUB, (half + 1) * bins // 2 // SUB):
                for block in range(SUB):
                    at = ((part * (bins // SUB) + group) * SUB + block) * SUB
                    image_ref[part, group * SUB : (group + 1) * SUB, block * SIDE : (block + 1) * SIDE] = tiles_ref[
                        at : at + SUB, :
                    ]
            copies.append(
                pltpu.make_async_copy(
                    image_ref.at[part, span], image_hbm.at[part, span], sems.at[part * 2 + half]
                )
            )
            copies[-1].start()
    for copy in copies:
        copy.wait()


def offsets(at_ref, line):
    return [at_ref[4 * line + where, 0] for where in range(3)]


def first_kernel(at_ref, rows_ref, window_ref, right_ref, twist_ref, out_ref, ring_ref):
    lines = []
    for at in range(2):
        row, lane, width = offsets(at_ref, at)
        parts = []
        for part in range(2):
            ring = ring_ref.at[at * 2 + part]
            ring[:SIDE, :] = rows_ref[:, part * 4 + at].reshape(SIDE, SIDE)
            ring[SIDE:, :] = rows_ref[: LOAD // SUB, part * 4 + at].reshape(LOAD, SIDE)
            parts.append(center(ring[pl.ds(row, WINDOW), :], ring[pl.ds(row + 1, WINDOW), :], lane, width))
        lines.append(parts)
    gradient_sums(forward(lines, window_ref[...], right_ref[...], twist_ref), out_ref)


def history_kernel(rows_ref, right_ref, right_t_ref, twist_ref, out_ref):
    lines = [[rows_ref[:, part * 4 + at].reshape(SIDE, SIDE) for part in range(2)] for at in range(4)]
    for at, (real, imag) in enumerate(forward(lines, right_t_ref[...], right_ref[...], twist_ref)):
        out_ref[at, 0] = real
        out_ref[at, 1] = imag


def share_kernel(in_ref, out_ref):
    out_ref[...] = jnp.broadcast_to(jnp.sum(in_ref[...], axis=0)[None], out_ref.shape)


def second_kernel(
    at_ref, sums_ref, history_ref, window_ref, ring_ref, right_ref, right_t_ref, twist_ref,
    out_ref, total_ref,
):
    total = phase_of(sums_ref)
    total_ref[...] = total
    lines = turn_back([(history_ref[at, 0], history_ref[at, 1]) for at in range(2)], total)
    centered = []
    for at, started in enumerate(inverse_start(lines, right_t_ref[...], twist_ref)):
        row, lane, width = offsets(at_ref, at)
        cosine, sine = ring_ref[0, pl.ds(row, LOAD), :], ring_ref[1, pl.ds(row, LOAD), :]
        left = [jnp.concatenate([cosine, -sine], axis=1), jnp.concatenate([sine, cosine], axis=1)]
        found = multiply(jnp.concatenate(left, axis=0), started)
        centered.append(
            [
                center(found[from_row : from_row + WINDOW], found[from_row + 1 : from_row + 1 + WINDOW], lane, width)
                for from_row in (0, LOAD)
            ]
        )
    gradient_sums(forward(centered, window_ref[...], right_ref[...], twist_ref), out_ref)


def final_kernel(
    sums_ref, total_ref, history_ref, right_ref, right_t_ref, twist_ref, out_ref, phase_ref, turned_ref
):
    total = total_ref[...] + phase_of(sums_ref)
    lines = turn_back([(history_ref[at, 0], history_ref[at, 1]) for at in range(4)], total)
    found = multiply(right_ref[...], jnp.concatenate(inverse_start(lines, right_t_ref[...], twist_ref), axis=1))
    for at in range(4):
        for part in range(2):
            line = found[part * SIDE : (part + 1) * SIDE, at * SIDE : (at + 1) * SIDE]
            out_ref[:, part * 4 + at] = line.reshape(TILES, SUB, SIDE)
    turned_ref[...] = total.T
    phase_ref[...] = turned_ref[pl.ds(pl.multiple_of(lax.axis_index(AZ) * SUB, SUB), SUB), :]


SMEM = pl.BlockSpec(memory_space=pltpu.SMEM)
VMEM = pl.BlockSpec(memory_space=pltpu.VMEM)
HBM = pl.BlockSpec(memory_space=pltpu.HBM)
PACK_VMEM = 60 * 1024 * 1024


def call(kernel, shapes, specs, *operands, scratch=(), out_specs=None, vmem=32 * 1024 * 1024):
    out = pl.pallas_call(
        kernel,
        out_shape=[jax.ShapeDtypeStruct(*shape) for shape in shapes],
        in_specs=list(specs),
        out_specs=out_specs or [VMEM] * len(shapes),
        scratch_shapes=list(scratch),
        compiler_params=pltpu.CompilerParams(vmem_limit_bytes=vmem),
    )(*operands)
    return out if len(out) > 1 else out[0]


def exchange(array, axes):
    return lax.all_to_all(array, axes, split_axis=0, concat_axis=0, tiled=True)


RNG = ("zh", "zl", "x")
AZ = ("yh", "yl", "core")
NEAR = ("zl", "x", "yl", "core")
FAR = ("zh", "yh")


def local(sar_image, strong_index, shifts, widths):
    f32, i32 = jnp.float32, jnp.int32
    az, near, far = lax.axis_size(AZ), lax.axis_size(NEAR), lax.axis_size(FAR)
    bins, pulses_local = sar_image.shape[1:]
    table = tables()
    tile = (SUB, SIDE)
    moved_tiles = pltpu.VMEM((2 * bins * SUB, SIDE), f32)

    packed, places = call(
        pack_kernel,
        [((az, 8) + tile, f32), ((SUB + bins, SIDE), i32)],
        [HBM] * 4,
        strong_index,
        shifts,
        widths,
        sar_image,
        scratch=[pltpu.SMEM((bins,), i32)]
        + [pltpu.SMEM(strong_index.shape, i32) for _ in range(3)]
        + [
            pltpu.VMEM(sar_image.shape, f32),
            moved_tiles,
            pltpu.VMEM((2, az, 4) + tile, f32),
            pltpu.SemaphoreType.DMA((3,)),
            pltpu.SemaphoreType.DMA((2,)),
            pltpu.SemaphoreType.DMA((2,)),
        ],
        out_specs=[HBM, VMEM],
        vmem=PACK_VMEM,
    )
    rows = exchange(packed, AZ)
    sums = call(
        first_kernel,
        [((2 * TILES,) + tile, f32)],
        [VMEM] * 5,
        places,
        rows,
        table["window"],
        table["right"],
        table["twist"],
        scratch=[pltpu.VMEM((4, SIDE + LOAD, SIDE), f32)],
    )
    history = call(
        history_kernel,
        [((4, 2, SIDE, SIDE), f32)],
        [VMEM] * 4,
        rows,
        table["right"],
        table["right_t"],
        table["twist"],
    )

    def all_sums(sums):
        each = 2 * TILES // near
        scattered = exchange(sums.reshape((near, each) + tile), NEAR)
        partial = call(share_kernel, [((far, each) + tile, f32)], [VMEM], scattered)
        everyone = exchange(partial, FAR)
        whole = call(share_kernel, [((near, each) + tile, f32)], [VMEM], everyone)
        return exchange(whole, NEAR).reshape((2 * TILES,) + tile)

    summed = all_sums(sums)
    sums, total = call(
        second_kernel,
        [((2 * TILES,) + tile, f32), ((SIDE, SIDE), f32)],
        [VMEM] * 8,
        places,
        summed,
        history,
        table["window"],
        table["ring"],
        table["right"],
        table["right_t"],
        table["twist"],
    )
    summed = all_sums(sums)
    corrected, phase = call(
        final_kernel,
        [((az, 8) + tile, f32), (tile, f32)],
        [VMEM] * 6,
        summed,
        total,
        history,
        table["right"],
        table["right_t"],
        table["twist"],
        scratch=[pltpu.VMEM((SIDE, SIDE), f32)],
    )
    returned = exchange(corrected, AZ)
    focused, phase = call(
        unpack_kernel,
        [(sar_image.shape, f32), (tile, f32)],
        [VMEM, VMEM, VMEM],
        places,
        returned.reshape((az * 8,) + tile),
        phase,
        scratch=[pltpu.VMEM(sar_image.shape, f32), moved_tiles, pltpu.SemaphoreType.DMA((5,))],
        out_specs=[HBM, HBM],
    )
    return focused, phase.reshape(pulses_local)


def solution(mesh):
    rng, az = mesh.devices.shape
    along_x = max(1, min(4, rng // 2))
    split = Mesh(
        mesh.devices.reshape(rng // (2 * along_x), 2, along_x, az // 4, 2, 2), RNG + AZ
    )
    placed = (P(None, RNG, AZ), P(RNG), P(RNG), P(RNG))
    return jax.shard_map(
        local,
        mesh=split,
        in_specs=placed,
        out_specs=(P(None, RNG, AZ), P(AZ)),
        check_vma=False,
    )
```

```python
import jax
import jax.numpy as jnp
import numpy as np
from jax import lax
from jax.experimental import pallas as pl
from jax.experimental.pallas import tpu as pltpu
from jax.sharding import Mesh, PartitionSpec as P

EPSILON = 1e-06
SIDE = 128
SUB = 8
TILES = SIDE // SUB
WINDOW = 16
FIRST = SIDE // 2 - WINDOW // 2
LOAD = 24


def tables():
    grid = np.arange(SIDE)
    product = grid[:, None] * grid[None, :]
    angle = 2.0 * np.pi * (product % SIDE) / SIDE
    cosine, sine = np.cos(angle), np.sin(angle)
    right = np.block([[cosine, -sine], [sine, cosine]])
    rows = slice(FIRST, FIRST + WINDOW)
    window = np.block([[cosine[:, rows], sine[:, rows]], [-sine[:, rows], cosine[:, rows]]])
    around = np.arange(SIDE + LOAD) % SIDE
    ring = np.stack([cosine[around], sine[around]])
    twist = 2.0 * np.pi * product / (SIDE * SIDE)
    twist = np.stack([np.cos(twist), np.sin(twist)]) / SIDE
    made = dict(ring=ring, twist=twist)
    made = {name: jnp.asarray(table.astype(np.float32)) for name, table in made.items()}
    for name, table in dict(right=right, right_t=right.T, window=window).items():
        parts, rest = [], table.astype(np.float32)
        for _ in range(3):
            parts.append(rest.astype(jnp.bfloat16))
            rest = rest - parts[-1].astype(np.float32)
        if name == "window":
            made[name] = jnp.asarray(np.concatenate([parts[at] for at in (0, 0, 1, 0, 1, 2)], axis=1))
        else:
            made[name] = jnp.asarray(np.concatenate(parts, axis=0))
    return made


def split(array, count):
    parts = []
    for _ in range(count):
        parts.append(array.astype(jnp.bfloat16))
        array = array - parts[-1].astype(jnp.float32)
    return parts


def dot(left, right):
    return jnp.dot(left, right, preferred_element_type=jnp.float32)


def stack(array, count=3):
    return jnp.concatenate(split(array, count), axis=0)


def multiply(left, right):
    count = len(right)
    rows = left.shape[0] // count
    by_order = [None] * count
    for at in range(count):
        product = dot(left[: (count - at) * rows], right[at])
        for order in range(count - at):
            term = product[order * rows : (order + 1) * rows]
            by_order[at + order] = term if by_order[at + order] is None else by_order[at + order] + term
    total = by_order[-1]
    for term in reversed(by_order[:-1]):
        total = total + term
    return total


def multiply_window(left, right):
    first, second, third = split(right, 3)
    return dot(left, jnp.concatenate([first, second, first, third, second, first], axis=0))


def forward(lines, first_stage, right_ref, twist_ref):
    cosine, sine = twist_ref[0], twist_ref[1]
    first = first_stage(jnp.concatenate([jnp.concatenate(line, axis=0) for line in lines], axis=1))
    turned = []
    for at in range(len(lines)):
        real = first[:SIDE, at * SIDE : (at + 1) * SIDE]
        imag = first[SIDE:, at * SIDE : (at + 1) * SIDE]
        turned.append(jnp.concatenate([real * cosine + imag * sine, imag * cosine - real * sine], axis=1))
    second = multiply(stack(jnp.concatenate(turned, axis=0)), parts_of(right_ref))
    return [
        (second[at * SIDE : (at + 1) * SIDE, :SIDE], second[at * SIDE : (at + 1) * SIDE, SIDE:])
        for at in range(len(lines))
    ]


def inverse_start(lines, right_t_ref, twist_ref, count=3):
    cosine, sine = twist_ref[0], twist_ref[1]
    stacked = jnp.concatenate([jnp.concatenate(line, axis=1) for line in lines], axis=0)
    first = multiply(stack(stacked, count), parts_of(right_t_ref, count))
    turned = []
    for at in range(len(lines)):
        real = first[at * SIDE : (at + 1) * SIDE, :SIDE]
        imag = first[at * SIDE : (at + 1) * SIDE, SIDE:]
        turned.append(jnp.concatenate([real * cosine - imag * sine, imag * cosine + real * sine], axis=0))
    return turned


def parts_of(table_ref, count=3):
    return [table_ref[at * 2 * SIDE : (at + 1) * 2 * SIDE, :] for at in range(count)]


def grid_of(rows):
    return (
        lax.broadcasted_iota(jnp.int32, (rows, SIDE), 0),
        lax.broadcasted_iota(jnp.int32, (rows, SIDE), 1),
    )


def running_sum(gradient):
    rows, cols = grid_of(SIDE)
    within = dot(
        (cols <= rows).astype(jnp.float32).astype(jnp.bfloat16), jnp.concatenate(split(gradient, 3), axis=1)
    )
    sums = jnp.broadcast_to(jnp.sum(gradient, axis=0, keepdims=True), (16, SIDE))
    before = dot(
        jnp.concatenate(split(sums, 3), axis=0), (rows < cols).astype(jnp.float32).astype(jnp.bfloat16)
    )
    within = within[:, :SIDE] + (within[:, SIDE : 2 * SIDE] + within[:, 2 * SIDE :])
    return within + (before[:1, :] + (before[16:17, :] + before[32:33, :]))


def phase_of(sums_ref):
    gradient = sums_ref[:TILES] / (sums_ref[TILES:] + EPSILON)
    return running_sum(gradient.reshape(SIDE, SIDE))


def cosine_sine(angle):
    quarters = jnp.floor(angle * (2.0 / np.pi) + 0.5)
    rest = angle - quarters * 1.5703125
    rest = rest - quarters * 4.837512969970703125e-4
    rest = rest - quarters * 7.54978995489188216e-8
    square = rest * rest
    sine = ((-1.9515295891e-4 * square + 8.3321608736e-3) * square - 1.6666654611e-1) * square * rest + rest
    cosine = (2.443315711809948e-5 * square - 1.388731625493765e-3) * square + 4.166664568298827e-2
    cosine = cosine * square * square - 0.5 * square + 1.0
    turn = quarters.astype(jnp.int32)
    odd = (turn & 1) == 1
    sine, cosine = jnp.where(odd, cosine, sine), jnp.where(odd, sine, cosine)
    return jnp.where(((turn + 1) & 2) == 2, -cosine, cosine), jnp.where((turn & 2) == 2, -sine, sine)


def turn_back(lines, total):
    cosine, sine = cosine_sine(total)
    return [(real * cosine + imag * sine, imag * cosine - real * sine) for real, imag in lines]


def row_offset(shift):
    begin = (shift + SIDE * SIDE // 2) & (SIDE * SIDE - 1)
    return ((begin >> 7) + FIRST) & (SIDE - 1), begin & (SIDE - 1)


def center(upper, lower, lane, width):
    rows, cols = grid_of(WINDOW)
    turn = (SIDE - lane) & (SIDE - 1)
    moved = jnp.where(cols >= SIDE - lane, pltpu.roll(lower, turn, 1), pltpu.roll(upper, turn, 1))
    cells = (rows + FIRST) * SIDE + cols
    least = SIDE * SIDE // 2 - width // 2
    return jnp.where((cells >= least) & (cells < least + width), moved, 0.0)


def gradient_sums(lines, out_ref):
    rows, cols = grid_of(SIDE)
    numerator = jnp.zeros((SIDE, SIDE), jnp.float32)
    denominator = jnp.zeros((SIDE, SIDE), jnp.float32)

    def before(part):
        down = pltpu.roll(part, 1, 0)
        return jnp.where(rows == 0, pltpu.roll(down, 1, 1), down)

    for real, imag in lines:
        numerator = numerator + (before(real) * imag - before(imag) * real)
        denominator = denominator + (real * real + imag * imag)
    numerator = jnp.where((rows == 0) & (cols == 0), 0.0, numerator)
    out_ref[:TILES] = numerator.reshape(TILES, SUB, SIDE)
    out_ref[TILES:] = denominator.reshape(TILES, SUB, SIDE)


def tile_at(bins, part, row):
    return (part * (bins // SUB) + row // SUB) * SUB * SUB + row % SUB


def pack_kernel(
    strong_hbm, shifts_hbm, widths_hbm, image_hbm, out_hbm, at_ref,
    place_ref, strong_ref, shifts_ref, widths_ref, image_ref, tiles_ref, out_ref, small_sems, sems, out_sems,
):
    bins = image_ref.shape[1]
    strong = strong_ref.shape[0]
    half = bins // 2
    indices = pltpu.make_async_copy(strong_hbm, strong_ref, small_sems.at[0])
    indices.start()
    chunks = []
    for part in range(2):
        for at in range(2):
            span = slice(at * half, (at + 1) * half)
            chunks.append(
                pltpu.make_async_copy(image_hbm.at[part, span], image_ref.at[part, span], sems.at[part * 2 + at])
            )
            chunks[-1].start()
    others_in = [
        pltpu.make_async_copy(shifts_hbm, shifts_ref, small_sems.at[1]),
        pltpu.make_async_copy(widths_hbm, widths_ref, small_sems.at[2]),
    ]
    for copy in others_in:
        copy.start()
    for row in range(bins):
        place_ref[row] = -1
    indices.wait()
    for at in range(strong):
        place_ref[strong_ref[at] & (bins - 1)] = at // 2 * 8 + at % 2
    others = jnp.int32(0)
    places = []
    for row in range(bins):
        held = place_ref[row]
        place = jnp.where(held < 0, ((others >> 1) << 3) + (others & 1) + 2, held)
        others = others + jnp.where(held < 0, 1, 0)
        places.append(place)
        at_ref[SUB + row : SUB + row + 1, :] = jnp.full((1, SIDE), place, jnp.int32)
    copies = []
    for part in range(2):
        for at in range(2):
            chunks[part * 2 + at].wait()
            for group in range(at * half // SUB, (at + 1) * half // SUB):
                for block in range(SUB):
                    tile = ((part * (bins // SUB) + group) * SUB + block) * SUB
                    tiles_ref[tile : tile + SUB, :] = image_ref[
                        part, group * SUB : (group + 1) * SUB, block * SIDE : (block + 1) * SIDE
                    ]
            for row in range(at * half, (at + 1) * half):
                out_ref[part, places[row] >> 3, places[row] & 3] = tiles_ref[
                    pl.ds(tile_at(bins, part, row), SUB, stride=SUB), :
                ]
        copies.append(
            pltpu.make_async_copy(out_ref.at[part], out_hbm.at[:, pl.ds(part * 4, 4)], out_sems.at[part])
        )
        copies[-1].start()
    for copy in others_in:
        copy.wait()
    for at in range(2):
        line = lax.axis_index(AZ) * 2 + at
        for where, value in enumerate(row_offset(shifts_ref[line]) + (widths_ref[line],)):
            at_ref[4 * at + where : 4 * at + where + 1, :] = jnp.full((1, SIDE), value, jnp.int32)
    for copy in copies:
        copy.wait()


def unpack_kernel(at_ref, rows_ref, phase_ref, image_hbm, phase_hbm, image_ref, tiles_ref, sems):
    bins = image_ref.shape[1]
    copies = [pltpu.make_async_copy(phase_ref, phase_hbm, sems.at[4])]
    copies[0].start()
    places = [at_ref[SUB + row, 0] for row in range(bins)]
    for part in range(2):
        for row in range(bins):
            tiles_ref[pl.ds(tile_at(bins, part, row), SUB, stride=SUB), :] = rows_ref[places[row] + part * 4]
        for half in range(2):
            span = slice(half * bins // 2, (half + 1) * bins // 2)
            for group in range(half * bins // 2 // SUB, (half + 1) * bins // 2 // SUB):
                for block in range(SUB):
                    at = ((part * (bins // SUB) + group) * SUB + block) * SUB
                    image_ref[part, group * SUB : (group + 1) * SUB, block * SIDE : (block + 1) * SIDE] = tiles_ref[
                        at : at + SUB, :
                    ]
            copies.append(
                pltpu.make_async_copy(
                    image_ref.at[part, span], image_hbm.at[part, span], sems.at[part * 2 + half]
                )
            )
            copies[-1].start()
    for copy in copies:
        copy.wait()


def offsets(at_ref, line):
    return [at_ref[4 * line + where, 0] for where in range(3)]


def first_kernel(at_ref, rows_ref, window_ref, right_ref, twist_ref, out_ref, ring_ref):
    lines = []
    for at in range(2):
        row, lane, width = offsets(at_ref, at)
        parts = []
        for part in range(2):
            ring = ring_ref.at[at * 2 + part]
            ring[:SIDE, :] = rows_ref[:, part * 4 + at].reshape(SIDE, SIDE)
            ring[SIDE:, :] = rows_ref[: LOAD // SUB, part * 4 + at].reshape(LOAD, SIDE)
            parts.append(center(ring[pl.ds(row, WINDOW), :], ring[pl.ds(row + 1, WINDOW), :], lane, width))
        lines.append(parts)
    gradient_sums(forward(lines, lambda lines: multiply_window(window_ref[...], lines), right_ref, twist_ref), out_ref)


def history_kernel(rows_ref, right_ref, right_t_ref, twist_ref, out_ref):
    lines = [[rows_ref[:, part * 4 + at].reshape(SIDE, SIDE) for part in range(2)] for at in range(4)]
    for at, (real, imag) in enumerate(forward(lines, lambda lines: multiply(right_t_ref[...], split(lines, 3)), right_ref, twist_ref)):
        out_ref[at, 0] = real
        out_ref[at, 1] = imag


def share_kernel(in_ref, out_ref):
    out_ref[...] = jnp.broadcast_to(jnp.sum(in_ref[...], axis=0)[None], out_ref.shape)


def second_kernel(
    at_ref, sums_ref, history_ref, window_ref, ring_ref, right_ref, right_t_ref, twist_ref,
    out_ref, total_ref,
):
    total = phase_of(sums_ref)
    total_ref[...] = total
    lines = turn_back([(history_ref[at, 0], history_ref[at, 1]) for at in range(2)], total)
    centered = []
    for at, started in enumerate(inverse_start(lines, right_t_ref, twist_ref)):
        row, lane, width = offsets(at_ref, at)
        cosine, sine = ring_ref[0, pl.ds(row, LOAD), :], ring_ref[1, pl.ds(row, LOAD), :]
        left = [jnp.concatenate([cosine, -sine], axis=1), jnp.concatenate([sine, cosine], axis=1)]
        found = multiply(stack(jnp.concatenate(left, axis=0)), split(started, 3))
        centered.append(
            [
                center(found[from_row : from_row + WINDOW], found[from_row + 1 : from_row + 1 + WINDOW], lane, width)
                for from_row in (0, LOAD)
            ]
        )
    gradient_sums(forward(centered, lambda lines: multiply_window(window_ref[...], lines), right_ref, twist_ref), out_ref)


def final_kernel(
    sums_ref, total_ref, history_ref, right_ref, right_t_ref, twist_ref, out_ref, phase_ref, turned_ref
):
    total = total_ref[...] + phase_of(sums_ref)
    lines = turn_back([(history_ref[at, 0], history_ref[at, 1]) for at in range(4)], total)
    started = inverse_start(lines, right_t_ref, twist_ref, 2)
    found = multiply(right_ref[: 4 * SIDE, :], split(jnp.concatenate(started, axis=1), 2))
    for at in range(4):
        for part in range(2):
            line = found[part * SIDE : (part + 1) * SIDE, at * SIDE : (at + 1) * SIDE]
            out_ref[:, part * 4 + at] = line.reshape(TILES, SUB, SIDE)
    turned_ref[...] = total.T
    phase_ref[...] = turned_ref[pl.ds(pl.multiple_of(lax.axis_index(AZ) * SUB, SUB), SUB), :]


SMEM = pl.BlockSpec(memory_space=pltpu.SMEM)
VMEM = pl.BlockSpec(memory_space=pltpu.VMEM)
HBM = pl.BlockSpec(memory_space=pltpu.HBM)
PACK_VMEM = 60 * 1024 * 1024


def call(kernel, shapes, specs, *operands, scratch=(), out_specs=None, vmem=32 * 1024 * 1024):
    out = pl.pallas_call(
        kernel,
        out_shape=[jax.ShapeDtypeStruct(*shape) for shape in shapes],
        in_specs=list(specs),
        out_specs=out_specs or [VMEM] * len(shapes),
        scratch_shapes=list(scratch),
        compiler_params=pltpu.CompilerParams(vmem_limit_bytes=vmem),
    )(*operands)
    return out if len(out) > 1 else out[0]


def exchange(array, axes):
    return lax.all_to_all(array, axes, split_axis=0, concat_axis=0, tiled=True)


RNG = ("zh", "zl", "x")
AZ = ("yh", "yl", "core")
NEAR = ("zl", "x", "yl", "core")
FAR = ("zh", "yh")


def local(sar_image, strong_index, shifts, widths):
    f32, i32 = jnp.float32, jnp.int32
    az, near, far = lax.axis_size(AZ), lax.axis_size(NEAR), lax.axis_size(FAR)
    bins, pulses_local = sar_image.shape[1:]
    table = tables()
    tile = (SUB, SIDE)
    moved_tiles = pltpu.VMEM((2 * bins * SUB, SIDE), f32)

    packed, places = call(
        pack_kernel,
        [((az, 8) + tile, f32), ((SUB + bins, SIDE), i32)],
        [HBM] * 4,
        strong_index,
        shifts,
        widths,
        sar_image,
        scratch=[pltpu.SMEM((bins,), i32)]
        + [pltpu.SMEM(strong_index.shape, i32) for _ in range(3)]
        + [
            pltpu.VMEM(sar_image.shape, f32),
            moved_tiles,
            pltpu.VMEM((2, az, 4) + tile, f32),
            pltpu.SemaphoreType.DMA((3,)),
            pltpu.SemaphoreType.DMA((4,)),
            pltpu.SemaphoreType.DMA((2,)),
        ],
        out_specs=[HBM, VMEM],
        vmem=PACK_VMEM,
    )
    rows = exchange(packed, AZ)
    sums = call(
        first_kernel,
        [((2 * TILES,) + tile, f32)],
        [VMEM] * 5,
        places,
        rows,
        table["window"],
        table["right"],
        table["twist"],
        scratch=[pltpu.VMEM((4, SIDE + LOAD, SIDE), f32)],
    )
    history = call(
        history_kernel,
        [((4, 2, SIDE, SIDE), f32)],
        [VMEM] * 4,
        rows,
        table["right"],
        table["right_t"],
        table["twist"],
    )

    def all_sums(sums):
        each = 2 * TILES // near
        scattered = exchange(sums.reshape((near, each) + tile), NEAR)
        partial = call(share_kernel, [((far, each) + tile, f32)], [VMEM], scattered)
        everyone = exchange(partial, FAR)
        whole = call(share_kernel, [((near, each) + tile, f32)], [VMEM], everyone)
        return exchange(whole, NEAR).reshape((2 * TILES,) + tile)

    summed = all_sums(sums)
    sums, total = call(
        second_kernel,
        [((2 * TILES,) + tile, f32), ((SIDE, SIDE), f32)],
        [VMEM] * 8,
        places,
        summed,
        history,
        table["window"],
        table["ring"],
        table["right"],
        table["right_t"],
        table["twist"],
    )
    summed = all_sums(sums)
    corrected, phase = call(
        final_kernel,
        [((az, 8) + tile, f32), (tile, f32)],
        [VMEM] * 6,
        summed,
        total,
        history,
        table["right"],
        table["right_t"],
        table["twist"],
        scratch=[pltpu.VMEM((SIDE, SIDE), f32)],
    )
    returned = exchange(corrected, AZ)
    focused, phase = call(
        unpack_kernel,
        [(sar_image.shape, f32), (tile, f32)],
        [VMEM, VMEM, VMEM],
        places,
        returned.reshape((az * 8,) + tile),
        phase,
        scratch=[pltpu.VMEM(sar_image.shape, f32), moved_tiles, pltpu.SemaphoreType.DMA((5,))],
        out_specs=[HBM, HBM],
    )
    return focused, phase.reshape(pulses_local)


def solution(mesh):
    rng, az = mesh.devices.shape
    along_x = max(1, min(4, rng // 2))
    split = Mesh(
        mesh.devices.reshape(rng // (2 * along_x), 2, along_x, az // 4, 2, 2), RNG + AZ
    )
    placed = (P(None, RNG, AZ), P(RNG), P(RNG), P(RNG))
    return jax.shard_map(
        local,
        mesh=split,
        in_specs=placed,
        out_specs=(P(None, RNG, AZ), P(AZ)),
        check_vma=False,
    )
```

```python
import jax
import jax.numpy as jnp
import numpy as np
from jax import lax
from jax.experimental import pallas as pl
from jax.experimental.pallas import tpu as pltpu
from jax.sharding import Mesh, PartitionSpec as P

EPSILON = 1e-06
SIDE = 128
SUB = 8
TILES = SIDE // SUB
WINDOW = 16
FIRST = SIDE // 2 - WINDOW // 2
RIGHT, RIGHT_T = 0, 1
LOAD = 24


def tables():
    grid = np.arange(SIDE)
    product = grid[:, None] * grid[None, :]
    angle = 2.0 * np.pi * (product % SIDE) / SIDE
    cosine, sine = np.cos(angle), np.sin(angle)
    right = np.block([[cosine, -sine], [sine, cosine]])
    rows = slice(FIRST, FIRST + WINDOW)
    window = np.block([[cosine[:, rows], sine[:, rows]], [-sine[:, rows], cosine[:, rows]]])
    around = np.arange(SIDE + LOAD) % SIDE
    ring = np.stack([cosine[around], sine[around]])
    twist = 2.0 * np.pi * product / (SIDE * SIDE)
    twist = np.stack([np.cos(twist), np.sin(twist)]) / SIDE
    made = dict(ring=ring, twist=twist)
    made = {name: jnp.asarray(table.astype(np.float32)) for name, table in made.items()}

    def parts(table):
        found, rest = [], table.astype(np.float32)
        for _ in range(3):
            found.append(rest.astype(jnp.bfloat16))
            rest = rest - found[-1].astype(np.float32)
        return found

    window = parts(window)
    made["window"] = jnp.asarray(np.concatenate([window[at] for at in (0, 0, 1, 0, 1, 2)], axis=1))
    made["sides"] = jnp.asarray(np.concatenate(parts(right) + parts(right.T), axis=0))
    return made


def split(array, count):
    parts = []
    for _ in range(count):
        parts.append(array.astype(jnp.bfloat16))
        array = array - parts[-1].astype(jnp.float32)
    return parts


def dot(left, right):
    return jnp.dot(left, right, preferred_element_type=jnp.float32)


def stack(array, count=3):
    return jnp.concatenate(split(array, count), axis=0)


def multiply(left, right):
    count = len(right)
    rows = left.shape[0] // count
    by_order = [None] * count
    for at in range(count):
        product = dot(left[: (count - at) * rows], right[at])
        for order in range(count - at):
            term = product[order * rows : (order + 1) * rows]
            by_order[at + order] = term if by_order[at + order] is None else by_order[at + order] + term
    total = by_order[-1]
    for term in reversed(by_order[:-1]):
        total = total + term
    return total


def multiply_window(left, right):
    first, second, third = split(right, 3)
    return dot(left, jnp.concatenate([first, second, first, third, second, first], axis=0))


def forward(lines, first_stage, sides_ref, twist_ref, count=3):
    cosine, sine = twist_ref[0], twist_ref[1]
    first = first_stage(jnp.concatenate([jnp.concatenate(line, axis=0) for line in lines], axis=1))
    turned = []
    for at in range(len(lines)):
        real = first[:SIDE, at * SIDE : (at + 1) * SIDE]
        imag = first[SIDE:, at * SIDE : (at + 1) * SIDE]
        turned.append(jnp.concatenate([real * cosine + imag * sine, imag * cosine - real * sine], axis=1))
    second = multiply(stack(jnp.concatenate(turned, axis=0), count), parts_of(sides_ref, RIGHT, count))
    return [
        (second[at * SIDE : (at + 1) * SIDE, :SIDE], second[at * SIDE : (at + 1) * SIDE, SIDE:])
        for at in range(len(lines))
    ]


def inverse_start(lines, sides_ref, twist_ref, count=3):
    cosine, sine = twist_ref[0], twist_ref[1]
    stacked = jnp.concatenate([jnp.concatenate(line, axis=1) for line in lines], axis=0)
    first = multiply(stack(stacked, count), parts_of(sides_ref, RIGHT_T, count))
    turned = []
    for at in range(len(lines)):
        real = first[at * SIDE : (at + 1) * SIDE, :SIDE]
        imag = first[at * SIDE : (at + 1) * SIDE, SIDE:]
        turned.append(jnp.concatenate([real * cosine - imag * sine, imag * cosine + real * sine], axis=0))
    return turned


def stacked_of(sides_ref, which, count=3):
    return sides_ref[which * 6 * SIDE : (which * 6 + 2 * count) * SIDE, :]


def parts_of(sides_ref, which, count=3):
    return [sides_ref[(which * 3 + at) * 2 * SIDE : (which * 3 + at + 1) * 2 * SIDE, :] for at in range(count)]


def grid_of(rows):
    return (
        lax.broadcasted_iota(jnp.int32, (rows, SIDE), 0),
        lax.broadcasted_iota(jnp.int32, (rows, SIDE), 1),
    )


def running_sum(gradient):
    rows, cols = grid_of(SIDE)
    within = dot(
        (cols <= rows).astype(jnp.float32).astype(jnp.bfloat16), jnp.concatenate(split(gradient, 3), axis=1)
    )
    sums = jnp.broadcast_to(jnp.sum(gradient, axis=0, keepdims=True), (16, SIDE))
    before = dot(
        jnp.concatenate(split(sums, 3), axis=0), (rows < cols).astype(jnp.float32).astype(jnp.bfloat16)
    )
    within = within[:, :SIDE] + (within[:, SIDE : 2 * SIDE] + within[:, 2 * SIDE :])
    return within + (before[:1, :] + (before[16:17, :] + before[32:33, :]))


def phase_of(sums_ref):
    gradient = sums_ref[:TILES] / (sums_ref[TILES:] + EPSILON)
    return running_sum(gradient.reshape(SIDE, SIDE))


def cosine_sine(angle):
    quarters = jnp.floor(angle * (2.0 / np.pi) + 0.5)
    rest = angle - quarters * 1.5703125
    rest = rest - quarters * 4.837512969970703125e-4
    rest = rest - quarters * 7.54978995489188216e-8
    square = rest * rest
    sine = ((-1.9515295891e-4 * square + 8.3321608736e-3) * square - 1.6666654611e-1) * square * rest + rest
    cosine = (2.443315711809948e-5 * square - 1.388731625493765e-3) * square + 4.166664568298827e-2
    cosine = cosine * square * square - 0.5 * square + 1.0
    turn = quarters.astype(jnp.int32)
    odd = (turn & 1) == 1
    sine, cosine = jnp.where(odd, cosine, sine), jnp.where(odd, sine, cosine)
    return jnp.where(((turn + 1) & 2) == 2, -cosine, cosine), jnp.where((turn & 2) == 2, -sine, sine)


def turn_back(lines, total):
    cosine, sine = cosine_sine(total)
    return [(real * cosine + imag * sine, imag * cosine - real * sine) for real, imag in lines]


def row_offset(shift):
    begin = (shift + SIDE * SIDE // 2) & (SIDE * SIDE - 1)
    return ((begin >> 7) + FIRST) & (SIDE - 1), begin & (SIDE - 1)


def center(upper, lower, lane, width):
    rows, cols = grid_of(WINDOW)
    turn = (SIDE - lane) & (SIDE - 1)
    moved = jnp.where(cols >= SIDE - lane, pltpu.roll(lower, turn, 1), pltpu.roll(upper, turn, 1))
    cells = (rows + FIRST) * SIDE + cols
    least = SIDE * SIDE // 2 - width // 2
    return jnp.where((cells >= least) & (cells < least + width), moved, 0.0)


def gradient_sums(lines, out_ref):
    rows, cols = grid_of(SIDE)
    numerator = jnp.zeros((SIDE, SIDE), jnp.float32)
    denominator = jnp.zeros((SIDE, SIDE), jnp.float32)

    def before(part):
        down = pltpu.roll(part, 1, 0)
        return jnp.where(rows == 0, pltpu.roll(down, 1, 1), down)

    for real, imag in lines:
        numerator = numerator + (before(real) * imag - before(imag) * real)
        denominator = denominator + (real * real + imag * imag)
    numerator = jnp.where((rows == 0) & (cols == 0), 0.0, numerator)
    out_ref[:TILES] = numerator.reshape(TILES, SUB, SIDE)
    out_ref[TILES:] = denominator.reshape(TILES, SUB, SIDE)


def tile_at(bins, part, row):
    return (part * (bins // SUB) + row // SUB) * SUB * SUB + row % SUB


def pack_kernel(
    strong_hbm, shifts_hbm, widths_hbm, image_hbm, out_hbm, at_hbm,
    place_ref, strong_ref, shifts_ref, widths_ref, image_ref, tiles_ref, out_ref, at_ref, small_sems, sems, out_sems,
):
    bins = image_ref.shape[1]
    strong = strong_ref.shape[0]
    half = bins // 2
    indices = pltpu.make_async_copy(strong_hbm, strong_ref, small_sems.at[0])
    indices.start()
    chunks = []
    for part in range(2):
        for at in range(2):
            span = slice(at * half, (at + 1) * half)
            chunks.append(
                pltpu.make_async_copy(image_hbm.at[part, span], image_ref.at[part, span], sems.at[part * 2 + at])
            )
            chunks[-1].start()
    others_in = [
        pltpu.make_async_copy(shifts_hbm, shifts_ref, small_sems.at[1]),
        pltpu.make_async_copy(widths_hbm, widths_ref, small_sems.at[2]),
    ]
    for copy in others_in:
        copy.start()
    for row in range(bins):
        place_ref[row] = -1
    indices.wait()
    for at in range(strong):
        place_ref[strong_ref[at] & (bins - 1)] = at // 2 * 8 + at % 2
    others = jnp.int32(0)
    places = []
    for row in range(bins):
        held = place_ref[row]
        place = jnp.where(held < 0, ((others >> 1) << 3) + (others & 1) + 2, held)
        others = others + jnp.where(held < 0, 1, 0)
        places.append(place)
        at_ref[SUB + row : SUB + row + 1, :] = jnp.full((1, SIDE), place, jnp.int32)
    for copy in others_in:
        copy.wait()
    for at in range(2):
        line = lax.axis_index(AZ) * 2 + at
        for where, value in enumerate(row_offset(shifts_ref[line]) + (widths_ref[line],)):
            at_ref[4 * at + where : 4 * at + where + 1, :] = jnp.full((1, SIDE), value, jnp.int32)
    copies = [pltpu.make_async_copy(at_ref, at_hbm, out_sems.at[2])]
    copies[0].start()
    for part in range(2):
        for at in range(2):
            chunks[part * 2 + at].wait()
            for group in range(at * half // SUB, (at + 1) * half // SUB):
                for block in range(SUB):
                    tile = ((part * (bins // SUB) + group) * SUB + block) * SUB
                    tiles_ref[tile : tile + SUB, :] = image_ref[
                        part, group * SUB : (group + 1) * SUB, block * SIDE : (block + 1) * SIDE
                    ]
            for row in range(at * half, (at + 1) * half):
                out_ref[part, places[row] >> 3, places[row] & 3] = tiles_ref[
                    pl.ds(tile_at(bins, part, row), SUB, stride=SUB), :
                ]
        copies.append(
            pltpu.make_async_copy(out_ref.at[part], out_hbm.at[:, pl.ds(part * 4, 4)], out_sems.at[part])
        )
        copies[-1].start()
    for copy in copies:
        copy.wait()


def unpack_kernel(at_ref, rows_ref, phase_ref, image_hbm, phase_hbm, image_ref, tiles_ref, sems):
    bins = image_ref.shape[1]
    copies = [pltpu.make_async_copy(phase_ref, phase_hbm, sems.at[4])]
    copies[0].start()
    places = [at_ref[SUB + row, 0] for row in range(bins)]
    for part in range(2):
        for row in range(bins):
            tiles_ref[pl.ds(tile_at(bins, part, row), SUB, stride=SUB), :] = rows_ref[places[row] + part * 4]
        for half in range(2):
            span = slice(half * bins // 2, (half + 1) * bins // 2)
            for group in range(half * bins // 2 // SUB, (half + 1) * bins // 2 // SUB):
                for block in range(SUB):
                    at = ((part * (bins // SUB) + group) * SUB + block) * SUB
                    image_ref[part, group * SUB : (group + 1) * SUB, block * SIDE : (block + 1) * SIDE] = tiles_ref[
                        at : at + SUB, :
                    ]
            copies.append(
                pltpu.make_async_copy(
                    image_ref.at[part, span], image_hbm.at[part, span], sems.at[part * 2 + half]
                )
            )
            copies[-1].start()
    for copy in copies:
        copy.wait()


def offsets(at_ref, line):
    return [at_ref[4 * line + where, 0] for where in range(3)]


def first_kernel(
    at_ref, rows_ref, window_ref, sides_ref, twist_ref, out_ref, history_ref, ring_ref
):
    lines = []
    for at in range(2):
        row, lane, width = offsets(at_ref, at)
        parts = []
        for part in range(2):
            ring = ring_ref.at[at * 2 + part]
            ring[:SIDE, :] = square(rows_ref, part * 4 + at)
            ring[SIDE:, :] = rows_ref[: LOAD // SUB, part * 4 + at].reshape(LOAD, SIDE)
            parts.append(center(ring[pl.ds(row, WINDOW), :], ring[pl.ds(row + 1, WINDOW), :], lane, width))
        lines.append(parts)
    gradient_sums(forward(lines, lambda lines: multiply_window(window_ref[...], lines), sides_ref, twist_ref), out_ref)
    for begin, count in ((0, 3), (2, 2)):
        lines = [[square(rows_ref, part * 4 + begin + at) for part in range(2)] for at in range(2)]
        whole = stacked_of(sides_ref, RIGHT_T, count)
        spectra = forward(lines, lambda lines: multiply(whole, split(lines, count)), sides_ref, twist_ref, count)
        for at in range(2):
            for part in range(2):
                history_ref[begin + at, part] = spectra[at][part]


def square(rows_ref, slot):
    return rows_ref[:, slot].reshape(SIDE, SIDE)


def share_kernel(in_ref, out_ref):
    out_ref[...] = jnp.broadcast_to(jnp.sum(in_ref[...], axis=0)[None], out_ref.shape)


def second_kernel(
    at_ref, sums_ref, history_ref, window_ref, ring_ref, sides_ref, twist_ref,
    out_ref, total_ref,
):
    total = phase_of(sums_ref)
    total_ref[...] = total
    lines = turn_back([(history_ref[at, 0], history_ref[at, 1]) for at in range(2)], total)
    centered = []
    for at, started in enumerate(inverse_start(lines, sides_ref, twist_ref)):
        row, lane, width = offsets(at_ref, at)
        cosine, sine = ring_ref[0, pl.ds(row, LOAD), :], ring_ref[1, pl.ds(row, LOAD), :]
        left = [jnp.concatenate([cosine, -sine], axis=1), jnp.concatenate([sine, cosine], axis=1)]
        found = multiply(stack(jnp.concatenate(left, axis=0)), split(started, 3))
        centered.append(
            [
                center(found[from_row : from_row + WINDOW], found[from_row + 1 : from_row + 1 + WINDOW], lane, width)
                for from_row in (0, LOAD)
            ]
        )
    gradient_sums(forward(centered, lambda lines: multiply_window(window_ref[...], lines), sides_ref, twist_ref), out_ref)


def final_kernel(
    sums_ref, total_ref, history_ref, sides_ref, twist_ref, out_ref, phase_ref, turned_ref
):
    total = total_ref[...] + phase_of(sums_ref)
    lines = turn_back([(history_ref[at, 0], history_ref[at, 1]) for at in range(4)], total)
    started = inverse_start(lines, sides_ref, twist_ref, 2)
    found = multiply(stacked_of(sides_ref, RIGHT, 2), split(jnp.concatenate(started, axis=1), 2))
    for at in range(4):
        for part in range(2):
            line = found[part * SIDE : (part + 1) * SIDE, at * SIDE : (at + 1) * SIDE]
            out_ref[:, part * 4 + at] = line.reshape(TILES, SUB, SIDE)
    turned_ref[...] = total.T
    phase_ref[...] = turned_ref[pl.ds(pl.multiple_of(lax.axis_index(AZ) * SUB, SUB), SUB), :]


SMEM = pl.BlockSpec(memory_space=pltpu.SMEM)
VMEM = pl.BlockSpec(memory_space=pltpu.VMEM)
HBM = pl.BlockSpec(memory_space=pltpu.HBM)
PACK_VMEM = 60 * 1024 * 1024


def call(kernel, shapes, specs, *operands, scratch=(), out_specs=None, vmem=32 * 1024 * 1024):
    out = pl.pallas_call(
        kernel,
        out_shape=[jax.ShapeDtypeStruct(*shape) for shape in shapes],
        in_specs=list(specs),
        out_specs=out_specs or [VMEM] * len(shapes),
        scratch_shapes=list(scratch),
        compiler_params=pltpu.CompilerParams(vmem_limit_bytes=vmem),
    )(*operands)
    return out if len(out) > 1 else out[0]


def exchange(array, axes):
    return lax.all_to_all(array, axes, split_axis=0, concat_axis=0, tiled=True)


RNG = ("zh", "zl", "x")
AZ = ("yh", "yl", "core")
NEAR = ("zl", "x", "yl", "core")
FAR = ("zh", "yh")


def local(sar_image, strong_index, shifts, widths):
    f32, i32 = jnp.float32, jnp.int32
    az, near, far = lax.axis_size(AZ), lax.axis_size(NEAR), lax.axis_size(FAR)
    bins, pulses_local = sar_image.shape[1:]
    table = tables()
    tile = (SUB, SIDE)
    moved_tiles = pltpu.VMEM((2 * bins * SUB, SIDE), f32)

    packed, places = call(
        pack_kernel,
        [((az, 8) + tile, f32), ((SUB + bins, SIDE), i32)],
        [HBM] * 4,
        strong_index,
        shifts,
        widths,
        sar_image,
        scratch=[pltpu.SMEM((bins,), i32)]
        + [pltpu.SMEM(strong_index.shape, i32) for _ in range(3)]
        + [
            pltpu.VMEM(sar_image.shape, f32),
            moved_tiles,
            pltpu.VMEM((2, az, 4) + tile, f32),
            pltpu.VMEM((SUB + bins, SIDE), i32),
            pltpu.SemaphoreType.DMA((3,)),
            pltpu.SemaphoreType.DMA((4,)),
            pltpu.SemaphoreType.DMA((3,)),
        ],
        out_specs=[HBM, HBM],
        vmem=PACK_VMEM,
    )
    rows = exchange(packed, AZ)
    sums, history = call(
        first_kernel,
        [((2 * TILES,) + tile, f32), ((4, 2, SIDE, SIDE), f32)],
        [VMEM] * 5,
        places,
        rows,
        table["window"],
        table["sides"],
        table["twist"],
        scratch=[pltpu.VMEM((4, SIDE + LOAD, SIDE), f32)],
    )

    def all_sums(sums):
        each = 2 * TILES // near
        scattered = exchange(sums.reshape((near, each) + tile), NEAR)
        partial = call(share_kernel, [((far, each) + tile, f32)], [VMEM], scattered)
        everyone = exchange(partial, FAR)
        whole = call(share_kernel, [((near, each) + tile, f32)], [VMEM], everyone)
        return exchange(whole, NEAR).reshape((2 * TILES,) + tile)

    summed = all_sums(sums)
    sums, total = call(
        second_kernel,
        [((2 * TILES,) + tile, f32), ((SIDE, SIDE), f32)],
        [VMEM] * 7,
        places,
        summed,
        history,
        table["window"],
        table["ring"],
        table["sides"],
        table["twist"],
    )
    summed = all_sums(sums)
    corrected, phase = call(
        final_kernel,
        [((az, 8) + tile, f32), (tile, f32)],
        [VMEM] * 5,
        summed,
        total,
        history,
        table["sides"],
        table["twist"],
        scratch=[pltpu.VMEM((SIDE, SIDE), f32)],
    )
    returned = exchange(corrected, AZ)
    focused, phase = call(
        unpack_kernel,
        [(sar_image.shape, f32), (tile, f32)],
        [VMEM, VMEM, VMEM],
        places,
        returned.reshape((az * 8,) + tile),
        phase,
        scratch=[pltpu.VMEM(sar_image.shape, f32), moved_tiles, pltpu.SemaphoreType.DMA((5,))],
        out_specs=[HBM, HBM],
    )
    return focused, phase.reshape(pulses_local)


def solution(mesh):
    rng, az = mesh.devices.shape
    along_x = max(1, min(4, rng // 2))
    split = Mesh(
        mesh.devices.reshape(rng // (2 * along_x), 2, along_x, az // 4, 2, 2), RNG + AZ
    )
    placed = (P(None, RNG, AZ), P(RNG), P(RNG), P(RNG))
    return jax.shard_map(
        local,
        mesh=split,
        in_specs=placed,
        out_specs=(P(None, RNG, AZ), P(AZ)),
        check_vma=False,
    )
```

```python
import jax
import jax.numpy as jnp
import numpy as np
from jax import lax
from jax.experimental import pallas as pl
from jax.experimental.pallas import tpu as pltpu
from jax.sharding import Mesh, PartitionSpec as P

EPSILON = 1e-06
SIDE = 128
SUB = 8
TILES = SIDE // SUB
WINDOW = 16
FIRST = SIDE // 2 - WINDOW // 2
RIGHT, RIGHT_T = 0, 1
LOAD = 24


def tables():
    grid = np.arange(SIDE)
    product = grid[:, None] * grid[None, :]
    angle = 2.0 * np.pi * (product % SIDE) / SIDE
    cosine, sine = np.cos(angle), np.sin(angle)
    right = np.block([[cosine, -sine], [sine, cosine]])
    rows = slice(FIRST, FIRST + WINDOW)
    window = np.block([[cosine[:, rows], sine[:, rows]], [-sine[:, rows], cosine[:, rows]]])
    around = np.arange(SIDE + LOAD) % SIDE
    ring = np.stack([cosine[around], sine[around]])
    twist = 2.0 * np.pi * product / (SIDE * SIDE)
    twist = np.stack([np.cos(twist), np.sin(twist)]) / SIDE
    made = dict(ring=ring, twist=twist)
    made = {name: jnp.asarray(table.astype(np.float32)) for name, table in made.items()}

    def parts(table):
        found, rest = [], table.astype(np.float32)
        for _ in range(3):
            found.append(rest.astype(jnp.bfloat16))
            rest = rest - found[-1].astype(np.float32)
        return found

    window = parts(window)
    made["window"] = jnp.asarray(np.concatenate([window[at] for at in (0, 0, 1, 0, 1, 2)], axis=1))
    made["sides"] = jnp.asarray(np.concatenate(parts(right) + parts(right.T), axis=0))
    return made


def split(array, count):
    parts = []
    for _ in range(count):
        parts.append(array.astype(jnp.bfloat16))
        array = array - parts[-1].astype(jnp.float32)
    return parts


def dot(left, right):
    return jnp.dot(left, right, preferred_element_type=jnp.float32)


def stack(array, count=3):
    return jnp.concatenate(split(array, count), axis=0)


def multiply(left, right):
    count = len(right)
    rows = left.shape[0] // count
    by_order = [None] * count
    for at in range(count):
        product = dot(left[: (count - at) * rows], right[at])
        for order in range(count - at):
            term = product[order * rows : (order + 1) * rows]
            by_order[at + order] = term if by_order[at + order] is None else by_order[at + order] + term
    total = by_order[-1]
    for term in reversed(by_order[:-1]):
        total = total + term
    return total


def multiply_window(left, right):
    first, second, third = split(right, 3)
    return dot(left, jnp.concatenate([first, second, first, third, second, first], axis=0))


def forward(lines, first_stage, sides_ref, twist_ref, count=3):
    cosine, sine = twist_ref[0], twist_ref[1]
    first = first_stage(jnp.concatenate([jnp.concatenate(line, axis=0) for line in lines], axis=1))
    turned = []
    for at in range(len(lines)):
        real = first[:SIDE, at * SIDE : (at + 1) * SIDE]
        imag = first[SIDE:, at * SIDE : (at + 1) * SIDE]
        turned.append(jnp.concatenate([real * cosine + imag * sine, imag * cosine - real * sine], axis=1))
    second = multiply(stack(jnp.concatenate(turned, axis=0), count), parts_of(sides_ref, RIGHT, count))
    return [
        (second[at * SIDE : (at + 1) * SIDE, :SIDE], second[at * SIDE : (at + 1) * SIDE, SIDE:])
        for at in range(len(lines))
    ]


def inverse_start(lines, sides_ref, twist_ref, count=3):
    cosine, sine = twist_ref[0], twist_ref[1]
    stacked = jnp.concatenate([jnp.concatenate(line, axis=1) for line in lines], axis=0)
    first = multiply(stack(stacked, count), parts_of(sides_ref, RIGHT_T, count))
    turned = []
    for at in range(len(lines)):
        real = first[at * SIDE : (at + 1) * SIDE, :SIDE]
        imag = first[at * SIDE : (at + 1) * SIDE, SIDE:]
        turned.append(jnp.concatenate([real * cosine - imag * sine, imag * cosine + real * sine], axis=0))
    return turned


def stacked_of(sides_ref, which, count=3):
    return sides_ref[which * 6 * SIDE : (which * 6 + 2 * count) * SIDE, :]


def parts_of(sides_ref, which, count=3):
    return [sides_ref[(which * 3 + at) * 2 * SIDE : (which * 3 + at + 1) * 2 * SIDE, :] for at in range(count)]


def grid_of(rows):
    return (
        lax.broadcasted_iota(jnp.int32, (rows, SIDE), 0),
        lax.broadcasted_iota(jnp.int32, (rows, SIDE), 1),
    )


def running_sum(gradient):
    rows, cols = grid_of(SIDE)
    within = dot(
        (cols <= rows).astype(jnp.float32).astype(jnp.bfloat16), jnp.concatenate(split(gradient, 3), axis=1)
    )
    sums = jnp.broadcast_to(jnp.sum(gradient, axis=0, keepdims=True), (16, SIDE))
    before = dot(
        jnp.concatenate(split(sums, 3), axis=0), (rows < cols).astype(jnp.float32).astype(jnp.bfloat16)
    )
    within = within[:, :SIDE] + (within[:, SIDE : 2 * SIDE] + within[:, 2 * SIDE :])
    return within + (before[:1, :] + (before[16:17, :] + before[32:33, :]))


def phase_of(gradient_ref, whole_ref):
    near, rows = gradient_ref.shape[:2]
    for at in range(near):
        whole_ref[at * rows : (at + 1) * rows, :] = gradient_ref[at]
    return running_sum(whole_ref[...])


def cosine_sine(angle):
    quarters = jnp.floor(angle * (2.0 / np.pi) + 0.5)
    rest = angle - quarters * 1.5703125
    rest = rest - quarters * 4.837512969970703125e-4
    rest = rest - quarters * 7.54978995489188216e-8
    square = rest * rest
    sine = ((-1.9515295891e-4 * square + 8.3321608736e-3) * square - 1.6666654611e-1) * square * rest + rest
    cosine = (2.443315711809948e-5 * square - 1.388731625493765e-3) * square + 4.166664568298827e-2
    cosine = cosine * square * square - 0.5 * square + 1.0
    turn = quarters.astype(jnp.int32)
    odd = (turn & 1) == 1
    sine, cosine = jnp.where(odd, cosine, sine), jnp.where(odd, sine, cosine)
    return jnp.where(((turn + 1) & 2) == 2, -cosine, cosine), jnp.where((turn & 2) == 2, -sine, sine)


def turn_back(lines, total):
    cosine, sine = cosine_sine(total)
    return [(real * cosine + imag * sine, imag * cosine - real * sine) for real, imag in lines]


def row_offset(shift):
    begin = (shift + SIDE * SIDE // 2) & (SIDE * SIDE - 1)
    return ((begin >> 7) + FIRST) & (SIDE - 1), begin & (SIDE - 1)


def center(upper, lower, lane, width):
    rows, cols = grid_of(WINDOW)
    turn = (SIDE - lane) & (SIDE - 1)
    moved = jnp.where(cols >= SIDE - lane, pltpu.roll(lower, turn, 1), pltpu.roll(upper, turn, 1))
    cells = (rows + FIRST) * SIDE + cols
    least = SIDE * SIDE // 2 - width // 2
    return jnp.where((cells >= least) & (cells < least + width), moved, 0.0)


def gradient_sums(lines, out_ref):
    rows, cols = grid_of(SIDE)
    numerator = jnp.zeros((SIDE, SIDE), jnp.float32)
    denominator = jnp.zeros((SIDE, SIDE), jnp.float32)

    def before(part):
        down = pltpu.roll(part, 1, 0)
        return jnp.where(rows == 0, pltpu.roll(down, 1, 1), down)

    for real, imag in lines:
        numerator = numerator + (before(real) * imag - before(imag) * real)
        denominator = denominator + (real * real + imag * imag)
    numerator = jnp.where((rows == 0) & (cols == 0), 0.0, numerator)
    near, _, part = out_ref.shape[:3]
    for at in range(near):
        out_ref[at, 0] = numerator[at * part : (at + 1) * part, :]
        out_ref[at, 1] = denominator[at * part : (at + 1) * part, :]


def tile_at(bins, part, row):
    return (part * (bins // SUB) + row // SUB) * SUB * SUB + row % SUB


def pack_kernel(
    strong_hbm, shifts_hbm, widths_hbm, image_hbm, out_hbm, at_hbm,
    place_ref, strong_ref, shifts_ref, widths_ref, image_ref, tiles_ref, out_ref, at_ref, small_sems, sems, out_sems,
):
    bins = image_ref.shape[1]
    strong = strong_ref.shape[0]
    half = bins // 2
    indices = pltpu.make_async_copy(strong_hbm, strong_ref, small_sems.at[0])
    indices.start()
    chunks = []
    for part in range(2):
        for at in range(2):
            span = slice(at * half, (at + 1) * half)
            chunks.append(
                pltpu.make_async_copy(image_hbm.at[part, span], image_ref.at[part, span], sems.at[part * 2 + at])
            )
            chunks[-1].start()
    others_in = [
        pltpu.make_async_copy(shifts_hbm, shifts_ref, small_sems.at[1]),
        pltpu.make_async_copy(widths_hbm, widths_ref, small_sems.at[2]),
    ]
    for copy in others_in:
        copy.start()
    for row in range(bins):
        place_ref[row] = -1
    indices.wait()
    for at in range(strong):
        place_ref[strong_ref[at] & (bins - 1)] = at // 2 * 8 + at % 2
    others = jnp.int32(0)
    places = []
    for row in range(bins):
        held = place_ref[row]
        place = jnp.where(held < 0, ((others >> 1) << 3) + (others & 1) + 2, held)
        others = others + jnp.where(held < 0, 1, 0)
        places.append(place)
        at_ref[SUB + row : SUB + row + 1, :] = jnp.full((1, SIDE), place, jnp.int32)
    for copy in others_in:
        copy.wait()
    for at in range(2):
        line = lax.axis_index(AZ) * 2 + at
        for where, value in enumerate(row_offset(shifts_ref[line]) + (widths_ref[line],)):
            at_ref[4 * at + where : 4 * at + where + 1, :] = jnp.full((1, SIDE), value, jnp.int32)
    copies = [pltpu.make_async_copy(at_ref, at_hbm, out_sems.at[2])]
    copies[0].start()
    for part in range(2):
        for at in range(2):
            chunks[part * 2 + at].wait()
            for group in range(at * half // SUB, (at + 1) * half // SUB):
                for block in range(SUB):
                    tile = ((part * (bins // SUB) + group) * SUB + block) * SUB
                    tiles_ref[tile : tile + SUB, :] = image_ref[
                        part, group * SUB : (group + 1) * SUB, block * SIDE : (block + 1) * SIDE
                    ]
            for row in range(at * half, (at + 1) * half):
                out_ref[part, places[row] >> 3, places[row] & 3] = tiles_ref[
                    pl.ds(tile_at(bins, part, row), SUB, stride=SUB), :
                ]
        copies.append(
            pltpu.make_async_copy(out_ref.at[part], out_hbm.at[:, pl.ds(part * 4, 4)], out_sems.at[part])
        )
        copies[-1].start()
    for copy in copies:
        copy.wait()


def unpack_kernel(at_ref, rows_ref, phase_ref, image_hbm, phase_hbm, image_ref, tiles_ref, sems):
    bins = image_ref.shape[1]
    copies = [pltpu.make_async_copy(phase_ref, phase_hbm, sems.at[4])]
    copies[0].start()
    places = [at_ref[SUB + row, 0] for row in range(bins)]
    for part in range(2):
        for row in range(bins):
            tiles_ref[pl.ds(tile_at(bins, part, row), SUB, stride=SUB), :] = rows_ref[places[row] + part * 4]
        for half in range(2):
            span = slice(half * bins // 2, (half + 1) * bins // 2)
            for group in range(half * bins // 2 // SUB, (half + 1) * bins // 2 // SUB):
                for block in range(SUB):
                    at = ((part * (bins // SUB) + group) * SUB + block) * SUB
                    image_ref[part, group * SUB : (group + 1) * SUB, block * SIDE : (block + 1) * SIDE] = tiles_ref[
                        at : at + SUB, :
                    ]
            copies.append(
                pltpu.make_async_copy(
                    image_ref.at[part, span], image_hbm.at[part, span], sems.at[part * 2 + half]
                )
            )
            copies[-1].start()
    for copy in copies:
        copy.wait()


def offsets(at_ref, line):
    return [at_ref[4 * line + where, 0] for where in range(3)]


def first_kernel(
    at_ref, rows_ref, window_ref, sides_ref, twist_ref, out_ref, history_ref, ring_ref
):
    lines = []
    for at in range(2):
        row, lane, width = offsets(at_ref, at)
        parts = []
        for part in range(2):
            ring = ring_ref.at[at * 2 + part]
            ring[:SIDE, :] = square(rows_ref, part * 4 + at)
            ring[SIDE:, :] = rows_ref[: LOAD // SUB, part * 4 + at].reshape(LOAD, SIDE)
            parts.append(center(ring[pl.ds(row, WINDOW), :], ring[pl.ds(row + 1, WINDOW), :], lane, width))
        lines.append(parts)
    gradient_sums(forward(lines, lambda lines: multiply_window(window_ref[...], lines), sides_ref, twist_ref), out_ref)
    for begin, count in ((0, 3), (2, 2)):
        lines = [[square(rows_ref, part * 4 + begin + at) for part in range(2)] for at in range(2)]
        whole = stacked_of(sides_ref, RIGHT_T, count)
        spectra = forward(lines, lambda lines: multiply(whole, split(lines, count)), sides_ref, twist_ref, count)
        for at in range(2):
            for part in range(2):
                history_ref[begin + at, part] = spectra[at][part]


def square(rows_ref, slot):
    return rows_ref[:, slot].reshape(SIDE, SIDE)


def share_kernel(in_ref, out_ref):
    out_ref[...] = jnp.broadcast_to(jnp.sum(in_ref[...], axis=0)[None], out_ref.shape)


def gradient_kernel(in_ref, out_ref):
    sums = jnp.sum(in_ref[...], axis=0)
    out_ref[...] = jnp.broadcast_to((sums[0] / (sums[1] + EPSILON))[None], out_ref.shape)


def second_kernel(
    at_ref, gradient_ref, history_ref, window_ref, ring_ref, sides_ref, twist_ref,
    out_ref, total_ref, whole_ref,
):
    total = phase_of(gradient_ref, whole_ref)
    total_ref[...] = total
    lines = turn_back([(history_ref[at, 0], history_ref[at, 1]) for at in range(2)], total)
    centered = []
    for at, started in enumerate(inverse_start(lines, sides_ref, twist_ref)):
        row, lane, width = offsets(at_ref, at)
        cosine, sine = ring_ref[0, pl.ds(row, LOAD), :], ring_ref[1, pl.ds(row, LOAD), :]
        left = [jnp.concatenate([cosine, -sine], axis=1), jnp.concatenate([sine, cosine], axis=1)]
        found = multiply(stack(jnp.concatenate(left, axis=0)), split(started, 3))
        centered.append(
            [
                center(found[from_row : from_row + WINDOW], found[from_row + 1 : from_row + 1 + WINDOW], lane, width)
                for from_row in (0, LOAD)
            ]
        )
    gradient_sums(forward(centered, lambda lines: multiply_window(window_ref[...], lines), sides_ref, twist_ref), out_ref)


def final_kernel(
    gradient_ref, total_ref, history_ref, sides_ref, twist_ref, out_ref, phase_ref, turned_ref
):
    total = total_ref[...] + phase_of(gradient_ref, turned_ref)
    lines = turn_back([(history_ref[at, 0], history_ref[at, 1]) for at in range(4)], total)
    started = inverse_start(lines, sides_ref, twist_ref, 2)
    found = multiply(stacked_of(sides_ref, RIGHT, 2), split(jnp.concatenate(started, axis=1), 2))
    for at in range(4):
        for part in range(2):
            line = found[part * SIDE : (part + 1) * SIDE, at * SIDE : (at + 1) * SIDE]
            out_ref[:, part * 4 + at] = line.reshape(TILES, SUB, SIDE)
    turned_ref[...] = total.T
    phase_ref[...] = turned_ref[pl.ds(pl.multiple_of(lax.axis_index(AZ) * SUB, SUB), SUB), :]


SMEM = pl.BlockSpec(memory_space=pltpu.SMEM)
VMEM = pl.BlockSpec(memory_space=pltpu.VMEM)
HBM = pl.BlockSpec(memory_space=pltpu.HBM)
PACK_VMEM = 60 * 1024 * 1024


def call(kernel, shapes, specs, *operands, scratch=(), out_specs=None, vmem=32 * 1024 * 1024):
    out = pl.pallas_call(
        kernel,
        out_shape=[jax.ShapeDtypeStruct(*shape) for shape in shapes],
        in_specs=list(specs),
        out_specs=out_specs or [VMEM] * len(shapes),
        scratch_shapes=list(scratch),
        compiler_params=pltpu.CompilerParams(vmem_limit_bytes=vmem),
    )(*operands)
    return out if len(out) > 1 else out[0]


def exchange(array, axes):
    return lax.all_to_all(array, axes, split_axis=0, concat_axis=0, tiled=True)


RNG = ("zh", "zl", "x")
AZ = ("yh", "yl", "core")
NEAR = ("zl", "x", "yl", "core")
FAR = ("zh", "yh")


def local(sar_image, strong_index, shifts, widths):
    f32, i32 = jnp.float32, jnp.int32
    az, near, far = lax.axis_size(AZ), lax.axis_size(NEAR), lax.axis_size(FAR)
    bins, pulses_local = sar_image.shape[1:]
    table = tables()
    tile = (SUB, SIDE)
    part = SIDE // near
    sums_shape = (near, 2, part, SIDE)
    moved_tiles = pltpu.VMEM((2 * bins * SUB, SIDE), f32)

    packed, places = call(
        pack_kernel,
        [((az, 8) + tile, f32), ((SUB + bins, SIDE), i32)],
        [HBM] * 4,
        strong_index,
        shifts,
        widths,
        sar_image,
        scratch=[pltpu.SMEM((bins,), i32)]
        + [pltpu.SMEM(strong_index.shape, i32) for _ in range(3)]
        + [
            pltpu.VMEM(sar_image.shape, f32),
            moved_tiles,
            pltpu.VMEM((2, az, 4) + tile, f32),
            pltpu.VMEM((SUB + bins, SIDE), i32),
            pltpu.SemaphoreType.DMA((3,)),
            pltpu.SemaphoreType.DMA((4,)),
            pltpu.SemaphoreType.DMA((3,)),
        ],
        out_specs=[HBM, HBM],
        vmem=PACK_VMEM,
    )
    rows = exchange(packed, AZ)
    sums, history = call(
        first_kernel,
        [(sums_shape, f32), ((4, 2, SIDE, SIDE), f32)],
        [VMEM] * 5,
        places,
        rows,
        table["window"],
        table["sides"],
        table["twist"],
        scratch=[pltpu.VMEM((4, SIDE + LOAD, SIDE), f32)],
    )

    def all_gradients(sums):
        scattered = exchange(sums, NEAR)
        partial = call(share_kernel, [((far, 2, part, SIDE), f32)], [VMEM], scattered)
        everyone = exchange(partial, FAR)
        gradient = call(gradient_kernel, [((near, part, SIDE), f32)], [VMEM], everyone)
        return exchange(gradient, NEAR)

    gradient = all_gradients(sums)
    sums, total = call(
        second_kernel,
        [(sums_shape, f32), ((SIDE, SIDE), f32)],
        [VMEM] * 7,
        places,
        gradient,
        history,
        table["window"],
        table["ring"],
        table["sides"],
        table["twist"],
        scratch=[pltpu.VMEM((SIDE, SIDE), f32)],
    )
    gradient = all_gradients(sums)
    corrected, phase = call(
        final_kernel,
        [((az, 8) + tile, f32), (tile, f32)],
        [VMEM] * 5,
        gradient,
        total,
        history,
        table["sides"],
        table["twist"],
        scratch=[pltpu.VMEM((SIDE, SIDE), f32)],
    )
    returned = exchange(corrected, AZ)
    focused, phase = call(
        unpack_kernel,
        [(sar_image.shape, f32), (tile, f32)],
        [VMEM, VMEM, VMEM],
        places,
        returned.reshape((az * 8,) + tile),
        phase,
        scratch=[pltpu.VMEM(sar_image.shape, f32), moved_tiles, pltpu.SemaphoreType.DMA((5,))],
        out_specs=[HBM, HBM],
    )
    return focused, phase.reshape(pulses_local)


def solution(mesh):
    rng, az = mesh.devices.shape
    along_x = max(1, min(4, rng // 2))
    split = Mesh(
        mesh.devices.reshape(rng // (2 * along_x), 2, along_x, az // 4, 2, 2), RNG + AZ
    )
    placed = (P(None, RNG, AZ), P(RNG), P(RNG), P(RNG))
    return jax.shard_map(
        local,
        mesh=split,
        in_specs=placed,
        out_specs=(P(None, RNG, AZ), P(AZ)),
        check_vma=False,
    )
```

```python
import jax
import jax.numpy as jnp
import numpy as np
from jax import lax
from jax.experimental import pallas as pl
from jax.experimental.pallas import tpu as pltpu
from jax.sharding import Mesh, PartitionSpec as P

EPSILON = 1e-06
SIDE = 128
SUB = 8
TILES = SIDE // SUB
WINDOW = 16
FIRST = SIDE // 2 - WINDOW // 2
RIGHT, RIGHT_T = 0, 1
LOAD = 24


def tables():
    grid = np.arange(SIDE)
    product = grid[:, None] * grid[None, :]
    angle = 2.0 * np.pi * (product % SIDE) / SIDE
    cosine, sine = np.cos(angle), np.sin(angle)
    right = np.block([[cosine, -sine], [sine, cosine]])
    rows = slice(FIRST, FIRST + WINDOW)
    window = np.block([[cosine[:, rows], sine[:, rows]], [-sine[:, rows], cosine[:, rows]]])
    around = np.arange(SIDE + LOAD) % SIDE
    ring = np.stack([cosine[around], sine[around]])
    twist = 2.0 * np.pi * product / (SIDE * SIDE)
    twist = np.stack([np.cos(twist), np.sin(twist)]) / SIDE
    made = dict(ring=ring, twist=twist)
    made = {name: jnp.asarray(table.astype(np.float32)) for name, table in made.items()}

    def parts(table):
        found, rest = [], table.astype(np.float32)
        for _ in range(3):
            found.append(rest.astype(jnp.bfloat16))
            rest = rest - found[-1].astype(np.float32)
        return found

    window = parts(window)
    made["window"] = jnp.asarray(np.concatenate([window[at] for at in (0, 0, 1, 0, 1, 2)], axis=1))
    made["sides"] = jnp.asarray(np.concatenate(parts(right) + parts(right.T), axis=0))
    return made


def split(array, count):
    parts = []
    for _ in range(count):
        parts.append(array.astype(jnp.bfloat16))
        array = array - parts[-1].astype(jnp.float32)
    return parts


def dot(left, right):
    return jnp.dot(left, right, preferred_element_type=jnp.float32)


def stack(array, count=3):
    return jnp.concatenate(split(array, count), axis=0)


def multiply(left, right):
    count = len(right)
    rows = left.shape[0] // count
    by_order = [None] * count
    for at in range(count):
        product = dot(left[: (count - at) * rows], right[at])
        for order in range(count - at):
            term = product[order * rows : (order + 1) * rows]
            by_order[at + order] = term if by_order[at + order] is None else by_order[at + order] + term
    total = by_order[-1]
    for term in reversed(by_order[:-1]):
        total = total + term
    return total


def multiply_window(left, right):
    first, second, third = split(right, 3)
    return dot(left, jnp.concatenate([first, second, first, third, second, first], axis=0))


def forward(lines, first_stage, sides_ref, twist_ref, count=3):
    cosine, sine = twist_ref[0], twist_ref[1]
    first = first_stage(jnp.concatenate([jnp.concatenate(line, axis=0) for line in lines], axis=1))
    turned = []
    for at in range(len(lines)):
        real = first[:SIDE, at * SIDE : (at + 1) * SIDE]
        imag = first[SIDE:, at * SIDE : (at + 1) * SIDE]
        turned.append(jnp.concatenate([real * cosine + imag * sine, imag * cosine - real * sine], axis=1))
    second = multiply(stack(jnp.concatenate(turned, axis=0), count), parts_of(sides_ref, RIGHT, count))
    return [
        (second[at * SIDE : (at + 1) * SIDE, :SIDE], second[at * SIDE : (at + 1) * SIDE, SIDE:])
        for at in range(len(lines))
    ]


def inverse_start(lines, sides_ref, twist_ref, count=3):
    cosine, sine = twist_ref[0], twist_ref[1]
    stacked = jnp.concatenate([jnp.concatenate(line, axis=1) for line in lines], axis=0)
    first = multiply(stack(stacked, count), parts_of(sides_ref, RIGHT_T, count))
    turned = []
    for at in range(len(lines)):
        real = first[at * SIDE : (at + 1) * SIDE, :SIDE]
        imag = first[at * SIDE : (at + 1) * SIDE, SIDE:]
        turned.append(jnp.concatenate([real * cosine - imag * sine, imag * cosine + real * sine], axis=0))
    return turned


def stacked_of(sides_ref, which, count=3):
    return sides_ref[which * 6 * SIDE : (which * 6 + 2 * count) * SIDE, :]


def parts_of(sides_ref, which, count=3):
    return [sides_ref[(which * 3 + at) * 2 * SIDE : (which * 3 + at + 1) * 2 * SIDE, :] for at in range(count)]


def grid_of(rows):
    return (
        lax.broadcasted_iota(jnp.int32, (rows, SIDE), 0),
        lax.broadcasted_iota(jnp.int32, (rows, SIDE), 1),
    )


def running_sum(gradient):
    rows, cols = grid_of(SIDE)
    within = dot(
        (cols <= rows).astype(jnp.float32).astype(jnp.bfloat16), jnp.concatenate(split(gradient, 3), axis=1)
    )
    sums = jnp.broadcast_to(jnp.sum(gradient, axis=0, keepdims=True), (16, SIDE))
    before = dot(
        jnp.concatenate(split(sums, 3), axis=0), (rows < cols).astype(jnp.float32).astype(jnp.bfloat16)
    )
    within = within[:, :SIDE] + (within[:, SIDE : 2 * SIDE] + within[:, 2 * SIDE :])
    return within + (before[:1, :] + (before[16:17, :] + before[32:33, :]))


def phase_of(gradient_ref, whole_ref):
    near, rows = gradient_ref.shape[:2]
    for at in range(near):
        whole_ref[at * rows : (at + 1) * rows, :] = gradient_ref[at]
    return running_sum(whole_ref[...])


def cosine_sine(angle):
    quarters = jnp.floor(angle * (2.0 / np.pi) + 0.5)
    rest = angle - quarters * 1.5703125
    rest = rest - quarters * 4.837512969970703125e-4
    rest = rest - quarters * 7.54978995489188216e-8
    square = rest * rest
    sine = ((-1.9515295891e-4 * square + 8.3321608736e-3) * square - 1.6666654611e-1) * square * rest + rest
    cosine = (2.443315711809948e-5 * square - 1.388731625493765e-3) * square + 4.166664568298827e-2
    cosine = cosine * square * square - 0.5 * square + 1.0
    turn = quarters.astype(jnp.int32)
    odd = (turn & 1) == 1
    sine, cosine = jnp.where(odd, cosine, sine), jnp.where(odd, sine, cosine)
    return jnp.where(((turn + 1) & 2) == 2, -cosine, cosine), jnp.where((turn & 2) == 2, -sine, sine)


def turn_back(lines, total):
    cosine, sine = cosine_sine(total)
    return [(real * cosine + imag * sine, imag * cosine - real * sine) for real, imag in lines]


def row_offset(shift):
    begin = (shift + SIDE * SIDE // 2) & (SIDE * SIDE - 1)
    return ((begin >> 7) + FIRST) & (SIDE - 1), begin & (SIDE - 1)


def center(upper, lower, lane, width):
    rows, cols = grid_of(WINDOW)
    turn = (SIDE - lane) & (SIDE - 1)
    moved = jnp.where(cols >= SIDE - lane, pltpu.roll(lower, turn, 1), pltpu.roll(upper, turn, 1))
    cells = (rows + FIRST) * SIDE + cols
    least = SIDE * SIDE // 2 - width // 2
    return jnp.where((cells >= least) & (cells < least + width), moved, 0.0)


def gradient_sums(lines, out_ref):
    rows, cols = grid_of(SIDE)
    numerator = jnp.zeros((SIDE, SIDE), jnp.float32)
    denominator = jnp.zeros((SIDE, SIDE), jnp.float32)

    def before(part):
        down = pltpu.roll(part, 1, 0)
        return jnp.where(rows == 0, pltpu.roll(down, 1, 1), down)

    for real, imag in lines:
        numerator = numerator + (before(real) * imag - before(imag) * real)
        denominator = denominator + (real * real + imag * imag)
    numerator = jnp.where((rows == 0) & (cols == 0), 0.0, numerator)
    near, _, part = out_ref.shape[:3]
    for at in range(near):
        out_ref[at, 0] = numerator[at * part : (at + 1) * part, :]
        out_ref[at, 1] = denominator[at * part : (at + 1) * part, :]


def tile_at(bins, part, row):
    return (part * (bins // SUB) + row // SUB) * SUB * SUB + row % SUB


def pack_kernel(
    strong_hbm, shifts_hbm, widths_hbm, image_hbm, out_ref, at_ref,
    place_ref, strong_ref, shifts_ref, widths_ref, image_ref, tiles_ref, small_sems, sems,
):
    bins = image_ref.shape[1]
    strong = strong_ref.shape[0]
    half = bins // 2
    indices = pltpu.make_async_copy(strong_hbm, strong_ref, small_sems.at[0])
    indices.start()
    chunks = []
    for part in range(2):
        for at in range(2):
            span = slice(at * half, (at + 1) * half)
            chunks.append(
                pltpu.make_async_copy(image_hbm.at[part, span], image_ref.at[part, span], sems.at[part * 2 + at])
            )
            chunks[-1].start()
    others_in = [
        pltpu.make_async_copy(shifts_hbm, shifts_ref, small_sems.at[1]),
        pltpu.make_async_copy(widths_hbm, widths_ref, small_sems.at[2]),
    ]
    for copy in others_in:
        copy.start()
    for row in range(bins):
        place_ref[row] = -1
    indices.wait()
    for at in range(strong):
        place_ref[strong_ref[at] & (bins - 1)] = at // 2 * 8 + at % 2
    others = jnp.int32(0)
    places = []
    for row in range(bins):
        held = place_ref[row]
        place = jnp.where(held < 0, ((others >> 1) << 3) + (others & 1) + 2, held)
        others = others + jnp.where(held < 0, 1, 0)
        places.append(place)
        at_ref[SUB + row : SUB + row + 1, :] = jnp.full((1, SIDE), place, jnp.int32)
    for copy in others_in:
        copy.wait()
    for at in range(2):
        line = lax.axis_index(AZ) * 2 + at
        for where, value in enumerate(row_offset(shifts_ref[line]) + (widths_ref[line],)):
            at_ref[4 * at + where : 4 * at + where + 1, :] = jnp.full((1, SIDE), value, jnp.int32)
    for part in range(2):
        for at in range(2):
            chunks[part * 2 + at].wait()
            for group in range(at * half // SUB, (at + 1) * half // SUB):
                for block in range(SUB):
                    tile = ((part * (bins // SUB) + group) * SUB + block) * SUB
                    tiles_ref[tile : tile + SUB, :] = image_ref[
                        part, group * SUB : (group + 1) * SUB, block * SIDE : (block + 1) * SIDE
                    ]
            for row in range(at * half, (at + 1) * half):
                out_ref[places[row] + part * 4] = tiles_ref[pl.ds(tile_at(bins, part, row), SUB, stride=SUB), :]


def unpack_kernel(at_ref, rows_ref, phase_ref, image_hbm, phase_hbm, image_ref, tiles_ref, sems):
    bins = image_ref.shape[1]
    copies = [pltpu.make_async_copy(phase_ref, phase_hbm, sems.at[4])]
    copies[0].start()
    places = [at_ref[SUB + row, 0] for row in range(bins)]
    for part in range(2):
        for row in range(bins):
            tiles_ref[pl.ds(tile_at(bins, part, row), SUB, stride=SUB), :] = rows_ref[places[row] + part * 4]
        for half in range(2):
            span = slice(half * bins // 2, (half + 1) * bins // 2)
            for group in range(half * bins // 2 // SUB, (half + 1) * bins // 2 // SUB):
                for block in range(SUB):
                    at = ((part * (bins // SUB) + group) * SUB + block) * SUB
                    image_ref[part, group * SUB : (group + 1) * SUB, block * SIDE : (block + 1) * SIDE] = tiles_ref[
                        at : at + SUB, :
                    ]
            copies.append(
                pltpu.make_async_copy(
                    image_ref.at[part, span], image_hbm.at[part, span], sems.at[part * 2 + half]
                )
            )
            copies[-1].start()
    for copy in copies:
        copy.wait()


def offsets(at_ref, line):
    return [at_ref[4 * line + where, 0] for where in range(3)]


def first_kernel(
    at_ref, rows_ref, window_ref, sides_ref, twist_ref, out_ref, history_ref, ring_ref
):
    lines = []
    for at in range(2):
        row, lane, width = offsets(at_ref, at)
        parts = []
        for part in range(2):
            ring = ring_ref.at[at * 2 + part]
            ring[:SIDE, :] = square(rows_ref, part * 4 + at)
            ring[SIDE:, :] = rows_ref[: LOAD // SUB, part * 4 + at].reshape(LOAD, SIDE)
            parts.append(center(ring[pl.ds(row, WINDOW), :], ring[pl.ds(row + 1, WINDOW), :], lane, width))
        lines.append(parts)
    gradient_sums(forward(lines, lambda lines: multiply_window(window_ref[...], lines), sides_ref, twist_ref), out_ref)
    for begin, count in ((0, 3), (2, 2)):
        lines = [[square(rows_ref, part * 4 + begin + at) for part in range(2)] for at in range(2)]
        whole = stacked_of(sides_ref, RIGHT_T, count)
        spectra = forward(lines, lambda lines: multiply(whole, split(lines, count)), sides_ref, twist_ref, count)
        for at in range(2):
            for part in range(2):
                history_ref[begin + at, part] = spectra[at][part]


def square(rows_ref, slot):
    return rows_ref[:, slot].reshape(SIDE, SIDE)


def share_kernel(in_ref, out_ref):
    out_ref[...] = jnp.broadcast_to(jnp.sum(in_ref[...], axis=0)[None], out_ref.shape)


def gradient_kernel(in_ref, out_ref):
    sums = jnp.sum(in_ref[...], axis=0)
    out_ref[...] = jnp.broadcast_to((sums[0] / (sums[1] + EPSILON))[None], out_ref.shape)


def second_kernel(
    at_ref, gradient_ref, history_ref, window_ref, ring_ref, sides_ref, twist_ref,
    out_ref, total_ref, whole_ref,
):
    total = phase_of(gradient_ref, whole_ref)
    total_ref[...] = total
    lines = turn_back([(history_ref[at, 0], history_ref[at, 1]) for at in range(2)], total)
    centered = []
    for at, started in enumerate(inverse_start(lines, sides_ref, twist_ref)):
        row, lane, width = offsets(at_ref, at)
        cosine, sine = ring_ref[0, pl.ds(row, LOAD), :], ring_ref[1, pl.ds(row, LOAD), :]
        left = [jnp.concatenate([cosine, -sine], axis=1), jnp.concatenate([sine, cosine], axis=1)]
        found = multiply(stack(jnp.concatenate(left, axis=0)), split(started, 3))
        centered.append(
            [
                center(found[from_row : from_row + WINDOW], found[from_row + 1 : from_row + 1 + WINDOW], lane, width)
                for from_row in (0, LOAD)
            ]
        )
    gradient_sums(forward(centered, lambda lines: multiply_window(window_ref[...], lines), sides_ref, twist_ref), out_ref)


def final_kernel(
    gradient_ref, total_ref, history_ref, sides_ref, twist_ref, out_ref, phase_ref, turned_ref
):
    total = total_ref[...] + phase_of(gradient_ref, turned_ref)
    lines = turn_back([(history_ref[at, 0], history_ref[at, 1]) for at in range(4)], total)
    started = inverse_start(lines, sides_ref, twist_ref, 2)
    found = multiply(stacked_of(sides_ref, RIGHT, 2), split(jnp.concatenate(started, axis=1), 2))
    for at in range(4):
        for part in range(2):
            line = found[part * SIDE : (part + 1) * SIDE, at * SIDE : (at + 1) * SIDE]
            out_ref[:, part * 4 + at] = line.reshape(TILES, SUB, SIDE)
    turned_ref[...] = total.T
    phase_ref[...] = turned_ref[pl.ds(pl.multiple_of(lax.axis_index(AZ) * SUB, SUB), SUB), :]


SMEM = pl.BlockSpec(memory_space=pltpu.SMEM)
VMEM = pl.BlockSpec(memory_space=pltpu.VMEM)
HBM = pl.BlockSpec(memory_space=pltpu.HBM)


def call(kernel, shapes, specs, *operands, scratch=(), out_specs=None):
    out = pl.pallas_call(
        kernel,
        out_shape=[jax.ShapeDtypeStruct(*shape) for shape in shapes],
        in_specs=list(specs),
        out_specs=out_specs or [VMEM] * len(shapes),
        scratch_shapes=list(scratch),
        compiler_params=pltpu.CompilerParams(vmem_limit_bytes=32 * 1024 * 1024),
    )(*operands)
    return out if len(out) > 1 else out[0]


def exchange(array, axes):
    return lax.all_to_all(array, axes, split_axis=0, concat_axis=0, tiled=True)


RNG = ("zh", "zl", "x")
AZ = ("yh", "yl", "core")
NEAR = ("zl", "x", "yl", "core")
FAR = ("zh", "yh")


def local(sar_image, strong_index, shifts, widths):
    f32, i32 = jnp.float32, jnp.int32
    az, near, far = lax.axis_size(AZ), lax.axis_size(NEAR), lax.axis_size(FAR)
    bins, pulses_local = sar_image.shape[1:]
    table = tables()
    tile = (SUB, SIDE)
    part = SIDE // near
    sums_shape = (near, 2, part, SIDE)
    moved_tiles = pltpu.VMEM((2 * bins * SUB, SIDE), f32)

    packed, places = call(
        pack_kernel,
        [((az * 8,) + tile, f32), ((SUB + bins, SIDE), i32)],
        [HBM] * 4,
        *(pltpu.with_memory_space_constraint(array, pltpu.HBM) for array in (strong_index, shifts, widths, sar_image)),
        scratch=[pltpu.SMEM((bins,), i32)]
        + [pltpu.SMEM(strong_index.shape, i32) for _ in range(3)]
        + [
            pltpu.VMEM(sar_image.shape, f32),
            moved_tiles,
            pltpu.SemaphoreType.DMA((3,)),
            pltpu.SemaphoreType.DMA((4,)),
        ],
        out_specs=[VMEM, VMEM],
    )
    rows = exchange(packed.reshape((az, 8) + tile), AZ)
    sums, history = call(
        first_kernel,
        [(sums_shape, f32), ((4, 2, SIDE, SIDE), f32)],
        [VMEM] * 5,
        places,
        rows,
        table["window"],
        table["sides"],
        table["twist"],
        scratch=[pltpu.VMEM((4, SIDE + LOAD, SIDE), f32)],
    )

    def all_gradients(sums):
        scattered = exchange(sums, NEAR)
        partial = call(share_kernel, [((far, 2, part, SIDE), f32)], [VMEM], scattered)
        everyone = exchange(partial, FAR)
        gradient = call(gradient_kernel, [((near, part, SIDE), f32)], [VMEM], everyone)
        return exchange(gradient, NEAR)

    gradient = all_gradients(sums)
    sums, total = call(
        second_kernel,
        [(sums_shape, f32), ((SIDE, SIDE), f32)],
        [VMEM] * 7,
        places,
        gradient,
        history,
        table["window"],
        table["ring"],
        table["sides"],
        table["twist"],
        scratch=[pltpu.VMEM((SIDE, SIDE), f32)],
    )
    gradient = all_gradients(sums)
    corrected, phase = call(
        final_kernel,
        [((az, 8) + tile, f32), (tile, f32)],
        [VMEM] * 5,
        gradient,
        total,
        history,
        table["sides"],
        table["twist"],
        scratch=[pltpu.VMEM((SIDE, SIDE), f32)],
    )
    returned = exchange(corrected, AZ)
    focused, phase = call(
        unpack_kernel,
        [(sar_image.shape, f32), (tile, f32)],
        [VMEM, VMEM, VMEM],
        places,
        returned.reshape((az * 8,) + tile),
        phase,
        scratch=[pltpu.VMEM(sar_image.shape, f32), moved_tiles, pltpu.SemaphoreType.DMA((5,))],
        out_specs=[HBM, HBM],
    )
    return focused, phase.reshape(pulses_local)


def solution(mesh):
    rng, az = mesh.devices.shape
    along_x = max(1, min(4, rng // 2))
    split = Mesh(
        mesh.devices.reshape(rng // (2 * along_x), 2, along_x, az // 4, 2, 2), RNG + AZ
    )
    placed = (P(None, RNG, AZ), P(RNG), P(RNG), P(RNG))
    return jax.shard_map(
        local,
        mesh=split,
        in_specs=placed,
        out_specs=(P(None, RNG, AZ), P(AZ)),
        check_vma=False,
    )
```

```python
import jax
import jax.numpy as jnp
import numpy as np
from jax import lax
from jax.experimental import pallas as pl
from jax.experimental.pallas import tpu as pltpu
from jax.sharding import Mesh, PartitionSpec as P

EPSILON = 1e-06
SIDE = 128
SUB = 8
TILES = SIDE // SUB
WINDOW = 16
FIRST = SIDE // 2 - WINDOW // 2
RIGHT, RIGHT_T = 0, 1
LOAD = 24


def tables():
    grid = np.arange(SIDE)
    product = grid[:, None] * grid[None, :]
    angle = 2.0 * np.pi * (product % SIDE) / SIDE
    cosine, sine = np.cos(angle), np.sin(angle)
    right = np.block([[cosine, -sine], [sine, cosine]])
    rows = slice(FIRST, FIRST + WINDOW)
    window = np.block([[cosine[:, rows], sine[:, rows]], [-sine[:, rows], cosine[:, rows]]])
    around = np.arange(SIDE + LOAD) % SIDE
    ring = np.stack([cosine[around], sine[around]])
    twist = 2.0 * np.pi * product / (SIDE * SIDE)
    twist = np.stack([np.cos(twist), np.sin(twist)]) / SIDE
    made = dict(ring=ring, twist=twist)
    made = {name: jnp.asarray(table.astype(np.float32)) for name, table in made.items()}

    def parts(table):
        found, rest = [], table.astype(np.float32)
        for _ in range(3):
            found.append(rest.astype(jnp.bfloat16))
            rest = rest - found[-1].astype(np.float32)
        return found

    window = parts(window)
    made["window"] = jnp.asarray(np.concatenate([window[at] for at in (0, 0, 1, 0, 1, 2)], axis=1))
    made["sides"] = jnp.asarray(np.concatenate(parts(right) + parts(right.T), axis=0))
    return made


def split(array, count):
    parts = []
    for _ in range(count):
        parts.append(array.astype(jnp.bfloat16))
        array = array - parts[-1].astype(jnp.float32)
    return parts


def dot(left, right):
    return jnp.dot(left, right, preferred_element_type=jnp.float32)


def stack(array, count=3):
    return jnp.concatenate(split(array, count), axis=0)


def multiply(left, right):
    count = len(right)
    rows = left.shape[0] // count
    by_order = [None] * count
    for at in range(count):
        product = dot(left[: (count - at) * rows], right[at])
        for order in range(count - at):
            term = product[order * rows : (order + 1) * rows]
            by_order[at + order] = term if by_order[at + order] is None else by_order[at + order] + term
    total = by_order[-1]
    for term in reversed(by_order[:-1]):
        total = total + term
    return total


def multiply_window(left, right):
    first, second, third = split(right, 3)
    return dot(left, jnp.concatenate([first, second, first, third, second, first], axis=0))


def forward(lines, first_stage, sides_ref, twist_ref, count=3):
    cosine, sine = twist_ref[0], twist_ref[1]
    first = first_stage(jnp.concatenate([jnp.concatenate(line, axis=0) for line in lines], axis=1))
    turned = []
    for at in range(len(lines)):
        real = first[:SIDE, at * SIDE : (at + 1) * SIDE]
        imag = first[SIDE:, at * SIDE : (at + 1) * SIDE]
        turned.append(jnp.concatenate([real * cosine + imag * sine, imag * cosine - real * sine], axis=1))
    second = multiply(stack(jnp.concatenate(turned, axis=0), count), parts_of(sides_ref, RIGHT, count))
    return [
        (second[at * SIDE : (at + 1) * SIDE, :SIDE], second[at * SIDE : (at + 1) * SIDE, SIDE:])
        for at in range(len(lines))
    ]


def inverse_start(lines, sides_ref, twist_ref, count=3):
    cosine, sine = twist_ref[0], twist_ref[1]
    stacked = jnp.concatenate([jnp.concatenate(line, axis=1) for line in lines], axis=0)
    first = multiply(stack(stacked, count), parts_of(sides_ref, RIGHT_T, count))
    turned = []
    for at in range(len(lines)):
        real = first[at * SIDE : (at + 1) * SIDE, :SIDE]
        imag = first[at * SIDE : (at + 1) * SIDE, SIDE:]
        turned.append(jnp.concatenate([real * cosine - imag * sine, imag * cosine + real * sine], axis=0))
    return turned


def stacked_of(sides_ref, which, count=3):
    return sides_ref[which * 6 * SIDE : (which * 6 + 2 * count) * SIDE, :]


def parts_of(sides_ref, which, count=3):
    return [sides_ref[(which * 3 + at) * 2 * SIDE : (which * 3 + at + 1) * 2 * SIDE, :] for at in range(count)]


def grid_of(rows):
    return (
        lax.broadcasted_iota(jnp.int32, (rows, SIDE), 0),
        lax.broadcasted_iota(jnp.int32, (rows, SIDE), 1),
    )


def running_sum(gradient):
    rows, cols = grid_of(SIDE)
    within = dot(
        (cols <= rows).astype(jnp.float32).astype(jnp.bfloat16), jnp.concatenate(split(gradient, 3), axis=1)
    )
    sums = jnp.broadcast_to(jnp.sum(gradient, axis=0, keepdims=True), (16, SIDE))
    before = dot(
        jnp.concatenate(split(sums, 3), axis=0), (rows < cols).astype(jnp.float32).astype(jnp.bfloat16)
    )
    within = within[:, :SIDE] + (within[:, SIDE : 2 * SIDE] + within[:, 2 * SIDE :])
    return within + (before[:1, :] + (before[16:17, :] + before[32:33, :]))


def phase_of(gradient_ref, whole_ref):
    near, rows = gradient_ref.shape[:2]
    for at in range(near):
        whole_ref[at * rows : (at + 1) * rows, :] = gradient_ref[at]
    return running_sum(whole_ref[...])


def cosine_sine(angle):
    quarters = jnp.floor(angle * (2.0 / np.pi) + 0.5)
    rest = angle - quarters * 1.5703125
    rest = rest - quarters * 4.837512969970703125e-4
    rest = rest - quarters * 7.54978995489188216e-8
    square = rest * rest
    sine = ((-1.9515295891e-4 * square + 8.3321608736e-3) * square - 1.6666654611e-1) * square * rest + rest
    cosine = (2.443315711809948e-5 * square - 1.388731625493765e-3) * square + 4.166664568298827e-2
    cosine = cosine * square * square - 0.5 * square + 1.0
    turn = quarters.astype(jnp.int32)
    odd = (turn & 1) == 1
    sine, cosine = jnp.where(odd, cosine, sine), jnp.where(odd, sine, cosine)
    return jnp.where(((turn + 1) & 2) == 2, -cosine, cosine), jnp.where((turn & 2) == 2, -sine, sine)


def turn_back(lines, total):
    cosine, sine = cosine_sine(total)
    return [(real * cosine + imag * sine, imag * cosine - real * sine) for real, imag in lines]


def row_offset(shift):
    begin = (shift + SIDE * SIDE // 2) & (SIDE * SIDE - 1)
    return ((begin >> 7) + FIRST) & (SIDE - 1), begin & (SIDE - 1)


def center(upper, lower, lane, width):
    rows, cols = grid_of(WINDOW)
    turn = (SIDE - lane) & (SIDE - 1)
    moved = jnp.where(cols >= SIDE - lane, pltpu.roll(lower, turn, 1), pltpu.roll(upper, turn, 1))
    cells = (rows + FIRST) * SIDE + cols
    least = SIDE * SIDE // 2 - width // 2
    return jnp.where((cells >= least) & (cells < least + width), moved, 0.0)


def gradient_sums(lines, out_ref):
    rows, cols = grid_of(SIDE)
    numerator = jnp.zeros((SIDE, SIDE), jnp.float32)
    denominator = jnp.zeros((SIDE, SIDE), jnp.float32)

    def before(part):
        down = pltpu.roll(part, 1, 0)
        return jnp.where(rows == 0, pltpu.roll(down, 1, 1), down)

    for real, imag in lines:
        numerator = numerator + (before(real) * imag - before(imag) * real)
        denominator = denominator + (real * real + imag * imag)
    numerator = jnp.where((rows == 0) & (cols == 0), 0.0, numerator)
    near, _, part = out_ref.shape[:3]
    for at in range(near):
        out_ref[at, 0] = numerator[at * part : (at + 1) * part, :]
        out_ref[at, 1] = denominator[at * part : (at + 1) * part, :]


def tile_at(bins, part, row):
    return (part * (bins // SUB) + row // SUB) * SUB * SUB + row % SUB


def pack_kernel(
    strong_hbm, shifts_hbm, widths_hbm, image_hbm, out_ref, at_ref,
    place_ref, strong_ref, shifts_ref, widths_ref, tiles_ref, small_sems, sems,
):
    bins = image_hbm.shape[0] // (2 * SUB)
    strong = strong_ref.shape[0]
    indices = pltpu.make_async_copy(strong_hbm, strong_ref, small_sems.at[0])
    indices.start()
    parts = [
        pltpu.make_async_copy(image_hbm.at[pl.ds(part * SUB * bins, SUB * bins)], tiles_ref.at[pl.ds(part * SUB * bins, SUB * bins)], sems.at[part])
        for part in range(2)
    ]
    for copy in parts:
        copy.start()
    others_in = [
        pltpu.make_async_copy(shifts_hbm, shifts_ref, small_sems.at[1]),
        pltpu.make_async_copy(widths_hbm, widths_ref, small_sems.at[2]),
    ]
    for copy in others_in:
        copy.start()
    for row in range(bins):
        place_ref[row] = -1
    indices.wait()
    for at in range(strong):
        place_ref[strong_ref[at] & (bins - 1)] = at // 2 * 8 + at % 2
    others = jnp.int32(0)
    for row in range(bins):
        held = place_ref[row]
        place = jnp.where(held < 0, ((others >> 1) << 3) + (others & 1) + 2, held)
        others = others + (held < 0).astype(jnp.int32)
        at_ref[SUB + row] = place
    for copy in others_in:
        copy.wait()
    for at in range(2):
        line = lax.axis_index(AZ) * 2 + at
        for where, value in enumerate(row_offset(shifts_ref[line]) + (widths_ref[line],)):
            at_ref[4 * at + where] = value
    for part in range(2):
        parts[part].wait()
        for row in range(bins):
            out_ref[at_ref[SUB + row] + part * 4] = tiles_ref[pl.ds(tile_at(bins, part, row), SUB, stride=SUB), :]


def unpack_kernel(at_ref, rows_ref, phase_ref, image_hbm, phase_hbm, tiles_ref, sems):
    bins = image_hbm.shape[0] // (2 * SUB)
    copies = [pltpu.make_async_copy(phase_ref, phase_hbm, sems.at[4])]
    copies[0].start()
    places = [at_ref[SUB + row] for row in range(bins)]
    for part in range(2):
        for half in range(2):
            for row in range(half * bins // 2, (half + 1) * bins // 2):
                tiles_ref[pl.ds(tile_at(bins, part, row), SUB, stride=SUB), :] = rows_ref[places[row] + part * 4]
            span = pl.ds((part * 2 + half) * SUB * bins // 2, SUB * bins // 2)
            copies.append(pltpu.make_async_copy(tiles_ref.at[span], image_hbm.at[span], sems.at[part * 2 + half]))
            copies[-1].start()
    for copy in copies:
        copy.wait()


def offsets(at_ref, line):
    return [at_ref[4 * line + where] for where in range(3)]


def first_kernel(
    at_ref, rows_ref, window_ref, sides_ref, twist_ref, out_ref, history_ref, ring_ref
):
    lines = []
    for at in range(2):
        row, lane, width = offsets(at_ref, at)
        parts = []
        for part in range(2):
            ring = ring_ref.at[at * 2 + part]
            ring[:SIDE, :] = square(rows_ref, part * 4 + at)
            ring[SIDE:, :] = rows_ref[: LOAD // SUB, part * 4 + at].reshape(LOAD, SIDE)
            parts.append(center(ring[pl.ds(row, WINDOW), :], ring[pl.ds(row + 1, WINDOW), :], lane, width))
        lines.append(parts)
    gradient_sums(forward(lines, lambda lines: multiply_window(window_ref[...], lines), sides_ref, twist_ref), out_ref)
    for begin, count in ((0, 3), (2, 2)):
        lines = [[square(rows_ref, part * 4 + begin + at) for part in range(2)] for at in range(2)]
        whole = stacked_of(sides_ref, RIGHT_T, count)
        spectra = forward(lines, lambda lines: multiply(whole, split(lines, count)), sides_ref, twist_ref, count)
        for at in range(2):
            for part in range(2):
                history_ref[begin + at, part] = spectra[at][part]


def square(rows_ref, slot):
    return rows_ref[:, slot].reshape(SIDE, SIDE)


def share_kernel(in_ref, out_ref):
    out_ref[...] = jnp.broadcast_to(jnp.sum(in_ref[...], axis=0)[None], out_ref.shape)


def gradient_kernel(in_ref, out_ref):
    sums = jnp.sum(in_ref[...], axis=0)
    out_ref[...] = jnp.broadcast_to((sums[0] / (sums[1] + EPSILON))[None], out_ref.shape)


def second_kernel(
    at_ref, gradient_ref, history_ref, window_ref, ring_ref, sides_ref, twist_ref,
    out_ref, total_ref, whole_ref,
):
    total = phase_of(gradient_ref, whole_ref)
    total_ref[...] = total
    lines = turn_back([(history_ref[at, 0], history_ref[at, 1]) for at in range(2)], total)
    centered = []
    for at, started in enumerate(inverse_start(lines, sides_ref, twist_ref)):
        row, lane, width = offsets(at_ref, at)
        cosine, sine = ring_ref[0, pl.ds(row, LOAD), :], ring_ref[1, pl.ds(row, LOAD), :]
        left = [jnp.concatenate([cosine, -sine], axis=1), jnp.concatenate([sine, cosine], axis=1)]
        found = multiply(stack(jnp.concatenate(left, axis=0)), split(started, 3))
        centered.append(
            [
                center(found[from_row : from_row + WINDOW], found[from_row + 1 : from_row + 1 + WINDOW], lane, width)
                for from_row in (0, LOAD)
            ]
        )
    gradient_sums(forward(centered, lambda lines: multiply_window(window_ref[...], lines), sides_ref, twist_ref), out_ref)


def final_kernel(
    gradient_ref, total_ref, history_ref, sides_ref, twist_ref, out_ref, phase_ref, turned_ref
):
    total = total_ref[...] + phase_of(gradient_ref, turned_ref)
    lines = turn_back([(history_ref[at, 0], history_ref[at, 1]) for at in range(4)], total)
    started = inverse_start(lines, sides_ref, twist_ref, 2)
    found = multiply(stacked_of(sides_ref, RIGHT, 2), split(jnp.concatenate(started, axis=1), 2))
    for at in range(4):
        for part in range(2):
            line = found[part * SIDE : (part + 1) * SIDE, at * SIDE : (at + 1) * SIDE]
            out_ref[:, part * 4 + at] = line.reshape(TILES, SUB, SIDE)
    turned_ref[...] = total.T
    phase_ref[...] = turned_ref[pl.ds(pl.multiple_of(lax.axis_index(AZ) * SUB, SUB), SUB), :]


SMEM = pl.BlockSpec(memory_space=pltpu.SMEM)
VMEM = pl.BlockSpec(memory_space=pltpu.VMEM)
HBM = pl.BlockSpec(memory_space=pltpu.HBM)


def call(kernel, shapes, specs, *operands, scratch=(), out_specs=None):
    out = pl.pallas_call(
        kernel,
        out_shape=[shape if isinstance(shape, pl.MemoryRef) else jax.ShapeDtypeStruct(*shape) for shape in shapes],
        in_specs=list(specs),
        out_specs=out_specs or [VMEM] * len(shapes),
        scratch_shapes=list(scratch),
        compiler_params=pltpu.CompilerParams(vmem_limit_bytes=32 * 1024 * 1024),
    )(*operands)
    return out if len(out) > 1 else out[0]


def exchange(array, axes):
    return lax.all_to_all(array, axes, split_axis=0, concat_axis=0, tiled=True)


RNG = ("zh", "zl", "x")
AZ = ("yh", "yl", "core")
NEAR = ("zl", "x", "yl", "core")
FAR = ("zh", "yh")


def local(sar_image, strong_index, shifts, widths):
    f32, i32 = jnp.float32, jnp.int32
    az, near, far = lax.axis_size(AZ), lax.axis_size(NEAR), lax.axis_size(FAR)
    bins, pulses_local = sar_image.shape[1:]
    table = tables()
    tile = (SUB, SIDE)
    tiles = (2, bins // SUB, SUB, pulses_local // SIDE, SIDE)
    image = sar_image.reshape(tiles).transpose(0, 1, 3, 2, 4).reshape(2 * bins * SUB, SIDE)
    part = SIDE // near
    sums_shape = (near, 2, part, SIDE)
    moved_tiles = pltpu.VMEM((2 * bins * SUB, SIDE), f32)

    packed, places = call(
        pack_kernel,
        [((az * 8,) + tile, f32), pltpu.SMEM((SUB + bins,), i32)],
        [HBM] * 4,
        *(pltpu.with_memory_space_constraint(array, pltpu.HBM) for array in (strong_index, shifts, widths, image)),
        scratch=[pltpu.SMEM((bins,), i32)]
        + [pltpu.SMEM(strong_index.shape, i32) for _ in range(3)]
        + [
            moved_tiles,
            pltpu.SemaphoreType.DMA((3,)),
            pltpu.SemaphoreType.DMA((2,)),
        ],
        out_specs=[VMEM, SMEM],
    )
    places = pltpu.with_memory_space_constraint(places, pltpu.SMEM)
    rows = exchange(packed.reshape((az, 8) + tile), AZ)
    sums, history = call(
        first_kernel,
        [(sums_shape, f32), ((4, 2, SIDE, SIDE), f32)],
        [SMEM] + [VMEM] * 4,
        places,
        rows,
        table["window"],
        table["sides"],
        table["twist"],
        scratch=[pltpu.VMEM((4, SIDE + LOAD, SIDE), f32)],
    )

    def all_gradients(sums):
        scattered = exchange(sums, NEAR)
        partial = call(share_kernel, [((far, 2, part, SIDE), f32)], [VMEM], scattered)
        everyone = exchange(partial, FAR)
        gradient = call(gradient_kernel, [((near, part, SIDE), f32)], [VMEM], everyone)
        return exchange(gradient, NEAR)

    gradient = all_gradients(sums)
    sums, total = call(
        second_kernel,
        [(sums_shape, f32), ((SIDE, SIDE), f32)],
        [SMEM] + [VMEM] * 6,
        places,
        gradient,
        history,
        table["window"],
        table["ring"],
        table["sides"],
        table["twist"],
        scratch=[pltpu.VMEM((SIDE, SIDE), f32)],
    )
    gradient = all_gradients(sums)
    corrected, phase = call(
        final_kernel,
        [((az, 8) + tile, f32), (tile, f32)],
        [VMEM] * 5,
        gradient,
        total,
        history,
        table["sides"],
        table["twist"],
        scratch=[pltpu.VMEM((SIDE, SIDE), f32)],
    )
    returned = exchange(corrected, AZ)
    focused, phase = call(
        unpack_kernel,
        [(image.shape, f32), (tile, f32)],
        [SMEM, VMEM, VMEM],
        places,
        returned.reshape((az * 8,) + tile),
        phase,
        scratch=[moved_tiles, pltpu.SemaphoreType.DMA((5,))],
        out_specs=[HBM, HBM],
    )
    focused = focused.reshape(2, bins // SUB, pulses_local // SIDE, SUB, SIDE).transpose(0, 1, 3, 2, 4)
    return focused.reshape(sar_image.shape), phase.reshape(pulses_local)


def solution(mesh):
    rng, az = mesh.devices.shape
    along_x = max(1, min(4, rng // 2))
    split = Mesh(
        mesh.devices.reshape(rng // (2 * along_x), 2, along_x, az // 4, 2, 2), RNG + AZ
    )
    placed = (P(None, RNG, AZ), P(RNG), P(RNG), P(RNG))
    return jax.shard_map(
        local,
        mesh=split,
        in_specs=placed,
        out_specs=(P(None, RNG, AZ), P(AZ)),
        check_vma=False,
    )
```

```python
import jax
import jax.numpy as jnp
import numpy as np
from jax import lax
from jax.experimental import pallas as pl
from jax.experimental.pallas import tpu as pltpu
from jax.sharding import Mesh, PartitionSpec as P

EPSILON = 1e-06
SIDE = 128
SUB = 8
TILES = SIDE // SUB
WINDOW = 16
FIRST = SIDE // 2 - WINDOW // 2
RIGHT, RIGHT_T = 0, 1
LOAD = 24


def tables():
    grid = np.arange(SIDE)
    product = grid[:, None] * grid[None, :]
    angle = 2.0 * np.pi * (product % SIDE) / SIDE
    cosine, sine = np.cos(angle), np.sin(angle)
    right = np.block([[cosine, -sine], [sine, cosine]])
    rows = slice(FIRST, FIRST + WINDOW)
    window = np.block([[cosine[:, rows], sine[:, rows]], [-sine[:, rows], cosine[:, rows]]])
    around = np.arange(SIDE + LOAD) % SIDE
    ring = np.stack([cosine[around], sine[around]])
    twist = 2.0 * np.pi * product / (SIDE * SIDE)
    twist = np.stack([np.cos(twist), np.sin(twist)]) / SIDE
    made = dict(ring=ring, twist=twist)
    made = {name: jnp.asarray(table.astype(np.float32)) for name, table in made.items()}

    def parts(table):
        found, rest = [], table.astype(np.float32)
        for _ in range(3):
            found.append(rest.astype(jnp.bfloat16))
            rest = rest - found[-1].astype(np.float32)
        return found

    window = parts(window)
    made["window"] = jnp.asarray(np.concatenate([window[at] for at in (0, 0, 1, 0, 1, 2)], axis=1))
    made["sides"] = jnp.asarray(np.concatenate(parts(right) + parts(right.T), axis=0))
    return made


def split(array, count):
    parts = []
    for _ in range(count):
        parts.append(array.astype(jnp.bfloat16))
        array = array - parts[-1].astype(jnp.float32)
    return parts


def dot(left, right):
    return jnp.dot(left, right, preferred_element_type=jnp.float32)


def stack(array, count=3):
    return jnp.concatenate(split(array, count), axis=0)


def multiply(left, right):
    count = len(right)
    rows = left.shape[0] // count
    by_order = [None] * count
    for at in range(count):
        product = dot(left[: (count - at) * rows], right[at])
        for order in range(count - at):
            term = product[order * rows : (order + 1) * rows]
            by_order[at + order] = term if by_order[at + order] is None else by_order[at + order] + term
    total = by_order[-1]
    for term in reversed(by_order[:-1]):
        total = total + term
    return total


def multiply_window(left, right):
    first, second, third = split(right, 3)
    return dot(left, jnp.concatenate([first, second, first, third, second, first], axis=0))


def forward(lines, first_stage, sides_ref, twist_ref, count=3):
    cosine, sine = twist_ref[0], twist_ref[1]
    first = first_stage(jnp.concatenate([jnp.concatenate(line, axis=0) for line in lines], axis=1))
    turned = []
    for at in range(len(lines)):
        real = first[:SIDE, at * SIDE : (at + 1) * SIDE]
        imag = first[SIDE:, at * SIDE : (at + 1) * SIDE]
        turned.append(jnp.concatenate([real * cosine + imag * sine, imag * cosine - real * sine], axis=1))
    second = multiply(stack(jnp.concatenate(turned, axis=0), count), parts_of(sides_ref, RIGHT, count))
    return [
        (second[at * SIDE : (at + 1) * SIDE, :SIDE], second[at * SIDE : (at + 1) * SIDE, SIDE:])
        for at in range(len(lines))
    ]


def inverse_start(lines, sides_ref, twist_ref, count=3):
    cosine, sine = twist_ref[0], twist_ref[1]
    stacked = jnp.concatenate([jnp.concatenate(line, axis=1) for line in lines], axis=0)
    first = multiply(stack(stacked, count), parts_of(sides_ref, RIGHT_T, count))
    turned = []
    for at in range(len(lines)):
        real = first[at * SIDE : (at + 1) * SIDE, :SIDE]
        imag = first[at * SIDE : (at + 1) * SIDE, SIDE:]
        turned.append(jnp.concatenate([real * cosine - imag * sine, imag * cosine + real * sine], axis=0))
    return turned


def stacked_of(sides_ref, which, count=3):
    return sides_ref[which * 6 * SIDE : (which * 6 + 2 * count) * SIDE, :]


def parts_of(sides_ref, which, count=3):
    return [sides_ref[(which * 3 + at) * 2 * SIDE : (which * 3 + at + 1) * 2 * SIDE, :] for at in range(count)]


def grid_of(rows):
    return (
        lax.broadcasted_iota(jnp.int32, (rows, SIDE), 0),
        lax.broadcasted_iota(jnp.int32, (rows, SIDE), 1),
    )


def running_sum(gradient):
    rows, cols = grid_of(SIDE)
    within = dot(
        (cols <= rows).astype(jnp.float32).astype(jnp.bfloat16), jnp.concatenate(split(gradient, 3), axis=1)
    )
    sums = jnp.broadcast_to(jnp.sum(gradient, axis=0, keepdims=True), (16, SIDE))
    before = dot(
        jnp.concatenate(split(sums, 3), axis=0), (rows < cols).astype(jnp.float32).astype(jnp.bfloat16)
    )
    within = within[:, :SIDE] + (within[:, SIDE : 2 * SIDE] + within[:, 2 * SIDE :])
    return within + (before[:1, :] + (before[16:17, :] + before[32:33, :]))


def phase_of(gradient_ref, whole_ref):
    near, rows = gradient_ref.shape[:2]
    for at in range(near):
        whole_ref[at * rows : (at + 1) * rows, :] = gradient_ref[at]
    return running_sum(whole_ref[...])


def cosine_sine(angle):
    quarters = jnp.floor(angle * (2.0 / np.pi) + 0.5)
    rest = angle - quarters * 1.5703125
    rest = rest - quarters * 4.837512969970703125e-4
    rest = rest - quarters * 7.54978995489188216e-8
    square = rest * rest
    sine = ((-1.9515295891e-4 * square + 8.3321608736e-3) * square - 1.6666654611e-1) * square * rest + rest
    cosine = (2.443315711809948e-5 * square - 1.388731625493765e-3) * square + 4.166664568298827e-2
    cosine = cosine * square * square - 0.5 * square + 1.0
    turn = quarters.astype(jnp.int32)
    odd = (turn & 1) == 1
    sine, cosine = jnp.where(odd, cosine, sine), jnp.where(odd, sine, cosine)
    return jnp.where(((turn + 1) & 2) == 2, -cosine, cosine), jnp.where((turn & 2) == 2, -sine, sine)


def turn_back(lines, total):
    cosine, sine = cosine_sine(total)
    return [(real * cosine + imag * sine, imag * cosine - real * sine) for real, imag in lines]


def row_offset(shift):
    begin = (shift + SIDE * SIDE // 2) & (SIDE * SIDE - 1)
    return ((begin >> 7) + FIRST) & (SIDE - 1), begin & (SIDE - 1)


def center(upper, lower, lane, width):
    rows, cols = grid_of(WINDOW)
    turn = (SIDE - lane) & (SIDE - 1)
    moved = jnp.where(cols >= SIDE - lane, pltpu.roll(lower, turn, 1), pltpu.roll(upper, turn, 1))
    cells = (rows + FIRST) * SIDE + cols
    least = SIDE * SIDE // 2 - width // 2
    return jnp.where((cells >= least) & (cells < least + width), moved, 0.0)


def gradient_sums(lines, out_ref):
    rows, cols = grid_of(SIDE)
    numerator = jnp.zeros((SIDE, SIDE), jnp.float32)
    denominator = jnp.zeros((SIDE, SIDE), jnp.float32)

    def before(part):
        down = pltpu.roll(part, 1, 0)
        top = jnp.where(rows[:SUB] == 0, pltpu.roll(down[:SUB], 1, 1), down[:SUB])
        return jnp.concatenate([top, down[SUB:]], axis=0)

    for real, imag in lines:
        numerator = numerator + (before(real) * imag - before(imag) * real)
        denominator = denominator + (real * real + imag * imag)
    numerator = jnp.where((rows == 0) & (cols == 0), 0.0, numerator)
    near, _, part = out_ref.shape[:3]
    for at in range(near):
        out_ref[at, 0] = numerator[at * part : (at + 1) * part, :]
        out_ref[at, 1] = denominator[at * part : (at + 1) * part, :]


def tile_at(bins, part, row):
    return (part * (bins // SUB) + row // SUB) * SUB * SUB + row % SUB


def pack_kernel(
    strong_hbm, shifts_hbm, widths_hbm, image_hbm, out_ref, at_ref,
    place_ref, strong_ref, shifts_ref, widths_ref, tiles_ref, small_sems, sems,
):
    bins = image_hbm.shape[0] // (2 * SUB)
    strong = strong_ref.shape[0]
    indices = pltpu.make_async_copy(strong_hbm, strong_ref, small_sems.at[0])
    indices.start()
    parts = [
        pltpu.make_async_copy(image_hbm.at[pl.ds(part * SUB * bins, SUB * bins)], tiles_ref.at[pl.ds(part * SUB * bins, SUB * bins)], sems.at[part])
        for part in range(2)
    ]
    for copy in parts:
        copy.start()
    others_in = [
        pltpu.make_async_copy(shifts_hbm, shifts_ref, small_sems.at[1]),
        pltpu.make_async_copy(widths_hbm, widths_ref, small_sems.at[2]),
    ]
    for copy in others_in:
        copy.start()
    for row in range(bins):
        place_ref[row] = -1
    indices.wait()
    for at in range(strong):
        place_ref[strong_ref[at] & (bins - 1)] = at // 2 * 8 + at % 2
    others = jnp.int32(0)
    places = []
    for row in range(bins):
        held = place_ref[row]
        place = jnp.where(held < 0, ((others >> 1) << 3) + (others & 1) + 2, held)
        others = others + jnp.where(held < 0, 1, 0)
        places.append(place)
        at_ref[SUB + row : SUB + row + 1, :] = jnp.full((1, SIDE), place, jnp.int32)
    for copy in others_in:
        copy.wait()
    for at in range(2):
        line = lax.axis_index(AZ) * 2 + at
        for where, value in enumerate(row_offset(shifts_ref[line]) + (widths_ref[line],)):
            at_ref[4 * at + where : 4 * at + where + 1, :] = jnp.full((1, SIDE), value, jnp.int32)
    for part in range(2):
        parts[part].wait()
        for row in range(bins):
            out_ref[places[row] + part * 4] = tiles_ref[pl.ds(tile_at(bins, part, row), SUB, stride=SUB), :]


def unpack_kernel(at_ref, rows_ref, phase_ref, image_hbm, phase_hbm, tiles_ref, sems):
    bins = image_hbm.shape[0] // (2 * SUB)
    copies = [pltpu.make_async_copy(phase_ref, phase_hbm, sems.at[4])]
    copies[0].start()
    places = [at_ref[SUB + row, 0] for row in range(bins)]
    for part in range(2):
        for half in range(2):
            for row in range(half * bins // 2, (half + 1) * bins // 2):
                tiles_ref[pl.ds(tile_at(bins, part, row), SUB, stride=SUB), :] = rows_ref[places[row] + part * 4]
            span = pl.ds((part * 2 + half) * SUB * bins // 2, SUB * bins // 2)
            copies.append(pltpu.make_async_copy(tiles_ref.at[span], image_hbm.at[span], sems.at[part * 2 + half]))
            copies[-1].start()
    for copy in copies:
        copy.wait()


def offsets(at_ref, line):
    return [at_ref[4 * line + where, 0] for where in range(3)]


def first_kernel(
    at_ref, rows_ref, window_ref, sides_ref, twist_ref, out_ref, history_ref, ring_ref
):
    lines = []
    for at in range(2):
        row, lane, width = offsets(at_ref, at)
        parts = []
        for part in range(2):
            ring = ring_ref.at[at * 2 + part]
            ring[:SIDE, :] = square(rows_ref, part * 4 + at)
            ring[SIDE:, :] = rows_ref[: LOAD // SUB, part * 4 + at].reshape(LOAD, SIDE)
            parts.append(center(ring[pl.ds(row, WINDOW), :], ring[pl.ds(row + 1, WINDOW), :], lane, width))
        lines.append(parts)
    gradient_sums(forward(lines, lambda lines: multiply_window(window_ref[...], lines), sides_ref, twist_ref), out_ref)
    for begin, count in ((0, 3), (2, 2)):
        lines = [[square(rows_ref, part * 4 + begin + at) for part in range(2)] for at in range(2)]
        whole = stacked_of(sides_ref, RIGHT_T, count)
        spectra = forward(lines, lambda lines: multiply(whole, split(lines, count)), sides_ref, twist_ref, count)
        for at in range(2):
            for part in range(2):
                history_ref[begin + at, part] = spectra[at][part]


def square(rows_ref, slot):
    return rows_ref[:, slot].reshape(SIDE, SIDE)


def share_kernel(in_ref, out_ref):
    out_ref[...] = jnp.broadcast_to(jnp.sum(in_ref[...], axis=0)[None], out_ref.shape)


def gradient_kernel(in_ref, out_ref):
    sums = jnp.sum(in_ref[...], axis=0)
    out_ref[...] = jnp.broadcast_to((sums[0] / (sums[1] + EPSILON))[None], out_ref.shape)


def second_kernel(
    at_ref, gradient_ref, history_ref, window_ref, ring_ref, sides_ref, twist_ref,
    out_ref, total_ref, whole_ref,
):
    total = phase_of(gradient_ref, whole_ref)
    total_ref[...] = total
    lines = turn_back([(history_ref[at, 0], history_ref[at, 1]) for at in range(2)], total)
    centered = []
    for at, started in enumerate(inverse_start(lines, sides_ref, twist_ref)):
        row, lane, width = offsets(at_ref, at)
        cosine, sine = ring_ref[0, pl.ds(row, LOAD), :], ring_ref[1, pl.ds(row, LOAD), :]
        left = [jnp.concatenate([cosine, -sine], axis=1), jnp.concatenate([sine, cosine], axis=1)]
        found = multiply(stack(jnp.concatenate(left, axis=0)), split(started, 3))
        centered.append(
            [
                center(found[from_row : from_row + WINDOW], found[from_row + 1 : from_row + 1 + WINDOW], lane, width)
                for from_row in (0, LOAD)
            ]
        )
    gradient_sums(forward(centered, lambda lines: multiply_window(window_ref[...], lines), sides_ref, twist_ref), out_ref)


def final_kernel(
    gradient_ref, total_ref, history_ref, sides_ref, twist_ref, out_ref, phase_ref, turned_ref
):
    total = total_ref[...] + phase_of(gradient_ref, turned_ref)
    lines = turn_back([(history_ref[at, 0], history_ref[at, 1]) for at in range(4)], total)
    started = inverse_start(lines, sides_ref, twist_ref, 2)
    found = multiply(stacked_of(sides_ref, RIGHT, 2), split(jnp.concatenate(started, axis=1), 2))
    for at in range(4):
        for part in range(2):
            line = found[part * SIDE : (part + 1) * SIDE, at * SIDE : (at + 1) * SIDE]
            out_ref[:, part * 4 + at] = line.reshape(TILES, SUB, SIDE)
    turned_ref[...] = total.T
    phase_ref[...] = turned_ref[pl.ds(pl.multiple_of(lax.axis_index(AZ) * SUB, SUB), SUB), :]


SMEM = pl.BlockSpec(memory_space=pltpu.SMEM)
VMEM = pl.BlockSpec(memory_space=pltpu.VMEM)
HBM = pl.BlockSpec(memory_space=pltpu.HBM)


def call(kernel, shapes, specs, *operands, scratch=(), out_specs=None):
    out = pl.pallas_call(
        kernel,
        out_shape=[jax.ShapeDtypeStruct(*shape) for shape in shapes],
        in_specs=list(specs),
        out_specs=out_specs or [VMEM] * len(shapes),
        scratch_shapes=list(scratch),
        compiler_params=pltpu.CompilerParams(vmem_limit_bytes=32 * 1024 * 1024),
    )(*operands)
    return out if len(out) > 1 else out[0]


def exchange(array, axes):
    return lax.all_to_all(array, axes, split_axis=0, concat_axis=0, tiled=True)


RNG = ("zh", "zl", "x")
AZ = ("yh", "yl", "core")
NEAR = ("zl", "x", "yl", "core")
FAR = ("zh", "yh")


def local(sar_image, strong_index, shifts, widths):
    f32, i32 = jnp.float32, jnp.int32
    az, near, far = lax.axis_size(AZ), lax.axis_size(NEAR), lax.axis_size(FAR)
    bins, pulses_local = sar_image.shape[1:]
    table = tables()
    tile = (SUB, SIDE)
    tiles = (2, bins // SUB, SUB, pulses_local // SIDE, SIDE)
    image = sar_image.reshape(tiles).transpose(0, 1, 3, 2, 4).reshape(2 * bins * SUB, SIDE)
    part = SIDE // near
    sums_shape = (near, 2, part, SIDE)
    moved_tiles = pltpu.VMEM((2 * bins * SUB, SIDE), f32)

    packed, places = call(
        pack_kernel,
        [((az * 8,) + tile, f32), ((SUB + bins, SIDE), i32)],
        [HBM] * 4,
        *(pltpu.with_memory_space_constraint(array, pltpu.HBM) for array in (strong_index, shifts, widths, image)),
        scratch=[pltpu.SMEM((bins,), i32)]
        + [pltpu.SMEM(strong_index.shape, i32) for _ in range(3)]
        + [
            moved_tiles,
            pltpu.SemaphoreType.DMA((3,)),
            pltpu.SemaphoreType.DMA((2,)),
        ],
        out_specs=[VMEM, VMEM],
    )
    rows = exchange(packed.reshape((az, 8) + tile), AZ)
    sums, history = call(
        first_kernel,
        [(sums_shape, f32), ((4, 2, SIDE, SIDE), f32)],
        [VMEM] * 5,
        places,
        rows,
        table["window"],
        table["sides"],
        table["twist"],
        scratch=[pltpu.VMEM((4, SIDE + LOAD, SIDE), f32)],
    )

    def all_gradients(sums):
        scattered = exchange(sums, NEAR)
        partial = call(share_kernel, [((far, 2, part, SIDE), f32)], [VMEM], scattered)
        everyone = exchange(partial, FAR)
        gradient = call(gradient_kernel, [((near, part, SIDE), f32)], [VMEM], everyone)
        return exchange(gradient, NEAR)

    gradient = all_gradients(sums)
    sums, total = call(
        second_kernel,
        [(sums_shape, f32), ((SIDE, SIDE), f32)],
        [VMEM] * 7,
        places,
        gradient,
        history,
        table["window"],
        table["ring"],
        table["sides"],
        table["twist"],
        scratch=[pltpu.VMEM((SIDE, SIDE), f32)],
    )
    gradient = all_gradients(sums)
    corrected, phase = call(
        final_kernel,
        [((az, 8) + tile, f32), (tile, f32)],
        [VMEM] * 5,
        gradient,
        total,
        history,
        table["sides"],
        table["twist"],
        scratch=[pltpu.VMEM((SIDE, SIDE), f32)],
    )
    returned = exchange(corrected, AZ)
    focused, phase = call(
        unpack_kernel,
        [(image.shape, f32), (tile, f32)],
        [VMEM, VMEM, VMEM],
        places,
        returned.reshape((az * 8,) + tile),
        phase,
        scratch=[moved_tiles, pltpu.SemaphoreType.DMA((5,))],
        out_specs=[HBM, HBM],
    )
    focused = focused.reshape(2, bins // SUB, pulses_local // SIDE, SUB, SIDE).transpose(0, 1, 3, 2, 4)
    return focused.reshape(sar_image.shape), phase.reshape(pulses_local)


def solution(mesh):
    rng, az = mesh.devices.shape
    along_x = max(1, min(4, rng // 2))
    split = Mesh(
        mesh.devices.reshape(rng // (2 * along_x), 2, along_x, az // 4, 2, 2), RNG + AZ
    )
    placed = (P(None, RNG, AZ), P(RNG), P(RNG), P(RNG))
    return jax.shard_map(
        local,
        mesh=split,
        in_specs=placed,
        out_specs=(P(None, RNG, AZ), P(AZ)),
        check_vma=False,
    )
```

```python
import jax
import jax.numpy as jnp
import numpy as np
from jax import lax
from jax.experimental import pallas as pl
from jax.experimental.pallas import tpu as pltpu
from jax.sharding import Mesh, PartitionSpec as P

EPSILON = 1e-06
SIDE = 128
SUB = 8
TILES = SIDE // SUB
WINDOW = 16
FIRST = SIDE // 2 - WINDOW // 2
RIGHT, RIGHT_T = 0, 1
LOAD = 24


def tables():
    grid = np.arange(SIDE)
    product = grid[:, None] * grid[None, :]
    angle = 2.0 * np.pi * (product % SIDE) / SIDE
    cosine, sine = np.cos(angle), np.sin(angle)
    right = np.block([[cosine, -sine], [sine, cosine]])
    rows = slice(FIRST, FIRST + WINDOW)
    window = np.block([[cosine[:, rows], sine[:, rows]], [-sine[:, rows], cosine[:, rows]]])
    around = np.arange(SIDE + LOAD) % SIDE
    ring = np.stack([cosine[around], sine[around]])
    twist = 2.0 * np.pi * product / (SIDE * SIDE)
    twist = np.stack([np.cos(twist), np.sin(twist)]) / SIDE
    made = dict(ring=ring, twist=twist)
    made = {name: jnp.asarray(table.astype(np.float32)) for name, table in made.items()}

    def parts(table):
        found, rest = [], table.astype(np.float32)
        for _ in range(3):
            found.append(rest.astype(jnp.bfloat16))
            rest = rest - found[-1].astype(np.float32)
        return found

    window = parts(window)
    made["window"] = jnp.asarray(np.concatenate([window[at] for at in (0, 0, 1, 0, 1, 2)], axis=1))
    made["sides"] = jnp.asarray(np.concatenate(parts(right) + parts(right.T), axis=0))
    return made


def split(array, count):
    parts = []
    for _ in range(count):
        parts.append(array.astype(jnp.bfloat16))
        array = array - parts[-1].astype(jnp.float32)
    return parts


def dot(left, right):
    return jnp.dot(left, right, preferred_element_type=jnp.float32)


def stack(array, count=3):
    return jnp.concatenate(split(array, count), axis=0)


def multiply(left, right):
    count = len(right)
    rows = left.shape[0] // count
    by_order = [None] * count
    for at in range(count):
        product = dot(left[: (count - at) * rows], right[at])
        for order in range(count - at):
            term = product[order * rows : (order + 1) * rows]
            by_order[at + order] = term if by_order[at + order] is None else by_order[at + order] + term
    total = by_order[-1]
    for term in reversed(by_order[:-1]):
        total = total + term
    return total


def multiply_window(left, right):
    first, second, third = split(right, 3)
    return dot(left, jnp.concatenate([first, second, first, third, second, first], axis=0))


def forward_start(lines, first_stage, twist_ref):
    cosine, sine = twist_ref[0], twist_ref[1]
    first = first_stage(jnp.concatenate([jnp.concatenate(line, axis=0) for line in lines], axis=1))
    turned = []
    for at in range(len(lines)):
        real = first[:SIDE, at * SIDE : (at + 1) * SIDE]
        imag = first[SIDE:, at * SIDE : (at + 1) * SIDE]
        turned.append(jnp.concatenate([real * cosine + imag * sine, imag * cosine - real * sine], axis=1))
    return jnp.concatenate(turned, axis=0)


def forward_end(started, sides_ref):
    parts = [split(lines, count) for lines, count in started]
    totals = [[] for _ in started]
    for at, right in enumerate(parts_of(sides_ref, RIGHT)):
        used = [(group, part) for group in range(len(started)) for part in range(started[group][1] - at)]
        product = dot(jnp.concatenate([parts[group][part] for group, part in used], axis=0), right)
        begin = 0
        for group, part in used:
            rows = started[group][0].shape[0]
            totals[group].append((at + part, product[begin : begin + rows]))
            begin += rows
    found = []
    for terms in totals:
        terms = [term for _, term in sorted(terms, key=lambda pair: -pair[0])]
        total = terms[0]
        for term in terms[1:]:
            total = total + term
        found.append(
            [(total[at : at + SIDE, :SIDE], total[at : at + SIDE, SIDE:]) for at in range(0, total.shape[0], SIDE)]
        )
    return found


def inverse_start(lines, sides_ref, twist_ref, count=3):
    cosine, sine = twist_ref[0], twist_ref[1]
    stacked = jnp.concatenate([jnp.concatenate(line, axis=1) for line in lines], axis=0)
    first = multiply(stack(stacked, count), parts_of(sides_ref, RIGHT_T, count))
    turned = []
    for at in range(len(lines)):
        real = first[at * SIDE : (at + 1) * SIDE, :SIDE]
        imag = first[at * SIDE : (at + 1) * SIDE, SIDE:]
        turned.append(jnp.concatenate([real * cosine - imag * sine, imag * cosine + real * sine], axis=0))
    return turned


def stacked_of(sides_ref, which, count=3):
    return sides_ref[which * 6 * SIDE : (which * 6 + 2 * count) * SIDE, :]


def parts_of(sides_ref, which, count=3):
    return [sides_ref[(which * 3 + at) * 2 * SIDE : (which * 3 + at + 1) * 2 * SIDE, :] for at in range(count)]


def grid_of(rows):
    return (
        lax.broadcasted_iota(jnp.int32, (rows, SIDE), 0),
        lax.broadcasted_iota(jnp.int32, (rows, SIDE), 1),
    )


def running_sum(gradient):
    rows, cols = grid_of(SIDE)
    within = dot(
        (cols <= rows).astype(jnp.float32).astype(jnp.bfloat16), jnp.concatenate(split(gradient, 3), axis=1)
    )
    sums = jnp.broadcast_to(jnp.sum(gradient, axis=0, keepdims=True), (16, SIDE))
    before = dot(
        jnp.concatenate(split(sums, 3), axis=0), (rows < cols).astype(jnp.float32).astype(jnp.bfloat16)
    )
    within = within[:, :SIDE] + (within[:, SIDE : 2 * SIDE] + within[:, 2 * SIDE :])
    return within + (before[:1, :] + (before[16:17, :] + before[32:33, :]))


def phase_of(gradient_ref, whole_ref):
    near, rows = gradient_ref.shape[:2]
    for at in range(near):
        whole_ref[at * rows : (at + 1) * rows, :] = gradient_ref[at]
    return running_sum(whole_ref[...])


def cosine_sine(angle):
    quarters = jnp.floor(angle * (2.0 / np.pi) + 0.5)
    rest = angle - quarters * 1.5703125
    rest = rest - quarters * 4.837512969970703125e-4
    rest = rest - quarters * 7.54978995489188216e-8
    square = rest * rest
    sine = ((-1.9515295891e-4 * square + 8.3321608736e-3) * square - 1.6666654611e-1) * square * rest + rest
    cosine = (2.443315711809948e-5 * square - 1.388731625493765e-3) * square + 4.166664568298827e-2
    cosine = cosine * square * square - 0.5 * square + 1.0
    turn = quarters.astype(jnp.int32)
    odd = (turn & 1) == 1
    sine, cosine = jnp.where(odd, cosine, sine), jnp.where(odd, sine, cosine)
    return jnp.where(((turn + 1) & 2) == 2, -cosine, cosine), jnp.where((turn & 2) == 2, -sine, sine)


def turn_back(lines, total):
    cosine, sine = cosine_sine(total)
    return [(real * cosine + imag * sine, imag * cosine - real * sine) for real, imag in lines]


def row_offset(shift):
    begin = (shift + SIDE * SIDE // 2) & (SIDE * SIDE - 1)
    return ((begin >> 7) + FIRST) & (SIDE - 1), begin & (SIDE - 1)


def center(upper, lower, lane, width):
    rows, cols = grid_of(WINDOW)
    turn = (SIDE - lane) & (SIDE - 1)
    moved = jnp.where(cols >= SIDE - lane, pltpu.roll(lower, turn, 1), pltpu.roll(upper, turn, 1))
    cells = (rows + FIRST) * SIDE + cols
    least = SIDE * SIDE // 2 - width // 2
    return jnp.where((cells >= least) & (cells < least + width), moved, 0.0)


def gradient_sums(lines, out_ref):
    rows, cols = grid_of(SIDE)
    numerator = jnp.zeros((SIDE, SIDE), jnp.float32)
    denominator = jnp.zeros((SIDE, SIDE), jnp.float32)

    def before(part):
        down = pltpu.roll(part, 1, 0)
        top = jnp.where(rows[:SUB] == 0, pltpu.roll(down[:SUB], 1, 1), down[:SUB])
        return jnp.concatenate([top, down[SUB:]], axis=0)

    for real, imag in lines:
        numerator = numerator + (before(real) * imag - before(imag) * real)
        denominator = denominator + (real * real + imag * imag)
    numerator = jnp.where((rows == 0) & (cols == 0), 0.0, numerator)
    near, _, part = out_ref.shape[:3]
    for at in range(near):
        out_ref[at, 0] = numerator[at * part : (at + 1) * part, :]
        out_ref[at, 1] = denominator[at * part : (at + 1) * part, :]


def tile_at(bins, part, row):
    return (part * (bins // SUB) + row // SUB) * SUB * SUB + row % SUB


def pack_kernel(
    strong_hbm, shifts_hbm, widths_hbm, image_hbm, out_ref, at_ref,
    place_ref, strong_ref, shifts_ref, widths_ref, tiles_ref, small_sems, sems,
):
    bins = image_hbm.shape[0] // (2 * SUB)
    strong = strong_ref.shape[0]
    indices = pltpu.make_async_copy(strong_hbm, strong_ref, small_sems.at[0])
    indices.start()
    parts = [
        pltpu.make_async_copy(image_hbm.at[pl.ds(part * SUB * bins, SUB * bins)], tiles_ref.at[pl.ds(part * SUB * bins, SUB * bins)], sems.at[part])
        for part in range(2)
    ]
    for copy in parts:
        copy.start()
    others_in = [
        pltpu.make_async_copy(shifts_hbm, shifts_ref, small_sems.at[1]),
        pltpu.make_async_copy(widths_hbm, widths_ref, small_sems.at[2]),
    ]
    for copy in others_in:
        copy.start()
    for row in range(bins):
        place_ref[row] = -1
    indices.wait()
    for at in range(strong):
        place_ref[strong_ref[at] & (bins - 1)] = at // 2 * 8 + at % 2
    others = jnp.int32(0)
    places = []
    for row in range(bins):
        held = place_ref[row]
        place = jnp.where(held < 0, ((others >> 1) << 3) + (others & 1) + 2, held)
        others = others + jnp.where(held < 0, 1, 0)
        places.append(place)
        at_ref[SUB + row : SUB + row + 1, :] = jnp.full((1, SIDE), place, jnp.int32)
    for copy in others_in:
        copy.wait()
    for at in range(2):
        line = lax.axis_index(AZ) * 2 + at
        for where, value in enumerate(row_offset(shifts_ref[line]) + (widths_ref[line],)):
            at_ref[4 * at + where : 4 * at + where + 1, :] = jnp.full((1, SIDE), value, jnp.int32)
    for part in range(2):
        parts[part].wait()
        for row in range(bins):
            out_ref[places[row] + part * 4] = tiles_ref[pl.ds(tile_at(bins, part, row), SUB, stride=SUB), :]


def unpack_kernel(at_ref, rows_ref, phase_ref, image_hbm, phase_hbm, tiles_ref, sems):
    bins = image_hbm.shape[0] // (2 * SUB)
    copies = [pltpu.make_async_copy(phase_ref, phase_hbm, sems.at[4])]
    copies[0].start()
    places = [at_ref[SUB + row, 0] for row in range(bins)]
    for part in range(2):
        for half in range(2):
            for row in range(half * bins // 2, (half + 1) * bins // 2):
                tiles_ref[pl.ds(tile_at(bins, part, row), SUB, stride=SUB), :] = rows_ref[places[row] + part * 4]
            span = pl.ds((part * 2 + half) * SUB * bins // 2, SUB * bins // 2)
            copies.append(pltpu.make_async_copy(tiles_ref.at[span], image_hbm.at[span], sems.at[part * 2 + half]))
            copies[-1].start()
    for copy in copies:
        copy.wait()


def offsets(at_ref, line):
    return [at_ref[4 * line + where, 0] for where in range(3)]


def first_kernel(
    at_ref, rows_ref, window_ref, sides_ref, twist_ref, out_ref, history_ref, ring_ref
):
    lines = []
    for at in range(2):
        row, lane, width = offsets(at_ref, at)
        parts = []
        for part in range(2):
            ring = ring_ref.at[at * 2 + part]
            ring[:SIDE, :] = square(rows_ref, part * 4 + at)
            ring[SIDE:, :] = rows_ref[: LOAD // SUB, part * 4 + at].reshape(LOAD, SIDE)
            parts.append(center(ring[pl.ds(row, WINDOW), :], ring[pl.ds(row + 1, WINDOW), :], lane, width))
        lines.append(parts)
    started = [(forward_start(lines, lambda lines: multiply_window(window_ref[...], lines), twist_ref), 3)]
    for begin, count in ((0, 3), (2, 2)):
        lines = [[square(rows_ref, part * 4 + begin + at) for part in range(2)] for at in range(2)]
        whole = stacked_of(sides_ref, RIGHT_T, count)
        started.append((forward_start(lines, lambda lines: multiply(whole, split(lines, count)), twist_ref), count))
    windowed, *history = forward_end(started, sides_ref)
    gradient_sums(windowed, out_ref)
    for begin, spectra in zip((0, 2), history):
        for at in range(2):
            for part in range(2):
                history_ref[begin + at, part] = spectra[at][part]


def square(rows_ref, slot):
    return rows_ref[:, slot].reshape(SIDE, SIDE)


def share_kernel(in_ref, out_ref):
    out_ref[...] = jnp.broadcast_to(jnp.sum(in_ref[...], axis=0)[None], out_ref.shape)


def gradient_kernel(in_ref, out_ref):
    sums = jnp.sum(in_ref[...], axis=0)
    out_ref[...] = jnp.broadcast_to((sums[0] / (sums[1] + EPSILON))[None], out_ref.shape)


def second_kernel(
    at_ref, gradient_ref, history_ref, window_ref, ring_ref, sides_ref, twist_ref,
    out_ref, total_ref, whole_ref,
):
    total = phase_of(gradient_ref, whole_ref)
    total_ref[...] = total
    lines = turn_back([(history_ref[at, 0], history_ref[at, 1]) for at in range(2)], total)
    centered = []
    for at, started in enumerate(inverse_start(lines, sides_ref, twist_ref)):
        row, lane, width = offsets(at_ref, at)
        cosine, sine = ring_ref[0, pl.ds(row, LOAD), :], ring_ref[1, pl.ds(row, LOAD), :]
        left = [jnp.concatenate([cosine, -sine], axis=1), jnp.concatenate([sine, cosine], axis=1)]
        found = multiply(stack(jnp.concatenate(left, axis=0)), split(started, 3))
        centered.append(
            [
                center(found[from_row : from_row + WINDOW], found[from_row + 1 : from_row + 1 + WINDOW], lane, width)
                for from_row in (0, LOAD)
            ]
        )
    started = forward_start(centered, lambda lines: multiply_window(window_ref[...], lines), twist_ref)
    gradient_sums(forward_end([(started, 3)], sides_ref)[0], out_ref)


def final_kernel(
    gradient_ref, total_ref, history_ref, sides_ref, twist_ref, out_ref, phase_ref, turned_ref
):
    total = total_ref[...] + phase_of(gradient_ref, turned_ref)
    lines = turn_back([(history_ref[at, 0], history_ref[at, 1]) for at in range(4)], total)
    started = inverse_start(lines, sides_ref, twist_ref, 2)
    found = multiply(stacked_of(sides_ref, RIGHT, 2), split(jnp.concatenate(started, axis=1), 2))
    for at in range(4):
        for part in range(2):
            line = found[part * SIDE : (part + 1) * SIDE, at * SIDE : (at + 1) * SIDE]
            out_ref[:, part * 4 + at] = line.reshape(TILES, SUB, SIDE)
    turned_ref[...] = total.T
    phase_ref[...] = turned_ref[pl.ds(pl.multiple_of(lax.axis_index(AZ) * SUB, SUB), SUB), :]


SMEM = pl.BlockSpec(memory_space=pltpu.SMEM)
VMEM = pl.BlockSpec(memory_space=pltpu.VMEM)
HBM = pl.BlockSpec(memory_space=pltpu.HBM)


def call(kernel, shapes, specs, *operands, scratch=(), out_specs=None):
    out = pl.pallas_call(
        kernel,
        out_shape=[jax.ShapeDtypeStruct(*shape) for shape in shapes],
        in_specs=list(specs),
        out_specs=out_specs or [VMEM] * len(shapes),
        scratch_shapes=list(scratch),
        compiler_params=pltpu.CompilerParams(vmem_limit_bytes=32 * 1024 * 1024),
    )(*operands)
    return out if len(out) > 1 else out[0]


def exchange(array, axes):
    return lax.all_to_all(array, axes, split_axis=0, concat_axis=0, tiled=True)


RNG = ("zh", "zl", "x")
AZ = ("yh", "yl", "core")
NEAR = ("zl", "x", "yl", "core")
FAR = ("zh", "yh")


def local(sar_image, strong_index, shifts, widths):
    f32, i32 = jnp.float32, jnp.int32
    az, near, far = lax.axis_size(AZ), lax.axis_size(NEAR), lax.axis_size(FAR)
    bins, pulses_local = sar_image.shape[1:]
    table = tables()
    tile = (SUB, SIDE)
    tiles = (2, bins // SUB, SUB, pulses_local // SIDE, SIDE)
    image = sar_image.reshape(tiles).transpose(0, 1, 3, 2, 4).reshape(2 * bins * SUB, SIDE)
    part = SIDE // near
    sums_shape = (near, 2, part, SIDE)
    moved_tiles = pltpu.VMEM((2 * bins * SUB, SIDE), f32)

    packed, places = call(
        pack_kernel,
        [((az * 8,) + tile, f32), ((SUB + bins, SIDE), i32)],
        [HBM] * 4,
        *(pltpu.with_memory_space_constraint(array, pltpu.HBM) for array in (strong_index, shifts, widths, image)),
        scratch=[pltpu.SMEM((bins,), i32)]
        + [pltpu.SMEM(strong_index.shape, i32) for _ in range(3)]
        + [
            moved_tiles,
            pltpu.SemaphoreType.DMA((3,)),
            pltpu.SemaphoreType.DMA((2,)),
        ],
        out_specs=[VMEM, VMEM],
    )
    rows = exchange(packed.reshape((az, 8) + tile), AZ)
    sums, history = call(
        first_kernel,
        [(sums_shape, f32), ((4, 2, SIDE, SIDE), f32)],
        [VMEM] * 5,
        places,
        rows,
        table["window"],
        table["sides"],
        table["twist"],
        scratch=[pltpu.VMEM((4, SIDE + LOAD, SIDE), f32)],
    )

    def all_gradients(sums):
        scattered = exchange(sums, NEAR)
        partial = call(share_kernel, [((far, 2, part, SIDE), f32)], [VMEM], scattered)
        everyone = exchange(partial, FAR)
        gradient = call(gradient_kernel, [((near, part, SIDE), f32)], [VMEM], everyone)
        return exchange(gradient, NEAR)

    gradient = all_gradients(sums)
    sums, total = call(
        second_kernel,
        [(sums_shape, f32), ((SIDE, SIDE), f32)],
        [VMEM] * 7,
        places,
        gradient,
        history,
        table["window"],
        table["ring"],
        table["sides"],
        table["twist"],
        scratch=[pltpu.VMEM((SIDE, SIDE), f32)],
    )
    gradient = all_gradients(sums)
    corrected, phase = call(
        final_kernel,
        [((az, 8) + tile, f32), (tile, f32)],
        [VMEM] * 5,
        gradient,
        total,
        history,
        table["sides"],
        table["twist"],
        scratch=[pltpu.VMEM((SIDE, SIDE), f32)],
    )
    returned = exchange(corrected, AZ)
    focused, phase = call(
        unpack_kernel,
        [(image.shape, f32), (tile, f32)],
        [VMEM, VMEM, VMEM],
        places,
        returned.reshape((az * 8,) + tile),
        phase,
        scratch=[moved_tiles, pltpu.SemaphoreType.DMA((5,))],
        out_specs=[HBM, HBM],
    )
    focused = focused.reshape(2, bins // SUB, pulses_local // SIDE, SUB, SIDE).transpose(0, 1, 3, 2, 4)
    return focused.reshape(sar_image.shape), phase.reshape(pulses_local)


def solution(mesh):
    rng, az = mesh.devices.shape
    along_x = max(1, min(4, rng // 2))
    split = Mesh(
        mesh.devices.reshape(rng // (2 * along_x), 2, along_x, az // 4, 2, 2), RNG + AZ
    )
    placed = (P(None, RNG, AZ), P(RNG), P(RNG), P(RNG))
    return jax.shard_map(
        local,
        mesh=split,
        in_specs=placed,
        out_specs=(P(None, RNG, AZ), P(AZ)),
        check_vma=False,
    )
```

```python
import jax
import jax.numpy as jnp
import numpy as np
from jax import lax
from jax.experimental import pallas as pl
from jax.experimental.pallas import tpu as pltpu
from jax.sharding import Mesh, PartitionSpec as P

EPSILON = 1e-06
SIDE = 128
SUB = 8
TILES = SIDE // SUB
WINDOW = 16
FIRST = SIDE // 2 - WINDOW // 2
RIGHT, RIGHT_T = 0, 1
LOAD = 24


def tables():
    grid = np.arange(SIDE)
    product = grid[:, None] * grid[None, :]
    angle = 2.0 * np.pi * (product % SIDE) / SIDE
    cosine, sine = np.cos(angle), np.sin(angle)
    right = np.block([[cosine, -sine], [sine, cosine]])
    rows = slice(FIRST, FIRST + WINDOW)
    window = np.block([[cosine[:, rows], sine[:, rows]], [-sine[:, rows], cosine[:, rows]]])
    around = np.arange(SIDE + LOAD) % SIDE
    ring = np.stack([cosine[around], sine[around]])
    twist = 2.0 * np.pi * product / (SIDE * SIDE)
    twist = np.stack([np.cos(twist), np.sin(twist)]) / SIDE
    made = dict(ring=ring, twist=twist)
    made = {name: jnp.asarray(table.astype(np.float32)) for name, table in made.items()}

    def parts(table):
        found, rest = [], table.astype(np.float32)
        for _ in range(3):
            found.append(rest.astype(jnp.bfloat16))
            rest = rest - found[-1].astype(np.float32)
        return found

    window = parts(window)
    made["window"] = jnp.asarray(np.concatenate([window[at] for at in (0, 0, 1, 0, 1, 2)], axis=1))
    made["sides"] = jnp.asarray(np.concatenate(parts(right) + parts(right.T), axis=0))
    return made


def split(array, count):
    parts = []
    for _ in range(count):
        parts.append(array.astype(jnp.bfloat16))
        array = array - parts[-1].astype(jnp.float32)
    return parts


def dot(left, right):
    return jnp.dot(left, right, preferred_element_type=jnp.float32)


def stack(array, count=3):
    return jnp.concatenate(split(array, count), axis=0)


def multiply(left, right):
    count = len(right)
    rows = left.shape[0] // count
    by_order = [None] * count
    for at in range(count):
        product = dot(left[: (count - at) * rows], right[at])
        for order in range(count - at):
            term = product[order * rows : (order + 1) * rows]
            by_order[at + order] = term if by_order[at + order] is None else by_order[at + order] + term
    total = by_order[-1]
    for term in reversed(by_order[:-1]):
        total = total + term
    return total


def multiply_window(left, right):
    first, second, third = split(right, 3)
    return dot(left, jnp.concatenate([first, second, first, third, second, first], axis=0))


def forward(lines, first_stage, sides_ref, twist_ref, count=3):
    cosine, sine = twist_ref[0], twist_ref[1]
    first = first_stage(jnp.concatenate([jnp.concatenate(line, axis=0) for line in lines], axis=1))
    turned = []
    for at in range(len(lines)):
        real = first[:SIDE, at * SIDE : (at + 1) * SIDE]
        imag = first[SIDE:, at * SIDE : (at + 1) * SIDE]
        turned.append(jnp.concatenate([real * cosine + imag * sine, imag * cosine - real * sine], axis=1))
    second = multiply(stack(jnp.concatenate(turned, axis=0), count), parts_of(sides_ref, RIGHT, count))
    return [
        (second[at * SIDE : (at + 1) * SIDE, :SIDE], second[at * SIDE : (at + 1) * SIDE, SIDE:])
        for at in range(len(lines))
    ]


def inverse_start(lines, sides_ref, twist_ref, count=3):
    cosine, sine = twist_ref[0], twist_ref[1]
    stacked = jnp.concatenate([jnp.concatenate(line, axis=1) for line in lines], axis=0)
    first = multiply(stack(stacked, count), parts_of(sides_ref, RIGHT_T, count))
    turned = []
    for at in range(len(lines)):
        real = first[at * SIDE : (at + 1) * SIDE, :SIDE]
        imag = first[at * SIDE : (at + 1) * SIDE, SIDE:]
        turned.append(jnp.concatenate([real * cosine - imag * sine, imag * cosine + real * sine], axis=0))
    return turned


def stacked_of(sides_ref, which, count=3):
    return sides_ref[which * 6 * SIDE : (which * 6 + 2 * count) * SIDE, :]


def parts_of(sides_ref, which, count=3):
    return [sides_ref[(which * 3 + at) * 2 * SIDE : (which * 3 + at + 1) * 2 * SIDE, :] for at in range(count)]


def grid_of(rows):
    return (
        lax.broadcasted_iota(jnp.int32, (rows, SIDE), 0),
        lax.broadcasted_iota(jnp.int32, (rows, SIDE), 1),
    )


def running_sum(gradient):
    rows, cols = grid_of(SIDE)
    within = dot(
        (cols <= rows).astype(jnp.float32).astype(jnp.bfloat16), jnp.concatenate(split(gradient, 3), axis=1)
    )
    sums = jnp.broadcast_to(jnp.sum(gradient, axis=0, keepdims=True), (16, SIDE))
    before = dot(
        jnp.concatenate(split(sums, 3), axis=0), (rows < cols).astype(jnp.float32).astype(jnp.bfloat16)
    )
    within = within[:, :SIDE] + (within[:, SIDE : 2 * SIDE] + within[:, 2 * SIDE :])
    return within + (before[:1, :] + (before[16:17, :] + before[32:33, :]))


def phase_of(gradient_ref, whole_ref):
    near, rows = gradient_ref.shape[:2]
    for at in range(near):
        whole_ref[at * rows : (at + 1) * rows, :] = gradient_ref[at]
    return running_sum(whole_ref[...])


def cosine_sine(angle):
    quarters = jnp.floor(angle * (2.0 / np.pi) + 0.5)
    rest = angle - quarters * 1.5703125
    rest = rest - quarters * 4.837512969970703125e-4
    rest = rest - quarters * 7.54978995489188216e-8
    square = rest * rest
    sine = ((-1.9515295891e-4 * square + 8.3321608736e-3) * square - 1.6666654611e-1) * square * rest + rest
    cosine = (2.443315711809948e-5 * square - 1.388731625493765e-3) * square + 4.166664568298827e-2
    cosine = cosine * square * square - 0.5 * square + 1.0
    turn = quarters.astype(jnp.int32)
    odd = (turn & 1) == 1
    sine, cosine = jnp.where(odd, cosine, sine), jnp.where(odd, sine, cosine)
    return jnp.where(((turn + 1) & 2) == 2, -cosine, cosine), jnp.where((turn & 2) == 2, -sine, sine)


def turn_back(lines, total):
    cosine, sine = cosine_sine(total)
    return [(real * cosine + imag * sine, imag * cosine - real * sine) for real, imag in lines]


def row_offset(shift):
    begin = (shift + SIDE * SIDE // 2) & (SIDE * SIDE - 1)
    return ((begin >> 7) + FIRST) & (SIDE - 1), begin & (SIDE - 1)


def center(upper, lower, lane, width):
    rows, cols = grid_of(WINDOW)
    turn = (SIDE - lane) & (SIDE - 1)
    moved = jnp.where(cols >= SIDE - lane, pltpu.roll(lower, turn, 1), pltpu.roll(upper, turn, 1))
    cells = (rows + FIRST) * SIDE + cols
    least = SIDE * SIDE // 2 - width // 2
    return jnp.where((cells >= least) & (cells < least + width), moved, 0.0)


def gradient_sums(lines, out_ref):
    rows, cols = grid_of(SIDE)
    numerator = jnp.zeros((SIDE, SIDE), jnp.float32)
    denominator = jnp.zeros((SIDE, SIDE), jnp.float32)

    def before(part):
        down = pltpu.roll(part, 1, 0)
        return jnp.where(rows == 0, pltpu.roll(down, 1, 1), down)

    for real, imag in lines:
        numerator = numerator + (before(real) * imag - before(imag) * real)
        denominator = denominator + (real * real + imag * imag)
    numerator = jnp.where((rows == 0) & (cols == 0), 0.0, numerator)
    near, _, part = out_ref.shape[:3]
    for at in range(near):
        out_ref[at, 0] = numerator[at * part : (at + 1) * part, :]
        out_ref[at, 1] = denominator[at * part : (at + 1) * part, :]


def tile_at(bins, part, row):
    return (part * (bins // SUB) + row // SUB) * SUB * SUB + row % SUB


def pack_kernel(
    strong_hbm, shifts_hbm, widths_hbm, image_hbm, out_ref, at_ref,
    place_ref, strong_ref, shifts_ref, widths_ref, image_ref, tiles_ref, small_sems, sems,
):
    bins = image_ref.shape[1]
    strong = strong_ref.shape[0]
    half = bins // 2
    indices = pltpu.make_async_copy(strong_hbm, strong_ref, small_sems.at[0])
    indices.start()
    chunks = []
    for part in range(2):
        for at in range(2):
            span = slice(at * half, (at + 1) * half)
            chunks.append(
                pltpu.make_async_copy(image_hbm.at[part, span], image_ref.at[part, span], sems.at[part * 2 + at])
            )
            chunks[-1].start()
    others_in = [
        pltpu.make_async_copy(shifts_hbm, shifts_ref, small_sems.at[1]),
        pltpu.make_async_copy(widths_hbm, widths_ref, small_sems.at[2]),
    ]
    for copy in others_in:
        copy.start()
    for row in range(bins):
        place_ref[row] = -1
    indices.wait()
    for at in range(strong):
        place_ref[strong_ref[at] & (bins - 1)] = at // 2 * 8 + at % 2
    others = jnp.int32(0)
    places = []
    for row in range(bins):
        held = place_ref[row]
        place = jnp.where(held < 0, ((others >> 1) << 3) + (others & 1) + 2, held)
        others = others + jnp.where(held < 0, 1, 0)
        places.append(place)
        at_ref[SUB + row : SUB + row + 1, :] = jnp.full((1, SIDE), place, jnp.int32)
    for copy in others_in:
        copy.wait()
    for at in range(2):
        line = lax.axis_index(AZ) * 2 + at
        for where, value in enumerate(row_offset(shifts_ref[line]) + (widths_ref[line],)):
            at_ref[4 * at + where : 4 * at + where + 1, :] = jnp.full((1, SIDE), value, jnp.int32)
    for part in range(2):
        for at in range(2):
            chunks[part * 2 + at].wait()
            for group in range(at * half // SUB, (at + 1) * half // SUB):
                for block in range(SUB):
                    tile = ((part * (bins // SUB) + group) * SUB + block) * SUB
                    tiles_ref[tile : tile + SUB, :] = image_ref[
                        part, group * SUB : (group + 1) * SUB, block * SIDE : (block + 1) * SIDE
                    ]
            for row in range(at * half, (at + 1) * half):
                out_ref[places[row] + part * 4] = tiles_ref[pl.ds(tile_at(bins, part, row), SUB, stride=SUB), :]


def unpack_kernel(at_ref, rows_ref, phase_ref, image_hbm, phase_hbm, image_ref, tiles_ref, sems):
    bins = image_ref.shape[1]
    copies = [pltpu.make_async_copy(phase_ref, phase_hbm, sems.at[4])]
    copies[0].start()
    places = [at_ref[SUB + row, 0] for row in range(bins)]
    for part in range(2):
        for row in range(bins):
            tiles_ref[pl.ds(tile_at(bins, part, row), SUB, stride=SUB), :] = rows_ref[places[row] + part * 4]
        for half in range(2):
            span = slice(half * bins // 2, (half + 1) * bins // 2)
            for group in range(half * bins // 2 // SUB, (half + 1) * bins // 2 // SUB):
                for block in range(SUB):
                    at = ((part * (bins // SUB) + group) * SUB + block) * SUB
                    image_ref[part, group * SUB : (group + 1) * SUB, block * SIDE : (block + 1) * SIDE] = tiles_ref[
                        at : at + SUB, :
                    ]
            copies.append(
                pltpu.make_async_copy(
                    image_ref.at[part, span], image_hbm.at[part, span], sems.at[part * 2 + half]
                )
            )
            copies[-1].start()
    for copy in copies:
        copy.wait()


def offsets(at_ref, line):
    return [at_ref[4 * line + where, 0] for where in range(3)]


def first_kernel(
    at_ref, rows_ref, window_ref, sides_ref, twist_ref, out_ref, history_ref, ring_ref
):
    lines = []
    for at in range(2):
        row, lane, width = offsets(at_ref, at)
        parts = []
        for part in range(2):
            ring = ring_ref.at[at * 2 + part]
            ring[:SIDE, :] = square(rows_ref, part * 4 + at)
            ring[SIDE:, :] = rows_ref[: LOAD // SUB, part * 4 + at].reshape(LOAD, SIDE)
            parts.append(center(ring[pl.ds(row, WINDOW), :], ring[pl.ds(row + 1, WINDOW), :], lane, width))
        lines.append(parts)
    gradient_sums(forward(lines, lambda lines: multiply_window(window_ref[...], lines), sides_ref, twist_ref), out_ref)
    for begin, count in ((0, 3), (2, 2)):
        lines = [[square(rows_ref, part * 4 + begin + at) for part in range(2)] for at in range(2)]
        whole = stacked_of(sides_ref, RIGHT_T, count)
        spectra = forward(lines, lambda lines: multiply(whole, split(lines, count)), sides_ref, twist_ref, count)
        for at in range(2):
            for part in range(2):
                history_ref[begin + at, part] = spectra[at][part]


def square(rows_ref, slot):
    return rows_ref[:, slot].reshape(SIDE, SIDE)


def share_kernel(in_ref, out_ref):
    out_ref[...] = jnp.broadcast_to(jnp.sum(in_ref[...], axis=0)[None], out_ref.shape)


def gradient_kernel(in_ref, out_ref):
    sums = jnp.sum(in_ref[...], axis=0)
    out_ref[...] = jnp.broadcast_to((sums[0] / (sums[1] + EPSILON))[None], out_ref.shape)


def second_kernel(
    at_ref, gradient_ref, history_ref, window_ref, ring_ref, sides_ref, twist_ref,
    out_ref, total_ref, whole_ref,
):
    total = phase_of(gradient_ref, whole_ref)
    total_ref[...] = total
    lines = turn_back([(history_ref[at, 0], history_ref[at, 1]) for at in range(2)], total)
    centered = []
    for at, started in enumerate(inverse_start(lines, sides_ref, twist_ref)):
        row, lane, width = offsets(at_ref, at)
        cosine, sine = ring_ref[0, pl.ds(row, LOAD), :], ring_ref[1, pl.ds(row, LOAD), :]
        left = [jnp.concatenate([cosine, -sine], axis=1), jnp.concatenate([sine, cosine], axis=1)]
        found = multiply(stack(jnp.concatenate(left, axis=0)), split(started, 3))
        centered.append(
            [
                center(found[from_row : from_row + WINDOW], found[from_row + 1 : from_row + 1 + WINDOW], lane, width)
                for from_row in (0, LOAD)
            ]
        )
    gradient_sums(forward(centered, lambda lines: multiply_window(window_ref[...], lines), sides_ref, twist_ref), out_ref)


def final_kernel(
    gradient_ref, total_ref, history_ref, sides_ref, twist_ref, out_ref, phase_ref, turned_ref
):
    total = total_ref[...] + phase_of(gradient_ref, turned_ref)
    lines = turn_back([(history_ref[at, 0], history_ref[at, 1]) for at in range(4)], total)
    started = inverse_start(lines, sides_ref, twist_ref, 2)
    found = multiply(stacked_of(sides_ref, RIGHT, 2), split(jnp.concatenate(started, axis=1), 2))
    for at in range(4):
        for part in range(2):
            line = found[part * SIDE : (part + 1) * SIDE, at * SIDE : (at + 1) * SIDE]
            out_ref[:, part * 4 + at] = line.reshape(TILES, SUB, SIDE)
    turned_ref[...] = total.T
    phase_ref[...] = turned_ref[pl.ds(pl.multiple_of(lax.axis_index(AZ) * SUB, SUB), SUB), :]


SMEM = pl.BlockSpec(memory_space=pltpu.SMEM)
VMEM = pl.BlockSpec(memory_space=pltpu.VMEM)
HBM = pl.BlockSpec(memory_space=pltpu.HBM)


def call(kernel, shapes, specs, *operands, scratch=(), out_specs=None):
    out = pl.pallas_call(
        kernel,
        out_shape=[jax.ShapeDtypeStruct(*shape) for shape in shapes],
        in_specs=list(specs),
        out_specs=out_specs or [VMEM] * len(shapes),
        scratch_shapes=list(scratch),
        compiler_params=pltpu.CompilerParams(vmem_limit_bytes=32 * 1024 * 1024),
    )(*operands)
    return out if len(out) > 1 else out[0]


def exchange(array, axes):
    return lax.all_to_all(array, axes, split_axis=0, concat_axis=0, tiled=True)


RNG = ("zh", "zl", "x")
AZ = ("yh", "yl", "core")
NEAR = ("zl", "yl", "core", "x")
FAR = ("zh", "yh")


def local(sar_image, strong_index, shifts, widths):
    f32, i32 = jnp.float32, jnp.int32
    az, near, far = lax.axis_size(AZ), lax.axis_size(NEAR), lax.axis_size(FAR)
    bins, pulses_local = sar_image.shape[1:]
    table = tables()
    tile = (SUB, SIDE)
    part = SIDE // near
    sums_shape = (near, 2, part, SIDE)
    moved_tiles = pltpu.VMEM((2 * bins * SUB, SIDE), f32)

    packed, places = call(
        pack_kernel,
        [((az * 8,) + tile, f32), ((SUB + bins, SIDE), i32)],
        [HBM] * 4,
        *(pltpu.with_memory_space_constraint(array, pltpu.HBM) for array in (strong_index, shifts, widths, sar_image)),
        scratch=[pltpu.SMEM((bins,), i32)]
        + [pltpu.SMEM(strong_index.shape, i32) for _ in range(3)]
        + [
            pltpu.VMEM(sar_image.shape, f32),
            moved_tiles,
            pltpu.SemaphoreType.DMA((3,)),
            pltpu.SemaphoreType.DMA((4,)),
        ],
        out_specs=[VMEM, VMEM],
    )
    rows = exchange(packed.reshape((az, 8) + tile), AZ)
    sums, history = call(
        first_kernel,
        [(sums_shape, f32), ((4, 2, SIDE, SIDE), f32)],
        [VMEM] * 5,
        places,
        rows,
        table["window"],
        table["sides"],
        table["twist"],
        scratch=[pltpu.VMEM((4, SIDE + LOAD, SIDE), f32)],
    )

    def all_gradients(sums):
        scattered = exchange(sums, NEAR)
        partial = call(share_kernel, [((far, 2, part, SIDE), f32)], [VMEM], scattered)
        everyone = exchange(partial, FAR)
        gradient = call(gradient_kernel, [((near, part, SIDE), f32)], [VMEM], everyone)
        return exchange(gradient, NEAR)

    gradient = all_gradients(sums)
    sums, total = call(
        second_kernel,
        [(sums_shape, f32), ((SIDE, SIDE), f32)],
        [VMEM] * 7,
        places,
        gradient,
        history,
        table["window"],
        table["ring"],
        table["sides"],
        table["twist"],
        scratch=[pltpu.VMEM((SIDE, SIDE), f32)],
    )
    gradient = all_gradients(sums)
    corrected, phase = call(
        final_kernel,
        [((az, 8) + tile, f32), (tile, f32)],
        [VMEM] * 5,
        gradient,
        total,
        history,
        table["sides"],
        table["twist"],
        scratch=[pltpu.VMEM((SIDE, SIDE), f32)],
    )
    returned = exchange(corrected, AZ)
    focused, phase = call(
        unpack_kernel,
        [(sar_image.shape, f32), (tile, f32)],
        [VMEM, VMEM, VMEM],
        places,
        returned.reshape((az * 8,) + tile),
        phase,
        scratch=[pltpu.VMEM(sar_image.shape, f32), moved_tiles, pltpu.SemaphoreType.DMA((5,))],
        out_specs=[HBM, HBM],
    )
    return focused, phase.reshape(pulses_local)


def solution(mesh):
    rng, az = mesh.devices.shape
    along_x = max(1, min(4, rng // 2))
    split = Mesh(
        mesh.devices.reshape(rng // (2 * along_x), 2, along_x, az // 4, 2, 2), RNG + AZ
    )
    placed = (P(None, RNG, AZ), P(RNG), P(RNG), P(RNG))
    return jax.shard_map(
        local,
        mesh=split,
        in_specs=placed,
        out_specs=(P(None, RNG, AZ), P(AZ)),
        check_vma=False,
    )
```

```python
import jax
import jax.numpy as jnp
import numpy as np
from jax import lax
from jax.experimental import pallas as pl
from jax.experimental.pallas import tpu as pltpu
from jax.sharding import Mesh, PartitionSpec as P

EPSILON = 1e-06
SIDE = 128
SUB = 8
TILES = SIDE // SUB
WINDOW = 16
FIRST = SIDE // 2 - WINDOW // 2
RIGHT, RIGHT_T = 0, 1
LOAD = 24


def tables():
    grid = np.arange(SIDE)
    product = grid[:, None] * grid[None, :]
    angle = 2.0 * np.pi * (product % SIDE) / SIDE
    cosine, sine = np.cos(angle), np.sin(angle)
    right = np.block([[cosine, -sine], [sine, cosine]])
    rows = slice(FIRST, FIRST + WINDOW)
    window = np.block([[cosine[:, rows], sine[:, rows]], [-sine[:, rows], cosine[:, rows]]])
    around = np.arange(SIDE + LOAD) % SIDE
    ring = np.stack([cosine[around], sine[around]])
    twist = 2.0 * np.pi * product / (SIDE * SIDE)
    twist = np.stack([np.cos(twist), np.sin(twist)]) / SIDE
    made = dict(ring=ring, twist=twist)
    made = {name: jnp.asarray(table.astype(np.float32)) for name, table in made.items()}

    def parts(table):
        found, rest = [], table.astype(np.float32)
        for _ in range(3):
            found.append(rest.astype(jnp.bfloat16))
            rest = rest - found[-1].astype(np.float32)
        return found

    window = parts(window)
    made["window"] = jnp.asarray(np.concatenate([window[at] for at in (0, 0, 1, 0, 1, 2)], axis=1))
    made["sides"] = jnp.asarray(np.concatenate(parts(right) + parts(right.T), axis=0))
    return made


def split(array, count):
    parts = []
    for _ in range(count):
        parts.append(array.astype(jnp.bfloat16))
        array = array - parts[-1].astype(jnp.float32)
    return parts


def dot(left, right):
    return jnp.dot(left, right, preferred_element_type=jnp.float32)


def stack(array, count=3):
    return jnp.concatenate(split(array, count), axis=0)


def multiply(left, right):
    count = len(right)
    rows = left.shape[0] // count
    by_order = [None] * count
    for at in range(count):
        product = dot(left[: (count - at) * rows], right[at])
        for order in range(count - at):
            term = product[order * rows : (order + 1) * rows]
            by_order[at + order] = term if by_order[at + order] is None else by_order[at + order] + term
    total = by_order[-1]
    for term in reversed(by_order[:-1]):
        total = total + term
    return total


def multiply_window(left, right):
    first, second, third = split(right, 3)
    return dot(left, jnp.concatenate([first, second, first, third, second, first], axis=0))


def forward(lines, first_stage, sides_ref, twist_ref, count=3):
    cosine, sine = twist_ref[0], twist_ref[1]
    first = first_stage(jnp.concatenate([jnp.concatenate(line, axis=0) for line in lines], axis=1))
    turned = []
    for at in range(len(lines)):
        real = first[:SIDE, at * SIDE : (at + 1) * SIDE]
        imag = first[SIDE:, at * SIDE : (at + 1) * SIDE]
        turned.append(jnp.concatenate([real * cosine + imag * sine, imag * cosine - real * sine], axis=1))
    second = multiply(stack(jnp.concatenate(turned, axis=0), count), parts_of(sides_ref, RIGHT, count))
    return [
        (second[at * SIDE : (at + 1) * SIDE, :SIDE], second[at * SIDE : (at + 1) * SIDE, SIDE:])
        for at in range(len(lines))
    ]


def inverse_start(lines, sides_ref, twist_ref, count=3):
    cosine, sine = twist_ref[0], twist_ref[1]
    stacked = jnp.concatenate([jnp.concatenate(line, axis=1) for line in lines], axis=0)
    first = multiply(stack(stacked, count), parts_of(sides_ref, RIGHT_T, count))
    turned = []
    for at in range(len(lines)):
        real = first[at * SIDE : (at + 1) * SIDE, :SIDE]
        imag = first[at * SIDE : (at + 1) * SIDE, SIDE:]
        turned.append(jnp.concatenate([real * cosine - imag * sine, imag * cosine + real * sine], axis=0))
    return turned


def stacked_of(sides_ref, which, count=3):
    return sides_ref[which * 6 * SIDE : (which * 6 + 2 * count) * SIDE, :]


def parts_of(sides_ref, which, count=3):
    return [sides_ref[(which * 3 + at) * 2 * SIDE : (which * 3 + at + 1) * 2 * SIDE, :] for at in range(count)]


def grid_of(rows):
    return (
        lax.broadcasted_iota(jnp.int32, (rows, SIDE), 0),
        lax.broadcasted_iota(jnp.int32, (rows, SIDE), 1),
    )


def running_sum(gradient):
    rows, cols = grid_of(SIDE)
    within = dot(
        (cols <= rows).astype(jnp.float32).astype(jnp.bfloat16), jnp.concatenate(split(gradient, 3), axis=1)
    )
    sums = jnp.broadcast_to(jnp.sum(gradient, axis=0, keepdims=True), (16, SIDE))
    before = dot(
        jnp.concatenate(split(sums, 3), axis=0), (rows < cols).astype(jnp.float32).astype(jnp.bfloat16)
    )
    within = within[:, :SIDE] + (within[:, SIDE : 2 * SIDE] + within[:, 2 * SIDE :])
    return within + (before[:1, :] + (before[16:17, :] + before[32:33, :]))


def phase_of(gradient_ref, whole_ref):
    near, rows = gradient_ref.shape[:2]
    for at in range(near):
        whole_ref[at * rows : (at + 1) * rows, :] = gradient_ref[at]
    return running_sum(whole_ref[...])


def cosine_sine(angle):
    quarters = jnp.floor(angle * (2.0 / np.pi) + 0.5)
    rest = angle - quarters * 1.5703125
    rest = rest - quarters * 4.837512969970703125e-4
    rest = rest - quarters * 7.54978995489188216e-8
    square = rest * rest
    sine = ((-1.9515295891e-4 * square + 8.3321608736e-3) * square - 1.6666654611e-1) * square * rest + rest
    cosine = (2.443315711809948e-5 * square - 1.388731625493765e-3) * square + 4.166664568298827e-2
    cosine = cosine * square * square - 0.5 * square + 1.0
    turn = quarters.astype(jnp.int32)
    odd = (turn & 1) == 1
    sine, cosine = jnp.where(odd, cosine, sine), jnp.where(odd, sine, cosine)
    return jnp.where(((turn + 1) & 2) == 2, -cosine, cosine), jnp.where((turn & 2) == 2, -sine, sine)


def turn_back(lines, total):
    cosine, sine = cosine_sine(total)
    return [(real * cosine + imag * sine, imag * cosine - real * sine) for real, imag in lines]


def row_offset(shift):
    begin = (shift + SIDE * SIDE // 2) & (SIDE * SIDE - 1)
    return ((begin >> 7) + FIRST) & (SIDE - 1), begin & (SIDE - 1)


def center(upper, lower, lane, width):
    rows, cols = grid_of(WINDOW)
    turn = (SIDE - lane) & (SIDE - 1)
    moved = jnp.where(cols >= SIDE - lane, pltpu.roll(lower, turn, 1), pltpu.roll(upper, turn, 1))
    cells = (rows + FIRST) * SIDE + cols
    least = SIDE * SIDE // 2 - width // 2
    return jnp.where((cells >= least) & (cells < least + width), moved, 0.0)


def gradient_sums(lines, out_ref):
    rows, cols = grid_of(SIDE)
    numerator = jnp.zeros((SIDE, SIDE), jnp.float32)
    denominator = jnp.zeros((SIDE, SIDE), jnp.float32)

    def before(part):
        down = pltpu.roll(part, 1, 0)
        return jnp.where(rows == 0, pltpu.roll(down, 1, 1), down)

    for real, imag in lines:
        numerator = numerator + (before(real) * imag - before(imag) * real)
        denominator = denominator + (real * real + imag * imag)
    numerator = jnp.where((rows == 0) & (cols == 0), 0.0, numerator)
    near, _, part = out_ref.shape[:3]
    for at in range(near):
        out_ref[at, 0] = numerator[at * part : (at + 1) * part, :]
        out_ref[at, 1] = denominator[at * part : (at + 1) * part, :]


def tile_at(bins, part, row):
    return (part * (bins // SUB) + row // SUB) * SUB * SUB + row % SUB


def pack_kernel(
    strong_hbm, shifts_hbm, widths_hbm, image_hbm, out_ref, at_ref,
    place_ref, strong_ref, shifts_ref, widths_ref, image_ref, tiles_ref, small_sems, sems,
):
    bins = image_ref.shape[1]
    strong = strong_ref.shape[0]
    half = bins // 2
    indices = pltpu.make_async_copy(strong_hbm, strong_ref, small_sems.at[0])
    indices.start()
    chunks = []
    for part in range(2):
        for at in range(2):
            span = slice(at * half, (at + 1) * half)
            chunks.append(
                pltpu.make_async_copy(image_hbm.at[part, span], image_ref.at[part, span], sems.at[part * 2 + at])
            )
            chunks[-1].start()
    others_in = [
        pltpu.make_async_copy(shifts_hbm, shifts_ref, small_sems.at[1]),
        pltpu.make_async_copy(widths_hbm, widths_ref, small_sems.at[2]),
    ]
    for copy in others_in:
        copy.start()
    for row in range(bins):
        place_ref[row] = -1
    indices.wait()
    for at in range(strong):
        place_ref[strong_ref[at] & (bins - 1)] = at // 2 * 8 + at % 2
    others = jnp.int32(0)
    places = []
    for row in range(bins):
        held = place_ref[row]
        place = jnp.where(held < 0, ((others >> 1) << 3) + (others & 1) + 2, held)
        others = others + jnp.where(held < 0, 1, 0)
        places.append(place)
        at_ref[SUB + row : SUB + row + 1, :] = jnp.full((1, SIDE), place, jnp.int32)
    for copy in others_in:
        copy.wait()
    for at in range(2):
        line = lax.axis_index(AZ) * 2 + at
        for where, value in enumerate(row_offset(shifts_ref[line]) + (widths_ref[line],)):
            at_ref[4 * at + where : 4 * at + where + 1, :] = jnp.full((1, SIDE), value, jnp.int32)
    for part in range(2):
        for at in range(2):
            chunks[part * 2 + at].wait()
            for group in range(at * half // SUB, (at + 1) * half // SUB):
                for block in range(SUB):
                    tile = ((part * (bins // SUB) + group) * SUB + block) * SUB
                    tiles_ref[tile : tile + SUB, :] = image_ref[
                        part, group * SUB : (group + 1) * SUB, block * SIDE : (block + 1) * SIDE
                    ]
            for row in range(at * half, (at + 1) * half):
                out_ref[places[row] + part * 4] = tiles_ref[pl.ds(tile_at(bins, part, row), SUB, stride=SUB), :]


def unpack_kernel(at_ref, rows_ref, phase_ref, image_hbm, phase_hbm, image_ref, tiles_ref, sems):
    bins = image_ref.shape[1]
    copies = [pltpu.make_async_copy(phase_ref, phase_hbm, sems.at[4])]
    copies[0].start()
    places = [at_ref[SUB + row, 0] for row in range(bins)]
    for part in range(2):
        for half in range(2):
            for row in range(half * bins // 2, (half + 1) * bins // 2):
                tiles_ref[pl.ds(tile_at(bins, part, row), SUB, stride=SUB), :] = rows_ref[places[row] + part * 4]
            span = slice(half * bins // 2, (half + 1) * bins // 2)
            for group in range(half * bins // 2 // SUB, (half + 1) * bins // 2 // SUB):
                for block in range(SUB):
                    at = ((part * (bins // SUB) + group) * SUB + block) * SUB
                    image_ref[part, group * SUB : (group + 1) * SUB, block * SIDE : (block + 1) * SIDE] = tiles_ref[
                        at : at + SUB, :
                    ]
            copies.append(
                pltpu.make_async_copy(
                    image_ref.at[part, span], image_hbm.at[part, span], sems.at[part * 2 + half]
                )
            )
            copies[-1].start()
    for copy in copies:
        copy.wait()


def offsets(at_ref, line):
    return [at_ref[4 * line + where, 0] for where in range(3)]


def first_kernel(
    at_ref, rows_ref, window_ref, sides_ref, twist_ref, out_ref, history_ref, ring_ref
):
    lines = []
    for at in range(2):
        row, lane, width = offsets(at_ref, at)
        parts = []
        for part in range(2):
            ring = ring_ref.at[at * 2 + part]
            ring[:SIDE, :] = square(rows_ref, part * 4 + at)
            ring[SIDE:, :] = rows_ref[: LOAD // SUB, part * 4 + at].reshape(LOAD, SIDE)
            parts.append(center(ring[pl.ds(row, WINDOW), :], ring[pl.ds(row + 1, WINDOW), :], lane, width))
        lines.append(parts)
    gradient_sums(forward(lines, lambda lines: multiply_window(window_ref[...], lines), sides_ref, twist_ref), out_ref)
    for begin, count in ((0, 3), (2, 2)):
        lines = [[square(rows_ref, part * 4 + begin + at) for part in range(2)] for at in range(2)]
        whole = stacked_of(sides_ref, RIGHT_T, count)
        spectra = forward(lines, lambda lines: multiply(whole, split(lines, count)), sides_ref, twist_ref, count)
        for at in range(2):
            for part in range(2):
                history_ref[begin + at, part] = spectra[at][part]


def square(rows_ref, slot):
    return rows_ref[:, slot].reshape(SIDE, SIDE)


def share_kernel(in_ref, out_ref):
    out_ref[...] = jnp.broadcast_to(jnp.sum(in_ref[...], axis=0)[None], out_ref.shape)


def gradient_kernel(in_ref, out_ref):
    sums = jnp.sum(in_ref[...], axis=0)
    out_ref[...] = jnp.broadcast_to((sums[0] / (sums[1] + EPSILON))[None], out_ref.shape)


def second_kernel(
    at_ref, gradient_ref, history_ref, window_ref, ring_ref, sides_ref, twist_ref,
    out_ref, total_ref, whole_ref,
):
    total = phase_of(gradient_ref, whole_ref)
    total_ref[...] = total
    lines = turn_back([(history_ref[at, 0], history_ref[at, 1]) for at in range(2)], total)
    centered = []
    for at, started in enumerate(inverse_start(lines, sides_ref, twist_ref)):
        row, lane, width = offsets(at_ref, at)
        cosine, sine = ring_ref[0, pl.ds(row, LOAD), :], ring_ref[1, pl.ds(row, LOAD), :]
        left = [jnp.concatenate([cosine, -sine], axis=1), jnp.concatenate([sine, cosine], axis=1)]
        found = multiply(stack(jnp.concatenate(left, axis=0)), split(started, 3))
        centered.append(
            [
                center(found[from_row : from_row + WINDOW], found[from_row + 1 : from_row + 1 + WINDOW], lane, width)
                for from_row in (0, LOAD)
            ]
        )
    gradient_sums(forward(centered, lambda lines: multiply_window(window_ref[...], lines), sides_ref, twist_ref), out_ref)


def final_kernel(
    gradient_ref, total_ref, history_ref, sides_ref, twist_ref, out_ref, phase_ref, turned_ref
):
    total = total_ref[...] + phase_of(gradient_ref, turned_ref)
    lines = turn_back([(history_ref[at, 0], history_ref[at, 1]) for at in range(4)], total)
    started = inverse_start(lines, sides_ref, twist_ref, 2)
    found = multiply(stacked_of(sides_ref, RIGHT, 2), split(jnp.concatenate(started, axis=1), 2))
    for at in range(4):
        for part in range(2):
            line = found[part * SIDE : (part + 1) * SIDE, at * SIDE : (at + 1) * SIDE]
            out_ref[:, part * 4 + at] = line.reshape(TILES, SUB, SIDE)
    turned_ref[...] = total.T
    phase_ref[...] = turned_ref[pl.ds(pl.multiple_of(lax.axis_index(AZ) * SUB, SUB), SUB), :]


SMEM = pl.BlockSpec(memory_space=pltpu.SMEM)
VMEM = pl.BlockSpec(memory_space=pltpu.VMEM)
HBM = pl.BlockSpec(memory_space=pltpu.HBM)


def call(kernel, shapes, specs, *operands, scratch=(), out_specs=None):
    out = pl.pallas_call(
        kernel,
        out_shape=[jax.ShapeDtypeStruct(*shape) for shape in shapes],
        in_specs=list(specs),
        out_specs=out_specs or [VMEM] * len(shapes),
        scratch_shapes=list(scratch),
        compiler_params=pltpu.CompilerParams(vmem_limit_bytes=32 * 1024 * 1024),
    )(*operands)
    return out if len(out) > 1 else out[0]


def exchange(array, axes):
    return lax.all_to_all(array, axes, split_axis=0, concat_axis=0, tiled=True)


RNG = ("zh", "zl", "x")
AZ = ("yh", "yl", "core")
NEAR = ("zl", "x", "yl", "core")
FAR = ("zh", "yh")


def local(sar_image, strong_index, shifts, widths):
    f32, i32 = jnp.float32, jnp.int32
    az, near, far = lax.axis_size(AZ), lax.axis_size(NEAR), lax.axis_size(FAR)
    bins, pulses_local = sar_image.shape[1:]
    table = tables()
    tile = (SUB, SIDE)
    part = SIDE // near
    sums_shape = (near, 2, part, SIDE)
    moved_tiles = pltpu.VMEM((2 * bins * SUB, SIDE), f32)

    packed, places = call(
        pack_kernel,
        [((az * 8,) + tile, f32), ((SUB + bins, SIDE), i32)],
        [HBM] * 4,
        *(pltpu.with_memory_space_constraint(array, pltpu.HBM) for array in (strong_index, shifts, widths, sar_image)),
        scratch=[pltpu.SMEM((bins,), i32)]
        + [pltpu.SMEM(strong_index.shape, i32) for _ in range(3)]
        + [
            pltpu.VMEM(sar_image.shape, f32),
            moved_tiles,
            pltpu.SemaphoreType.DMA((3,)),
            pltpu.SemaphoreType.DMA((4,)),
        ],
        out_specs=[VMEM, VMEM],
    )
    rows = exchange(packed.reshape((az, 8) + tile), AZ)
    sums, history = call(
        first_kernel,
        [(sums_shape, f32), ((4, 2, SIDE, SIDE), f32)],
        [VMEM] * 5,
        places,
        rows,
        table["window"],
        table["sides"],
        table["twist"],
        scratch=[pltpu.VMEM((4, SIDE + LOAD, SIDE), f32)],
    )

    def all_gradients(sums):
        scattered = exchange(sums, NEAR)
        partial = call(share_kernel, [((far, 2, part, SIDE), f32)], [VMEM], scattered)
        everyone = exchange(partial, FAR)
        gradient = call(gradient_kernel, [((near, part, SIDE), f32)], [VMEM], everyone)
        return exchange(gradient, NEAR)

    gradient = all_gradients(sums)
    sums, total = call(
        second_kernel,
        [(sums_shape, f32), ((SIDE, SIDE), f32)],
        [VMEM] * 7,
        places,
        gradient,
        history,
        table["window"],
        table["ring"],
        table["sides"],
        table["twist"],
        scratch=[pltpu.VMEM((SIDE, SIDE), f32)],
    )
    gradient = all_gradients(sums)
    corrected, phase = call(
        final_kernel,
        [((az, 8) + tile, f32), (tile, f32)],
        [VMEM] * 5,
        gradient,
        total,
        history,
        table["sides"],
        table["twist"],
        scratch=[pltpu.VMEM((SIDE, SIDE), f32)],
    )
    returned = exchange(corrected, AZ)
    focused, phase = call(
        unpack_kernel,
        [(sar_image.shape, f32), (tile, f32)],
        [VMEM, VMEM, VMEM],
        places,
        returned.reshape((az * 8,) + tile),
        phase,
        scratch=[pltpu.VMEM(sar_image.shape, f32), moved_tiles, pltpu.SemaphoreType.DMA((5,))],
        out_specs=[HBM, HBM],
    )
    return focused, phase.reshape(pulses_local)


def solution(mesh):
    rng, az = mesh.devices.shape
    along_x = max(1, min(4, rng // 2))
    split = Mesh(
        mesh.devices.reshape(rng // (2 * along_x), 2, along_x, az // 4, 2, 2), RNG + AZ
    )
    placed = (P(None, RNG, AZ), P(RNG), P(RNG), P(RNG))
    return jax.shard_map(
        local,
        mesh=split,
        in_specs=placed,
        out_specs=(P(None, RNG, AZ), P(AZ)),
        check_vma=False,
    )
```
